128 devices in a mesh: dp: 64 (over z, x_lo, y, core), rep: 2 (over x_hi).
Axes of the slice: x: 4 (x_hi: 2, x_lo: 2; x = x_hi * 2 + x_lo), y: 4, z: 4, core: 2. Of those that a mesh axis runs over, the one named last changes fastest.
Arguments:
- states: bfloat16 [2, 128, 256, 768], P(None, ('dp', 'rep')), may hold values from -24 to 24
- qkv_weight: bfloat16 [768, 2304], P('dp'), may hold values from -0.21875 to 0.21875
- query_bias: bfloat16 [768], P('dp'), may hold values from -3 to 3
- value_bias: bfloat16 [768], P('dp'), may hold values from -3 to 3
- out_weight: bfloat16 [768, 768], P('dp'), may hold values from -0.625 to 0.625
- out_bias: bfloat16 [768], P('dp'), may hold values from -3 to 3
- attn_gain: bfloat16 [768], P('dp'), may hold values from 0.099609375 to 1.8984375
- attn_shift: bfloat16 [768], P('dp'), may hold values from -3 to 3
- up_weight: bfloat16 [768, 3072], P('dp'), may hold values from -0.21875 to 0.21875
- up_bias: bfloat16 [3072], P('dp'), may hold values from -3 to 3
- down_weight: bfloat16 [3072, 768], P('dp'), may hold values from -0.109375 to 0.109375
- down_bias: bfloat16 [768], P('dp'), may hold values from -3 to 3
- ffn_gain: bfloat16 [768], P('dp'), may hold values from 0.099609375 to 1.8984375
- ffn_shift: bfloat16 [768], P('dp'), may hold values from -3 to 3
- out_grad: bfloat16 [2, 128, 256, 768], P(None, ('dp', 'rep')), may hold values from -6 to 6
- lengths: int32 [2, 128], P(None, ('dp', 'rep')), may hold values from 64 to 256, as said below
Outputs:
- encoded: bfloat16 [2, 128, 256, 768], P(None, ('dp', 'rep'))
- states_grad: float32 [2, 128, 256, 768], P(None, ('dp', 'rep'))
- grad_qkv_weight: float32 [768, 2304], P('dp')
- grad_query_bias: float32 [768], P('dp')
- grad_value_bias: float32 [768], P('dp')
- grad_out_weight: float32 [768, 768], P('dp')
- grad_out_bias: float32 [768], P('dp')
- grad_attn_gain: float32 [768], P('dp')
- grad_attn_shift: float32 [768], P('dp')
- grad_up_weight: float32 [768, 3072], P('dp')
- grad_up_bias: float32 [3072], P('dp')
- grad_down_weight: float32 [3072, 768], P('dp')
- grad_down_bias: float32 [768], P('dp')
- grad_ffn_gain: float32 [768], P('dp')
- grad_ffn_shift: float32 [768], P('dp')
The draws below stay inside these ranges and needn't reach their ends.
Inputs may be any that keep to these rules, and one draw needn't show every extreme that they name: Slot [m, s] holds one sequence of lengths[m, s] tokens at its start; later key slots are padding. In every draw some slot is full (256) and some holds 64.
All inputs are finite; a program needn't handle non-finite values.
Results may differ from the reference program's by a relative error of at most 0.013.
The reference program's roundings to bfloat16 on the way count: a program that leaves them out, or rounds other values in their place, can miss the bound.
Values may be sent and summed in bfloat16 or wider, within the bound.
A program may use at most 128 MiB of HBM per device.

```python
import math
import jax
import jax.numpy as jnp
from jax import lax

D = 768
HD = 64
FF = 3072
SEQ_LEN = 256
MICRO = 2
SEQS = 128


def draw_lengths(key, part):
    key = jax.random.fold_in(key, 7)
    key_draw, key_full, key_short = jax.random.split(key, 3)
    drawn = jax.random.randint(key_draw, (MICRO, SEQS), SEQ_LEN // 4, SEQ_LEN + 1)
    full_slot = jax.random.randint(key_full, (), 0, SEQS)
    short_slot = jax.random.randint(key_short, (), 0, SEQS)
    drawn = drawn.at[0, full_slot].set(SEQ_LEN)
    drawn = drawn.at[MICRO - 1, short_slot].set(SEQ_LEN // 4)
    return drawn.astype(jnp.int32)


def strengthened(values, own_key, source, target, parts, factor):
    owner, partner = [(jnp.arange(values.shape[dim]) // (values.shape[dim] // parts)).reshape([-1 if axis == dim else 1 for axis in range(values.ndim)]) for dim in (source, target)]
    chosen = jax.random.permutation(own_key, parts)[partner]
    strong = (owner == chosen) | (owner == (partner + parts // 2) % parts)
    return jnp.where(strong, factor * values, values)


def block_levels(key, extent, shards, smallest, top_value):
    loudness = 1.0
    for position, parts in shards:
        draws = jax.random.uniform(jax.random.fold_in(jax.random.fold_in(key, 6), position), (parts,), jnp.float32, smallest / len(shards), top_value / len(shards))
        loudness = loudness * jnp.repeat(jnp.exp(draws), extent[position] // parts).reshape((-1,) + (1,) * (len(extent) - 1 - position))
    return loudness


def centred(rng, shape, spread, reach, pieces=(), held_as=jnp.bfloat16):
    values = spread * jax.random.normal(rng, shape, jnp.float32)
    if pieces:
        values = values * block_levels(rng, shape, pieces, -0.22, 0.18)
    return jnp.clip(values, -reach, reach).astype(held_as)


def bell_draw_with(rng, extent, spread, bound, cuts, heavy, held_as=jnp.bfloat16):
    result = spread * jax.random.normal(rng, extent, jnp.float32)
    if cuts:
        result = result * block_levels(rng, extent, cuts, -0.22, 0.18)
    return jnp.clip(strengthened(result, jax.random.fold_in(rng, 3), *heavy), -bound, bound).astype(held_as)


def setup_inputs(seed: int = 0) -> dict:
    seeds = jax.random.split(jax.random.key(seed), 17)
    states = bell_draw_with(seeds[0], (MICRO, SEQS, SEQ_LEN, D), 1.0, 24.0, ((1, 128),), (1, 3, 128, 5.5))
    qkv_weight = centred(seeds[1], (D, 3 * D), D ** -0.5, 0.21875, ((0, 64),))
    query_bias = centred(seeds[2], (D,), 0.5, 3.0, ((0, 64),))
    value_bias = centred(seeds[3], (D,), 0.5, 3.0, ((0, 64),))
    out_weight = centred(seeds[4], (D, D), (D // 8) ** -0.5, 0.625, ((0, 64),))
    out_bias = centred(seeds[5], (D,), 0.5, 3.0, ((0, 64),))
    attn_gain = jnp.clip(1.0 + 0.18 * jax.random.normal(seeds[6], (D,), jnp.float32), 0.099609375, 1.8984375).astype(jnp.bfloat16)
    attn_shift = centred(seeds[7], (D,), 0.5, 3.0, ((0, 64),))
    up_weight = centred(seeds[8], (D, FF), D ** -0.5, 0.21875, ((0, 64),))
    up_bias = centred(seeds[9], (FF,), 0.5, 3.0, ((0, 64),))
    down_weight = centred(seeds[10], (FF, D), FF ** -0.5, 0.109375, ((0, 64),))
    down_bias = centred(seeds[11], (D,), 0.5, 3.0, ((0, 64),))
    ffn_gain = jnp.clip(1.0 + 0.18 * jax.random.normal(seeds[12], (D,), jnp.float32), 0.099609375, 1.8984375).astype(jnp.bfloat16)
    ffn_shift = centred(seeds[13], (D,), 0.5, 3.0, ((0, 64),))
    out_grad = centred(seeds[14], (MICRO, SEQS, SEQ_LEN, D), 1.0, 6.0, ((1, 128),))
    lengths = draw_lengths(jax.random.fold_in(seeds[16], 71), 0)
    return {"states": states, "qkv_weight": qkv_weight, "query_bias": query_bias, "value_bias": value_bias, "out_weight": out_weight, "out_bias": out_bias, "attn_gain": attn_gain, "attn_shift": attn_shift, "up_weight": up_weight, "up_bias": up_bias, "down_weight": down_weight, "down_bias": down_bias, "ffn_gain": ffn_gain, "ffn_shift": ffn_shift, "out_grad": out_grad, "lengths": lengths}


@jax.custom_vjp
def low(v):
    return lax.optimization_barrier(v.astype(jnp.bfloat16)).astype(jnp.float32)

@jax.custom_vjp
def low_back(v):
    return v

def low_keep(v):
    return (low(v), None)

def low_pass(kept, grad):
    return (grad,)

def back_keep(v):
    return (v, None)

def back_low(kept, grad):
    return (low(grad),)
low.defvjp(low_keep, low_pass)
low_back.defvjp(back_keep, back_low)
epsilon = 1e-05
highest = lax.Precision.HIGHEST

def matmul(left, right):
    return jnp.dot(left, right, precision=highest, preferred_element_type=jnp.float32)

def layer_norm(hidden, gain, shift):
    center = hidden - lax.optimization_barrier(jnp.mean(hidden, -1, keepdims=True))
    variance = lax.optimization_barrier(jnp.mean(center * center, -1, keepdims=True))
    return center * lax.rsqrt(variance + epsilon) * gain + shift

def gelu_exact(value):
    return 0.5 * value * (1.0 + lax.erf(value * (1.0 / math.sqrt(2.0))))

def layer(parameters, states, valid_keys):
    qkv_weight, query_bias, value_bias, out_weight, out_bias, attn_gain, attn_shift, up_weight, up_bias, down_weight, down_bias, ffn_gain, ffn_shift = parameters
    group_size, length, width = states.shape
    head_count = width // HD
    shaped = (group_size, length, head_count, HD)
    joint_proj = matmul(states, qkv_weight)
    queries = low(low_back(joint_proj[..., :width] + query_bias)).reshape(shaped)
    key_rows = low(low_back(joint_proj[..., width:2 * width])).reshape(shaped)
    values = low(low_back(joint_proj[..., 2 * width:] + value_bias)).reshape(shaped)
    scores = jnp.einsum('gqhd,gkhd->ghqk', queries, key_rows, precision=highest) * (1.0 / math.sqrt(HD))
    scores = low_back(scores)
    scores = jnp.where(valid_keys[:, None, None, :], scores, -1000000000.0)
    row_peak = lax.optimization_barrier(jnp.max(scores, -1, keepdims=True))
    exponent = jnp.exp(scores - row_peak)
    attention = low(exponent / lax.optimization_barrier(jnp.sum(exponent, -1, keepdims=True)))
    mixed_heads = jnp.einsum('ghqk,gkhd->gqhd', attention, values, precision=highest)
    mixed_heads = low(low_back(mixed_heads.reshape(group_size, length, width)))
    branch = low_back(matmul(mixed_heads, out_weight) + out_bias)
    normed = layer_norm(states + branch, attn_gain, attn_shift)
    pre_act = low_back(matmul(low(normed), up_weight) + up_bias)
    activation = low(gelu_exact(pre_act))
    update = low_back(matmul(activation, down_weight) + down_bias)
    return layer_norm(normed + update, ffn_gain, ffn_shift)

def add_pair(left_item, right_item):
    return left_item + right_item

def reference(states, qkv_weight, query_bias, value_bias, out_weight, out_bias, attn_gain, attn_shift, up_weight, up_bias, down_weight, down_bias, ffn_gain, ffn_shift, out_grad, lengths):
    given = (qkv_weight, query_bias, value_bias, out_weight, out_bias, attn_gain, attn_shift, up_weight, up_bias, down_weight, down_bias, ffn_gain, ffn_shift)
    parameters = tuple((weight_item.astype(jnp.float32) for weight_item in given))
    slot_count = MICRO * SEQS
    group_size = math.gcd(slot_count, max(1, 4096 // SEQ_LEN))
    group_count = slot_count // group_size
    flat_states = states.astype(jnp.float32).reshape(group_count, group_size, SEQ_LEN, D)
    flat_grad = out_grad.astype(jnp.float32).reshape(group_count, group_size, SEQ_LEN, D)
    flat_len = lengths.astype(jnp.int32).reshape(group_count, group_size)
    positions = jnp.arange(SEQ_LEN, dtype=jnp.int32)

    def step(carried, group_data):
        group_states, group_grad, group_len = group_data
        valid_keys = positions[None, :] < group_len[:, None]

        def forward(params_now, inputs):
            return layer(params_now, inputs, valid_keys)
        encoded, pullback = jax.vjp(forward, parameters, group_states)
        param_grads, input_grad = pullback(group_grad)
        carried = jax.tree.map(add_pair, carried, param_grads)
        return (carried, (encoded.astype(jnp.bfloat16), input_grad))
    zeros = tuple((jnp.zeros(weight_item.shape, jnp.float32) for weight_item in parameters))
    totals, (encoded, input_grad) = lax.scan(step, zeros, (flat_states, flat_grad, flat_len))
    return (encoded.reshape(MICRO, SEQS, SEQ_LEN, D), input_grad.reshape(MICRO, SEQS, SEQ_LEN, D), totals[0], totals[1], totals[2], totals[3], totals[4], totals[5], totals[6], totals[7], totals[8], totals[9], totals[10], totals[11], totals[12])
```

```python
import functools
import itertools
import math

import jax
import jax.numpy as jnp
from jax import lax
from jax.experimental import pallas as pl
from jax.experimental.pallas import tpu as pltpu
from jax.sharding import PartitionSpec as P

MESH = pl.DeviceIdType.MESH
BF = jnp.bfloat16
F32 = jnp.float32
WIDTH = 768
UNIT = 48
LANES = 128
PARTS = 6

ORDERS = (
    ("z1", "z3", "y1", "y3", "x1"),
    ("y1", "y3", "z1", "z3", "x3"),
    ("y3", "z1", "z3", "x1", "y1"),
    ("y1", "z3", "x1", "z1", "y3"),
    ("y1", "z3", "x3", "y3", "z1"),
    ("z1", "y3", "x3", "y1", "z3"),
)


def position():
    dp = lax.axis_index("dp")
    rep = lax.axis_index("rep")
    return {"core": dp % 2, "y": (dp // 2) % 4, "z": dp // 16, "x": rep * 2 + (dp // 8) % 2}


def device_of(place):
    dp = ((place["z"] * 2 + place["x"] % 2) * 4 + place["y"]) * 2 + place["core"]
    return (dp, place["x"] // 2)


def hop(place, link):
    moved = dict(place)
    if link == "core":
        moved["core"] = 1 - place["core"]
    elif link[1] == "1":
        p = place[link[0]]
        moved[link[0]] = p + 1 - 2 * (p % 2)
    elif link[1] == "3":
        moved[link[0]] = 3 - place[link[0]]
    else:
        moved[link[0]] = (place[link[0]] + 2) % 4
    return moved


def boxes(place, links):
    y, z, x = place["y"], place["z"], place["x"] % 2
    if "y1" in links and "y3" in links:
        ys = [((0, 2), (0, 2))]
    elif "y1" in links:
        ys = [((0, 2), (y // 2, 1))]
    elif "y3" in links:
        ys = [((y % 2, 1), (y // 2, 1)), ((1 - y % 2, 1), (1 - y // 2, 1))]
    else:
        ys = [((y % 2, 1), (y // 2, 1))]
    if "z1" in links and "z3" in links:
        zs = [(0, 4)]
    elif "z1" in links:
        zs = [((z // 2) * 2, 2)]
    elif "z3" in links:
        zs = [(z, 1), (3 - z, 1)]
    else:
        zs = [(z, 1)]
    xs = (0, 2) if "x1" in links or "x3" in links else (x, 1)
    return [(ylow, zz, xs, yhigh) for (ylow, yhigh) in ys for zz in zs]


def slices(phase, core, box, part):
    ylow, z, x, yhigh = (pl.ds(*s) for s in box)
    cols = pl.ds(part * LANES, LANES)
    if phase < 2:
        return (ylow, pl.ds(core, 1), z, x, yhigh, slice(None), cols)
    return (z, x, yhigh, ylow, pl.ds(core, 1), slice(None), cols)


SHAPES = (
    (2, 2, 4, 2, 2, UNIT, WIDTH),
    (2, 2, 4, 2, 2, UNIT, WIDTH),
    (4, 2, 2, 2, 2, UNIT, WIDTH),
)


def size_box(count):
    sizes = {1: (1, 1, 1, 1), 2: (1, 1, 1, 2), 4: (1, 1, 2, 2), 8: (1, 2, 2, 2), 16: (1, 4, 2, 2), 32: (2, 4, 2, 2)}[count]
    return tuple((0, n) for n in sizes)


def wait_units(ref, phase, count, part, sem):
    view = ref.at[slices(phase, 0, size_box(count), part)]
    pltpu.make_async_copy(view, view, sem).wait()


def remote(src, dst, send_sem, recv_sem, place):
    return pltpu.make_async_remote_copy(
        src_ref=src, dst_ref=dst, send_sem=send_sem, recv_sem=recv_sem,
        device_id=device_of(place), device_id_type=MESH,
    )


def greet(places):
    barrier = pltpu.get_barrier_semaphore()
    for place in places:
        pl.semaphore_signal(barrier, inc=1, device_id=device_of(place), device_id_type=MESH)
    pl.semaphore_wait(barrier, len(places))


def member_of(place):
    return (place["y"] % 2) * 2 + place["core"]


def mates(here):
    return [hop(here, "core"), hop(here, "y1"), hop(hop(here, "core"), "y1")]


def own_box(here):
    return boxes(here, ())[0]
def ag_kernel(first_ref, up_ref, down_ref, wa, wb, wc, stage, landed, tall, unit, local_sem, mate_send, mate_recv, send, recv, sib_send, sib_recv):
    here = position()
    me = member_of(here)
    sibling = hop(here, "core")
    greet([hop(here, l) for l in ("y1", "y3", "z1", "z3", "x1", "x3", "core")] + [mates(here)[2]])
    weights = (wa, wb, wc)
    copies = []
    for which, src in enumerate((first_ref, up_ref)):
        for i in range(4):
            stage[which, i, 0:12, :] = src[:, i * WIDTH:(i + 1) * WIDTH].astype(F32)
    for which in range(2):
        for k, mate in enumerate(mates(here)):
            cp = remote(stage.at[which, member_of(mate)], landed.at[which, me], mate_send.at[which, k], mate_recv.at[which, k], mate)
            cp.start()
            copies.append(cp)
    for cp in copies:
        cp.wait()
    for which in range(2):
        for i in range(4):
            @pl.when(me == i)
            def _():
                tall[which, 12 * i:12 * i + 12, :] = stage[which, i, 0:12, :]
            @pl.when(me != i)
            def _():
                tall[which, 12 * i:12 * i + 12, :] = landed[which, i, 0:12, :]
        unit[which] = tall[which].astype(BF)
    unit[2] = down_ref[...]
    own = own_box(here)
    cps = []
    for phase in range(3):
        w = weights[phase]
        ylow, z, x, yhigh = (s for s, n in own)
        at = (ylow, here["core"], z, x, yhigh) if phase < 2 else (z, x, yhigh, ylow, here["core"])
        cp = pltpu.make_async_copy(unit.at[phase], w.at[at], local_sem.at[phase])
        cp.start()
        cps.append(cp)
    for cp in cps:
        cp.wait()
    for step in range(6):
        for phase in range(3):
            w = weights[phase]
            for part in range(PARTS):
                order = ORDERS[part]
                if step > 0:
                    wait_units(w, phase, 1 << (step - 1), part, recv.at[phase, part, step - 1])
                if step < 5:
                    there = hop(here, order[step])
                    for box in boxes(here, order[:step]):
                        view = w.at[slices(phase, here["core"], box, part)]
                        remote(view, view, send.at[phase, part, step], recv.at[phase, part, step], there).start()
                if step >= 4:
                    new = boxes(here, order[:4]) if step == 4 else boxes(hop(here, order[4]), order[:4])
                    for box in new:
                        view = w.at[slices(phase, here["core"], box, part)]
                        remote(view, view, sib_send.at[phase, part], sib_recv.at[phase, part], sibling).start()
    for phase in range(3):
        w = weights[phase]
        for part in range(PARTS):
            wait_units(w, phase, 32, part, sib_recv.at[phase, part])
            wait_units(w, phase, 32, part, sib_send.at[phase, part])
            for s in range(5):
                wait_units(w, phase, 1 << s, part, send.at[phase, part, s])

def gather_weights(first, up, down, cid=1, space=pl.ANY):
    vm = pl.BlockSpec(memory_space=pltpu.VMEM)
    return pl.pallas_call(
        ag_kernel,
        out_shape=[jax.ShapeDtypeStruct(s, BF) for s in SHAPES],
        in_specs=[vm]*3,
        out_specs=[pl.BlockSpec(memory_space=space)]*3,
        scratch_shapes=[
            pltpu.VMEM((2, 4, 16, WIDTH), F32), pltpu.VMEM((2, 4, 16, WIDTH), F32), pltpu.VMEM((2, UNIT, WIDTH), F32), pltpu.VMEM((3, UNIT, WIDTH), BF),
            pltpu.SemaphoreType.DMA((3,)),
            pltpu.SemaphoreType.DMA((2, 3)), pltpu.SemaphoreType.DMA((2, 3)),
            pltpu.SemaphoreType.DMA((3, PARTS, 5)), pltpu.SemaphoreType.DMA((3, PARTS, 5)),
            pltpu.SemaphoreType.DMA((3, PARTS)), pltpu.SemaphoreType.DMA((3, PARTS)),
        ],
        compiler_params=pltpu.CompilerParams(collective_id=cid, has_side_effects=True, vmem_limit_bytes=60 * 2**20),
    )(first, up, down)


START = {16: 0, 8: 16, 4: 24, 2: 28, 1: 30}
VLINKS = ("core", "y1", "y3", "x1", "z1", "z3")


def box_count(box):
    return box[0][1] * box[1][1] * box[2][1] * box[3][1]


def rs_kernel(ga, gb, gc, gv, oqkv, oout, oup, odown, ovec, rda, rdb, rdc, rk, rx, tall, stage, landed, rv,
              sib_send, sib_recv, send, recv, rep_send, rep_recv, mate_send, mate_recv, vsend, vrecv):
    here = position()
    me = member_of(here)
    sibling = hop(here, "core")
    twin = hop(here, "x2")
    greet([hop(here, l) for l in ("y1", "y3", "z1", "z3", "x1", "x3", "core", "x2")] + [mates(here)[2]])
    grads = (ga, gb, gc)
    rds = (rda, rdb, rdc)
    every = ((0, 2), (0, 4), (0, 2), (0, 2))
    dp = ((here["z"] * 2 + here["x"] % 2) * 4 + here["y"]) * 2 + here["core"]

    def vec_start(r):
        if r < 6:
            n = 32 >> r
            there = hop(here, VLINKS[5 - r])
            to = ((there["z"] * 2 + there["x"] % 2) * 4 + there["y"]) * 2 + there["core"]
            src = gv.at[pl.ds(to // n * n, n)]
            dst = rv.at[pl.ds(64 - 2 * n, n)]
        else:
            n, there, src, dst = 1, twin, gv.at[pl.ds(dp, 1)], rv.at[pl.ds(63, 1)]
        cp = remote(src, dst, vsend.at[r], vrecv.at[r], there)
        cp.start()
        return cp

    def vec_add(r, cp):
        cp.wait()
        n = 32 >> r if r < 6 else 1
        lo = 64 - 2 * n if r < 6 else 63
        mine = pl.ds(dp // n * n, n)
        gv[mine] = gv[mine] + rv[lo:lo + n]

    def sib_slices(phase, part):
        cols = pl.ds(part * LANES, LANES)
        if phase < 2:
            return (slice(None), pl.ds(0, 1), slice(None), slice(None), slice(None), slice(None), cols)
        return (slice(None), slice(None), slice(None), slice(None), pl.ds(0, 1), slice(None), cols)

    def sib_copy(phase, part):
        return remote(grads[phase].at[slices(phase, 1 - here["core"], every, part)], rds[phase].at[sib_slices(phase, part)],
                      sib_send.at[phase, part], sib_recv.at[phase, part], sibling)

    def sib_add(phase, part):
        sib_copy(phase, part).wait()
        for z in range(4):
            box = ((0, 2), (z, 1), (0, 2), (0, 2))
            at = slices(phase, here["core"], box, part)
            g = grads[phase]
            g[at] = (g[at].astype(F32) + rds[phase][slices(phase, 0, box, part)].astype(F32)).astype(BF)

    def hop_start(phase, part, step):
        order = ORDERS[part]
        there = hop(here, order[step])
        at = START[1 << step]
        for box in boxes(there, order[:step]):
            n = box_count(box)
            src = grads[phase].at[slices(phase, here["core"], box, part)]
            shape = src.shape[:5]
            dst = rk.at[phase, pl.ds(at, n)].reshape(shape + (UNIT, WIDTH)).at[:, :, :, :, :, :, pl.ds(part * LANES, LANES)]
            remote(src, dst, send.at[phase, part, step], recv.at[phase, part, step], there).start()
            at += n

    def hop_add(phase, part, step):
        order = ORDERS[part]
        n = 1 << step
        at = START[n]
        cols = pl.ds(part * LANES, LANES)
        view = rk.at[phase, pl.ds(at, n), :, cols]
        pltpu.make_async_copy(view, view, recv.at[phase, part, step]).wait()
        for box in boxes(here, order[:step]):
            m = box_count(box)
            g = grads[phase]
            where = slices(phase, here["core"], box, part)
            old = g[where]
            g[where] = (old.astype(F32) + rk[phase, at:at + m, :, part * LANES:(part + 1) * LANES].reshape(old.shape).astype(F32)).astype(BF)
            at += m

    def hop_sent(phase, part, step):
        n = 1 << step
        view = rk.at[phase, pl.ds(START[n], n), :, pl.ds(part * LANES, LANES)]
        pltpu.make_async_copy(view, view, send.at[phase, part, step]).wait()

    for phase in range(3):
        for part in range(PARTS):
            sib_copy(phase, part).start()
    v = vec_start(0)
    for phase in range(3):
        for part in range(PARTS):
            sib_add(phase, part)
            hop_start(phase, part, 4)
    vec_add(0, v)
    for step in range(4, -1, -1):
        v = vec_start(5 - step)
        for phase in range(3):
            for part in range(PARTS):
                hop_add(phase, part, step)
                if step > 0:
                    hop_start(phase, part, step - 1)
            if step == 0:
                ylow, z, x, yhigh = (s for s, n in own_box(here))
                at = (ylow, here["core"], z, x, yhigh) if phase < 2 else (z, x, yhigh, ylow, here["core"])
                remote(grads[phase].at[at], rx.at[phase], rep_send.at[phase], rep_recv.at[phase], twin).start()
        vec_add(5 - step, v)
    v = vec_start(6)
    ylow, z, x, yhigh = (s for s, n in own_box(here))
    swaps = []
    for phase in range(3):
        at = (ylow, here["core"], z, x, yhigh) if phase < 2 else (z, x, yhigh, ylow, here["core"])
        remote(grads[phase].at[at], rx.at[phase], rep_send.at[phase], rep_recv.at[phase], twin).wait()
        total = grads[phase][at].astype(F32) + rx[phase].astype(F32)
        if phase == 2:
            odown[...] = total
        else:
            tall[phase] = total
            for i in range(4):
                stage[phase, i, 0:12, :] = tall[phase, 12 * i:12 * i + 12, :]
            for k, mate in enumerate(mates(here)):
                cp = remote(stage.at[phase, member_of(mate)], landed.at[phase, me], mate_send.at[phase, k], mate_recv.at[phase, k], mate)
                cp.start()
                swaps.append(cp)
    vec_add(6, v)
    ovec[...] = gv[dp]
    for cp in swaps:
        cp.wait()
    for phase in range(2):
        for i in range(4):
            dst = oup.at[:, pl.ds(i * WIDTH, WIDTH)] if phase else (oqkv.at[:, pl.ds(i * WIDTH, WIDTH)] if i < 3 else oout)

            @pl.when(me == i)
            def _():
                dst[...] = stage[phase, i, 0:12, :]

            @pl.when(me != i)
            def _():
                dst[...] = landed[phase, i, 0:12, :]
    for phase in range(3):
        for part in range(PARTS):
            for step in range(5):
                hop_sent(phase, part, step)


def scatter_grads(ga, gb, gc, gv, cid=2):
    vm = pl.BlockSpec(memory_space=pltpu.VMEM)
    dma = pltpu.SemaphoreType.DMA
    return pl.pallas_call(
        rs_kernel,
        out_shape=[jax.ShapeDtypeStruct((12, 3 * WIDTH), F32), jax.ShapeDtypeStruct((12, WIDTH), F32), jax.ShapeDtypeStruct((12, 4 * WIDTH), F32),
                   jax.ShapeDtypeStruct((UNIT, WIDTH), F32), jax.ShapeDtypeStruct((8, LANES), F32)],
        in_specs=[vm] * 4,
        out_specs=[vm] * 5,
        scratch_shapes=[
            pltpu.VMEM((2, 1, 4, 2, 2, UNIT, WIDTH), BF), pltpu.VMEM((2, 1, 4, 2, 2, UNIT, WIDTH), BF), pltpu.VMEM((4, 2, 2, 2, 1, UNIT, WIDTH), BF),
            pltpu.VMEM((3, 31, UNIT, WIDTH), BF), pltpu.VMEM((3, UNIT, WIDTH), BF),
            pltpu.VMEM((2, UNIT, WIDTH), F32), pltpu.VMEM((2, 4, 16, WIDTH), F32), pltpu.VMEM((2, 4, 16, WIDTH), F32), pltpu.VMEM((64, 8, LANES), F32),
            dma((3, PARTS)), dma((3, PARTS)), dma((3, PARTS, 5)), dma((3, PARTS, 5)), dma((3,)), dma((3,)), dma((2, 3)), dma((2, 3)), dma((7,)), dma((7,)),
        ],
        input_output_aliases={},
        compiler_params=pltpu.CompilerParams(collective_id=cid, has_side_effects=True, vmem_limit_bytes=60 * 2**20),
    )(ga, gb, gc, gv)


HD = 64


epsilon = 1e-05


def layer_norm(hidden, gain, shift):
    center = hidden - jnp.mean(hidden, -1, keepdims=True)
    variance = jnp.mean(center * center, -1, keepdims=True)
    return center * lax.rsqrt(variance + epsilon) * gain + shift


def gelu_exact(value):
    return 0.5 * value * (1.0 + lax.erf(value * (1.0 / math.sqrt(2.0))))


def contract_rows(left, right):
    return lax.dot_general(
        left, right, (((0,), (0,)), ((), ())), preferred_element_type=jnp.float32
    )


def times_transposed(left, right):
    return lax.dot_general(
        left, right, (((1,), (1,)), ((), ())), preferred_element_type=jnp.float32
    )


def masked_scores(queries, key_rows, valid_keys):
    scores = jnp.einsum("bqhd,bkhd->bhqk", queries, key_rows, preferred_element_type=jnp.float32)
    scores = scores * (1.0 / math.sqrt(HD))
    return jnp.where(valid_keys[:, None, None, :], scores, -1000000000.0)


def column_sum(matrix):
    return jnp.sum(matrix.astype(jnp.float32), 0)


def forward(weights, states, valid_keys):
    (
        qkv_weight,
        query_bias,
        value_bias,
        out_weight,
        out_bias,
        attn_gain,
        attn_shift,
        up_weight,
        up_bias,
        down_weight,
        down_bias,
        ffn_gain,
        ffn_shift,
    ) = weights
    seq_count, length, width = states.shape
    head_count = width // HD
    shaped = (seq_count, length, head_count, HD)
    flat_rows = states.reshape(seq_count * length, width)
    joint_proj = jnp.dot(flat_rows, qkv_weight, preferred_element_type=jnp.float32)
    queries = (joint_proj[:, :width] + query_bias.astype(jnp.float32)).astype(jnp.bfloat16)
    key_rows = joint_proj[:, width : 2 * width].astype(jnp.bfloat16)
    values = (joint_proj[:, 2 * width :] + value_bias.astype(jnp.float32)).astype(jnp.bfloat16)
    scores = masked_scores(queries.reshape(shaped), key_rows.reshape(shaped), valid_keys)
    row_peak = jnp.max(scores, -1, keepdims=True)
    exponent = jnp.exp(scores - row_peak)
    row_total = jnp.sum(exponent, -1, keepdims=True)
    attention = (exponent / row_total).astype(jnp.bfloat16)
    log_total = row_peak + jnp.log(row_total)
    mixed_heads = jnp.einsum(
        "bhqk,bkhd->bqhd", attention, values.reshape(shaped), preferred_element_type=jnp.float32
    )
    mixed_heads = mixed_heads.reshape(seq_count * length, width).astype(jnp.bfloat16)
    branch = jnp.dot(mixed_heads, out_weight, preferred_element_type=jnp.float32) + out_bias.astype(
        jnp.float32
    )
    residual = flat_rows.astype(jnp.float32) + branch
    normed = layer_norm(residual, attn_gain.astype(jnp.float32), attn_shift.astype(jnp.float32))
    normed_low = normed.astype(jnp.bfloat16)
    pre_act = jnp.dot(normed_low, up_weight, preferred_element_type=jnp.float32) + up_bias.astype(
        jnp.float32
    )
    activation = gelu_exact(pre_act).astype(jnp.bfloat16)
    update = jnp.dot(
        activation, down_weight, preferred_element_type=jnp.float32
    ) + down_bias.astype(jnp.float32)
    second = normed + update
    encoded = layer_norm(second, ffn_gain.astype(jnp.float32), ffn_shift.astype(jnp.float32))
    saved_state = (
        flat_rows,
        queries,
        key_rows,
        values,
        log_total,
        mixed_heads,
        residual,
        normed_low,
        pre_act,
        activation,
        second,
        valid_keys,
    )
    return (encoded, saved_state)


def backward(weights, saved_state, cotangent):
    (
        qkv_weight,
        query_bias,
        value_bias,
        out_weight,
        out_bias,
        attn_gain,
        attn_shift,
        up_weight,
        up_bias,
        down_weight,
        down_bias,
        ffn_gain,
        ffn_shift,
    ) = weights
    (
        flat_rows,
        queries,
        key_rows,
        values,
        log_total,
        mixed_heads,
        residual,
        normed_low,
        pre_act,
        activation,
        second,
        valid_keys,
    ) = saved_state
    row_count, width = flat_rows.shape
    seq_count, length = valid_keys.shape
    shaped = (seq_count, length, width // HD, HD)
    scale = 1.0 / math.sqrt(HD)
    ignored, ffn_pull = jax.vjp(
        layer_norm, second, ffn_gain.astype(jnp.float32), ffn_shift.astype(jnp.float32)
    )
    grad_second, grad_ffn_gain, grad_ffn_shift = ffn_pull(cotangent)
    grad_update = grad_second.astype(jnp.bfloat16)
    grad_down = contract_rows(activation, grad_update)
    grad_down_bias = column_sum(grad_update)
    grad_activation = times_transposed(grad_update, down_weight)
    ignored, gelu_pull = jax.vjp(gelu_exact, pre_act)
    grad_pre = gelu_pull(grad_activation)[0].astype(jnp.bfloat16)
    grad_up = contract_rows(normed_low, grad_pre)
    grad_up_bias = column_sum(grad_pre)
    grad_normed = grad_second + times_transposed(grad_pre, up_weight)
    ignored, attn_pull = jax.vjp(
        layer_norm, residual, attn_gain.astype(jnp.float32), attn_shift.astype(jnp.float32)
    )
    grad_residual, grad_attn_gain, grad_attn_shift = attn_pull(grad_normed)
    grad_branch = grad_residual.astype(jnp.bfloat16)
    grad_out = contract_rows(mixed_heads, grad_branch)
    grad_out_bias = column_sum(grad_branch)
    grad_mixed = times_transposed(grad_branch, out_weight).astype(jnp.bfloat16).reshape(shaped)
    query_heads = queries.reshape(shaped)
    key_heads = key_rows.reshape(shaped)
    value_heads = values.reshape(shaped)
    scores = masked_scores(query_heads, key_heads, valid_keys)
    attention_full = jnp.exp(scores - log_total)
    attention_low = attention_full.astype(jnp.bfloat16)
    grad_attention = jnp.einsum(
        "bqhd,bkhd->bhqk", grad_mixed, value_heads, preferred_element_type=jnp.float32
    )
    grad_values = jnp.einsum(
        "bhqk,bqhd->bkhd", attention_low, grad_mixed, preferred_element_type=jnp.float32
    )
    grad_values = grad_values.reshape(row_count, width).astype(jnp.bfloat16)
    grad_scores = attention_full * (
        grad_attention - jnp.sum(attention_full * grad_attention, -1, keepdims=True)
    )
    grad_scores = grad_scores.astype(jnp.bfloat16)
    grad_queries = (
        jnp.einsum("bhqk,bkhd->bqhd", grad_scores, key_heads, preferred_element_type=jnp.float32)
        * scale
    )
    grad_queries = grad_queries.reshape(row_count, width).astype(jnp.bfloat16)
    grad_keys = (
        jnp.einsum("bhqk,bqhd->bkhd", grad_scores, query_heads, preferred_element_type=jnp.float32)
        * scale
    )
    grad_keys = grad_keys.reshape(row_count, width).astype(jnp.bfloat16)
    grad_joint = jnp.concatenate([grad_queries, grad_keys, grad_values], axis=1)
    grad_qkv = contract_rows(flat_rows, grad_joint)
    grad_query_bias = column_sum(grad_queries)
    grad_value_bias = column_sum(grad_values)
    input_grad = grad_residual + times_transposed(grad_joint, qkv_weight)
    gradients = (
        grad_qkv,
        grad_query_bias,
        grad_value_bias,
        grad_out,
        grad_out_bias,
        grad_attn_gain,
        grad_attn_shift,
        grad_up,
        grad_up_bias,
        grad_down,
        grad_down_bias,
        grad_ffn_gain,
        grad_ffn_shift,
    )
    return (gradients, input_grad)


def spread(vector):
    return vector.reshape(64, -1)


def local(states, qkv_weight, query_bias, value_bias, out_weight, out_bias, attn_gain, attn_shift, up_weight, up_bias,
          down_weight, down_bias, ffn_gain, ffn_shift, out_grad, lengths):
    micro_count, seq_count, length, width = states.shape
    positions = jnp.arange(length, dtype=jnp.int32)
    valid = (positions[None, None, :] < lengths[:, :, None]).reshape(micro_count * seq_count, length)
    short = (query_bias, value_bias, out_bias, attn_gain, attn_shift, down_bias, ffn_gain, ffn_shift)
    packed = lax.all_gather(jnp.concatenate(short + (up_bias,)), "dp", axis=0)
    qb, vb, ob, ag, ash, db, fg, fs = (packed[:, 12 * i:12 * i + 12].reshape(width) for i in range(8))
    ub = packed[:, 96:].reshape(4 * width)
    wa, wb, wc = gather_weights(jnp.concatenate([qkv_weight, out_weight], 1), up_weight, down_weight)
    wa = wa.reshape(4, width, width)
    wb = wb.reshape(4, width, width)
    full = (jnp.concatenate([wa[0], wa[1], wa[2]], 1), qb, vb, wa[3], ob, ag, ash,
            jnp.concatenate([wb[i] for i in range(4)], 1), ub, wc.reshape(4 * width, width), db, fg, fs)
    x = states.reshape(micro_count * seq_count, length, width)
    encoded, saved = forward(full, x, valid)
    grads, input_grad = backward(full, saved, out_grad.reshape(-1, width).astype(F32))
    gqkv, gqb, gvb, gow, gob, gag, gash, gup, gub, gdn, gdb, gfg, gfs = grads
    low = lambda a: a.astype(BF)
    ga = jnp.stack([low(gqkv[:, i * width:(i + 1) * width]) for i in range(3)] + [low(gow)]).reshape(SHAPES[0])
    gb = jnp.stack([low(gup[:, i * width:(i + 1) * width]) for i in range(4)]).reshape(SHAPES[1])
    gc = low(gdn).reshape(SHAPES[2])
    row = jnp.concatenate([spread(v) for v in (gqb, gvb, gob, gag, gash, gdb, gfg, gfs)], 1)
    row = jnp.pad(row, ((0, 0), (0, 32)))
    gv = jnp.concatenate([row[:, None], jnp.pad(spread(gub), ((0, 0), (0, 80)))[:, None], jnp.zeros((64, 6, 128), F32)], 1)
    oqkv, oout, oup, odown, ovec = scatter_grads(ga, gb, gc, gv)
    o = [ovec[0, 12 * i:12 * i + 12] for i in range(8)]
    return (encoded.reshape(states.shape).astype(BF), input_grad.reshape(states.shape), oqkv, o[0], o[1], oout, o[2], o[3], o[4],
            oup, ovec[1, :48], odown, o[5], o[6], o[7])


def solution(mesh):
    return jax.shard_map(
        local,
        mesh=mesh,
        in_specs=(
            P(None, ("dp", "rep"), None, None),
            P("dp", None),
            P("dp"),
            P("dp"),
            P("dp", None),
            P("dp"),
            P("dp"),
            P("dp"),
            P("dp", None),
            P("dp"),
            P("dp", None),
            P("dp"),
            P("dp"),
            P("dp"),
            P(None, ("dp", "rep"), None, None),
            P(None, ("dp", "rep")),
        ),
        out_specs=(
            P(None, ("dp", "rep"), None, None),
            P(None, ("dp", "rep"), None, None),
            P("dp", None),
            P("dp"),
            P("dp"),
            P("dp", None),
            P("dp"),
            P("dp"),
            P("dp"),
            P("dp", None),
            P("dp"),
            P("dp", None),
            P("dp"),
            P("dp"),
            P("dp"),
        ),
        check_vma=False,
    )
```

```python
import collections
import math
import types

import jax
import jax.numpy as jnp
from jax import lax
from jax.experimental import pallas as pl
from jax.experimental.pallas import tpu as pltpu
from jax.sharding import PartitionSpec as P

Place = collections.namedtuple("Place", "core y z x")
MESH = pl.DeviceIdType.MESH
BF = jnp.bfloat16
F32 = jnp.float32
WIDTH = 768
UNIT = 48
LANES = 128
PARTS = 6

CORE, Y1, Y3, Z1, Z3, X1, X2, X3 = (0, 0), (1, 1), (1, 3), (2, 1), (2, 3), (3, 1), (3, 2), (3, 3)

ORDERS = (
    (Z1, Z3, Y1, Y3, X1),
    (Y1, Y3, Z1, Z3, X3),
    (Y3, Z1, Z3, X1, Y1),
    (Y1, Z3, X1, Z1, Y3),
    (Y1, Z3, X3, Y3, Z1),
    (Z1, Y3, X3, Y1, Z3),
)


def position():
    dp = lax.axis_index("dp")
    rep = lax.axis_index("rep")
    return Place(dp % 2, (dp // 2) % 4, dp // 16, rep * 2 + (dp // 8) % 2)


def device_of(place):
    dp = ((place.z * 2 + place.x % 2) * 4 + place.y) * 2 + place.core
    return (dp, place.x // 2)


def hop(place, link):
    axis, how = link
    p = place[axis]
    moved = (1 - p, p + 1 - 2 * (p % 2), (p + 2) % 4, 3 - p)[how]
    return Place(*(moved if i == axis else q for i, q in enumerate(place)))


def boxes(place, links):
    y, z, x = place.y, place.z, place.x % 2
    if Y1 in links and Y3 in links:
        ys = [((0, 2), (0, 2))]
    elif Y1 in links:
        ys = [((0, 2), (y // 2, 1))]
    elif Y3 in links:
        ys = [((y % 2, 1), (y // 2, 1)), ((1 - y % 2, 1), (1 - y // 2, 1))]
    else:
        ys = [((y % 2, 1), (y // 2, 1))]
    if Z1 in links and Z3 in links:
        zs = [(0, 4)]
    elif Z1 in links:
        zs = [((z // 2) * 2, 2)]
    elif Z3 in links:
        zs = [(z, 1), (3 - z, 1)]
    else:
        zs = [(z, 1)]
    xs = (0, 2) if X1 in links or X3 in links else (x, 1)
    return [(ylow, zz, xs, yhigh) for (ylow, yhigh) in ys for zz in zs]


def slices(phase, core, box, part):
    ylow, z, x, yhigh = (pl.ds(*s) for s in box)
    cols = pl.ds(part * LANES, LANES)
    if phase < 2:
        return (ylow, pl.ds(core, 1), z, x, yhigh, slice(None), cols)
    return (z, x, yhigh, ylow, pl.ds(core, 1), slice(None), cols)


SHAPES = (
    (2, 2, 4, 2, 2, UNIT, WIDTH),
    (2, 2, 4, 2, 2, UNIT, WIDTH),
    (4, 2, 2, 2, 2, UNIT, WIDTH),
)


def size_box(count):
    sizes = {1: (1, 1, 1, 1), 2: (1, 1, 1, 2), 4: (1, 1, 2, 2), 8: (1, 2, 2, 2), 16: (1, 4, 2, 2), 32: (2, 4, 2, 2)}[count]
    return tuple((0, n) for n in sizes)


def wait_units(ref, phase, count, part, sem):
    view = ref.at[slices(phase, 0, size_box(count), part)]
    pltpu.make_async_copy(view, view, sem).wait()


def remote(src, dst, send_sem, recv_sem, place):
    return pltpu.make_async_remote_copy(
        src_ref=src, dst_ref=dst, send_sem=send_sem, recv_sem=recv_sem,
        device_id=device_of(place), device_id_type=MESH,
    )


def greet(places):
    barrier = pltpu.get_barrier_semaphore()
    for place in places:
        pl.semaphore_signal(barrier, inc=1, device_id=device_of(place), device_id_type=MESH)
    pl.semaphore_wait(barrier, len(places))


def member_of(place):
    return (place.y % 2) * 2 + place.core


def mates(here):
    return [hop(here, CORE), hop(here, Y1), hop(hop(here, CORE), Y1)]


def own_box(here):
    return boxes(here, ())[0]


HALF = 256
SEQ = 256
TOKENS = 512
epsilon = 1e-05
NT = (((1,), (1,)), ((), ()))
TN = (((0,), (0,)), ((), ()))
VQ, VV, VO, VAG, VAS, VD, VFG, VFS, VUP = range(9)


def mm(left, right):
    return jnp.dot(left, right, preferred_element_type=F32)


def mm_nt(left, right):
    return lax.dot_general(left, right, NT, preferred_element_type=F32)


def mm_tn(left, right):
    return lax.dot_general(left, right, TN, preferred_element_type=F32)


def normalise(value):
    center = value - jnp.mean(value, -1, keepdims=True)
    scale = lax.rsqrt(jnp.mean(center * center, -1, keepdims=True) + epsilon)
    return center * scale, scale


def norm_back(cot, gain, n, scale):
    e = cot * gain
    return scale * (e - jnp.mean(e, -1, keepdims=True) - n * jnp.mean(e * n, -1, keepdims=True))


def half_masks():
    lane = lax.broadcasted_iota(jnp.int32, (1, LANES), 1)
    low = (lane < 64).astype(F32).astype(BF)
    return low, (1.0 - low.astype(F32)).astype(BF)


def column_total(ref_rows):
    return jnp.sum(ref_rows.astype(F32), 0, keepdims=True)


class Layer:
    def __init__(self, slabs, grads, vec, lengths, x, og, enc, gvec, b):
        self.slabs, self.grads, self.vec, self.lengths, self.x, self.og = slabs, grads, vec, lengths, x, og
        self.enc, self.gvec, self.b = enc, gvec, b

    def v(self, row):
        return self.vec[row:row + 1, :]

    def project(self):
        b = self.b
        for j, (dst, row) in enumerate(((b.q, VQ), (b.k, None), (b.v, VV))):
            for n in range(3):
                cols = slice(n * 256, n * 256 + 256)
                acc = mm(self.x[...], self.slabs[0].at[j][:, cols])
                if row is not None:
                    acc = acc + self.vec[row:row + 1, cols]
                low = acc.astype(BF)
                if j == 0:
                    low = (low.astype(F32) * 0.125).astype(BF)
                dst[:, cols] = low

    def attend(self):
        b = self.b
        masks = half_masks()

        def body(i, _):
            s, p = i // 6, i % 6
            rows = pl.ds(pl.multiple_of(s * SEQ, SEQ), SEQ)
            cols = pl.ds(pl.multiple_of(p * LANES, LANES), LANES)
            q, k, v = b.q[rows, cols], b.k[rows, cols], b.v[rows, cols]
            length = self.lengths[s, 0]
            key = lax.broadcasted_iota(jnp.int32, (SEQ, SEQ), 0)
            out = None
            for a in range(2):
                st = mm_nt(k * masks[a], q)
                st = jnp.where(key < length, st, -1e9)
                e = jnp.exp(st - jnp.max(st, 0, keepdims=True))
                att = e * (1.0 / jnp.sum(e, 0, keepdims=True))
                b.p[i * 2 + a] = att
                o = mm_tn(v * masks[a], att.astype(BF))
                out = o if out is None else out + o
            b.mixed[rows, cols] = out.T.astype(BF)
            return 0

        lax.fori_loop(0, 12, body, 0)

    def attn_out(self):
        b = self.b
        for n in range(3):
            cols = slice(n * 256, n * 256 + 256)
            acc = mm(b.mixed[...], self.slabs[0].at[3][:, cols]) + self.vec[VO:VO + 1, cols]
            b.n1[:, cols] = self.x[:, cols].astype(F32) + acc

        def body(r, _):
            rows = pl.ds(pl.multiple_of(r * 32, 32), 32)
            n, scale = normalise(b.n1[rows, :])
            b.n1[rows, :] = n
            b.r1[rows, :] = jnp.broadcast_to(scale, (32, LANES))
            b.nl[rows, :] = (n * self.v(VAG) + self.v(VAS)).astype(BF)
            return 0

        lax.fori_loop(0, TOKENS // 32, body, 0)

    def feed(self):
        b = self.b

        def body(j, _):
            w = self.slabs[1].at[j]
            for n in range(3):
                cols = slice(n * 256, n * 256 + 256)
                bias = self.vec[pl.ds(VUP + j, 1), cols]
                for h in range(2):
                    rows = slice(h * 256, h * 256 + 256)
                    pre = mm(b.nl[rows, :], w[:, cols]) + bias
                    cdf = 0.5 * (1.0 + lax.erf(pre * (1.0 / math.sqrt(2.0))))
                    pdf = jnp.exp(pre * pre * -0.5) * (1.0 / math.sqrt(2.0 * math.pi))
                    b.act[j, rows, cols] = (pre * cdf).astype(BF)
                    b.gp[j, rows, cols] = cdf + pre * pdf
            return 0

        lax.fori_loop(0, 4, body, 0)

    def feed_out(self):
        b = self.b
        for n in range(3):
            cols = slice(n * 256, n * 256 + 256)
            acc = self.b.n1[:, cols] * self.vec[VAG:VAG + 1, cols] + self.vec[VAS:VAS + 1, cols] + self.vec[VD:VD + 1, cols]
            for j in range(4):
                acc = acc + mm(b.act[j], self.slabs[2].at[j][:, cols])
            b.second[:, cols] = acc

        def body(r, sums):
            rows = pl.ds(pl.multiple_of(r * 32, 32), 32)
            n, scale = normalise(b.second[rows, :])
            c = self.og[rows, :].astype(F32)
            self.enc[rows, :] = (n * self.v(VFG) + self.v(VFS)).astype(BF)
            g = norm_back(c, self.v(VFG), n, scale)
            b.second[rows, :] = g
            low = g.astype(BF)
            b.nl[rows, :] = low
            return sums[0] + column_total(c * n), sums[1] + column_total(c), sums[2] + column_total(low)

        zero = jnp.zeros((1, WIDTH), F32)
        sums = lax.fori_loop(0, TOKENS // 32, body, (zero, zero, zero))
        self.gvec[VFG:VFG + 1, :], self.gvec[VFS:VFS + 1, :], self.gvec[VD:VD + 1, :] = sums

    def down_grads(self):
        b = self.b

        def body(j, _):
            for n in range(3):
                cols = slice(n * 256, n * 256 + 256)
                self.grads[2][j, :, cols] = mm_tn(b.act[j], b.nl[:, cols]).astype(BF)
            return 0

        lax.fori_loop(0, 4, body, 0)

    def feed_back(self):
        b = self.b

        def body(j, _):
            w = self.slabs[2].at[j]
            for n in range(3):
                cols = slice(n * 256, n * 256 + 256)
                total = jnp.zeros((1, 256), F32)
                for h in range(2):
                    rows = slice(h * 256, h * 256 + 256)
                    acc = mm_nt(b.nl[rows, :], w[cols, :])
                    low = (acc * b.gp[j, rows, cols]).astype(BF)
                    b.gpre[j, rows, cols] = low
                    total = total + column_total(low)
                self.gvec[pl.ds(VUP + j, 1), cols] = total
            return 0

        lax.fori_loop(0, 4, body, 0)

    def up_grads(self):
        b = self.b

        def body(j, _):
            for n in range(3):
                cols = slice(n * 256, n * 256 + 256)
                self.grads[1][j, :, cols] = mm(b.nlt[...], b.gpre[j, :, cols]).astype(BF)
            return 0

        lax.fori_loop(0, 4, body, 0)

    def norm1_back(self):
        b = self.b
        for n in range(3):
            cols = slice(n * 256, n * 256 + 256)
            acc = b.second[:, cols]
            for j in range(4):
                acc = acc + mm_nt(b.gpre[j], self.slabs[1].at[j][cols, :])
            b.second[:, cols] = acc

    def norm1_rows(self):
        b = self.b

        def body(r, sums):
            rows = pl.ds(pl.multiple_of(r * 32, 32), 32)
            c = b.second[rows, :]
            n = b.n1[rows, :]
            g = norm_back(c, self.v(VAG), n, b.r1[rows, 0:1])
            b.second[rows, :] = g
            low = g.astype(BF)
            b.nl[rows, :] = low
            return sums[0] + column_total(c * n), sums[1] + column_total(c), sums[2] + column_total(low)

        zero = jnp.zeros((1, WIDTH), F32)
        sums = lax.fori_loop(0, TOKENS // 32, body, (zero, zero, zero))
        self.gvec[VAG:VAG + 1, :], self.gvec[VAS:VAS + 1, :], self.gvec[VO:VO + 1, :] = sums

    def out_grads(self):
        b = self.b
        for n in range(3):
            cols = slice(n * 256, n * 256 + 256)
            self.grads[0][3, :, cols] = mm_tn(b.mixed[...], b.nl[:, cols]).astype(BF)
        for n in range(3):
            cols = slice(n * 256, n * 256 + 256)
            b.mixed[:, cols] = mm_nt(b.nl[...], self.slabs[0].at[3][cols, :]).astype(BF)

    def attend_back(self, p):
        b = self.b
        masks = half_masks()
        cols = slice(p * LANES, p * LANES + LANES)

        def body(s, _):
            rows = pl.ds(pl.multiple_of(s * SEQ, SEQ), SEQ)
            q, k, v, do = b.q[rows, cols], b.k[rows, cols], b.v[rows, cols], b.mixed[rows, cols]
            dq = dk = dv = 0.0
            for a in range(2):
                att = b.p[s * 12 + p * 2 + a]
                do_a = do * masks[a]
                dv = dv + mm(att.astype(BF), do_a)
                dp = mm_nt(v, do_a)
                ds = (att * (dp - jnp.sum(att * dp, 0, keepdims=True))).astype(BF)
                dk = dk + mm(ds, q * masks[a])
                dq = dq + mm_tn(k * masks[a], ds)
            b.gpre[0, rows, cols] = (dq.T * 0.125).astype(BF)
            b.gpre[1, rows, cols] = dk.astype(BF)
            b.gpre[2, rows, cols] = dv.astype(BF)
            return 0

        lax.fori_loop(0, 2, body, 0)
        both = mm(b.xt[...], jnp.concatenate([b.gpre[0, :, cols], b.gpre[1, :, cols]], 1))
        self.grads[0][0, :, cols] = both[:, :LANES].astype(BF)
        self.grads[0][1, :, cols] = both[:, LANES:].astype(BF)
        self.grads[0][2, :, cols] = mm(b.xt[...], b.gpre[2, :, cols]).astype(BF)

    def qkv_totals(self):
        b = self.b
        self.gvec[VQ:VQ + 1, :] = column_total(b.gpre[0])
        self.gvec[VV:VV + 1, :] = column_total(b.gpre[2])

    def input_grad(self, n):
        b = self.b
        cols = slice(n * 256, n * 256 + 256)
        acc = b.second[:, cols]
        for j in range(3):
            acc = acc + mm_nt(b.gpre[j], self.slabs[0].at[j][cols, :])
        b.second[:, cols] = acc


BUFFERS = dict(
    q=((TOKENS, WIDTH), BF), k=((TOKENS, WIDTH), BF), v=((TOKENS, WIDTH), BF), p=((24, SEQ, SEQ), F32),
    mixed=((TOKENS, WIDTH), BF), n1=((TOKENS, WIDTH), F32), r1=((TOKENS, LANES), F32), nl=((TOKENS, WIDTH), BF),
    act=((4, TOKENS, WIDTH), BF), gp=((4, TOKENS, WIDTH), F32), second=((TOKENS, WIDTH), F32),
    gpre=((4, TOKENS, WIDTH), BF), xt=((WIDTH, TOKENS), BF), nlt=((WIDTH, TOKENS), BF),
)


START = {16: 0, 8: 16, 4: 24, 2: 28, 1: 30}
VLINKS = (CORE, Y1, Y3, X1, Z1, Z3)
EVERY = ((0, 2), (0, 4), (0, 2), (0, 2))
SCRATCH = dict(
    wa=(SHAPES[0], BF), wb=(SHAPES[1], BF), wc=(SHAPES[2], BF), ga=(SHAPES[0], BF),
    rdb=((2, 1, 4, 2, 2, UNIT, WIDTH), BF), rdc=((4, 2, 2, 2, 1, UNIT, WIDTH), BF),
    rk=((3, 31, UNIT, WIDTH), BF), rx=((3, UNIT, WIDTH), BF), tall=((2, UNIT, WIDTH), F32),
    stage=((2, 4, 16, WIDTH), F32), landed=((2, 4, 16, WIDTH), F32),
    vt=((64, 8, LANES), F32), gv=((64, 8, LANES), F32), rv=((64, 8, LANES), F32),
    vec=((16, WIDTH), F32), gvec=((16, WIDTH), F32),
    x=((TOKENS, WIDTH), BF),
)
SEMS = dict(
    loads=(4,), mate_send=(2, 3), mate_recv=(2, 3), send=(3, PARTS, 5), recv=(3, PARTS, 5),
    sib_send=(3, PARTS), sib_recv=(3, PARTS), vsend=(6,), vrecv=(6,),
    gsib_send=(3, PARTS), gsib_recv=(3, PARTS), gsend=(3, PARTS, 5), grecv=(3, PARTS, 5),
    rep_send=(3,), rep_recv=(3,), gmate_send=(2, 3), gmate_recv=(2, 3), gvsend=(7,), gvrecv=(7,),
)


def box_count(box):
    return box[0][1] * box[1][1] * box[2][1] * box[3][1]


def split3(value):
    high = value.astype(BF)
    rest = value - high.astype(F32)
    mid = rest.astype(BF)
    return high, mid, (rest - mid.astype(F32)).astype(BF)


def owner_masks(block):
    d = lax.broadcasted_iota(jnp.int32, (64, WIDTH), 0)
    c = lax.broadcasted_iota(jnp.int32, (64, WIDTH), 1)
    if block is None:
        return d == (c * 43691) >> 19
    return d == 16 * block + ((c * 43691) >> 21)


def lane_picks(row):
    c = lax.broadcasted_iota(jnp.int32, (WIDTH, LANES), 0)
    lane = lax.broadcasted_iota(jnp.int32, (WIDTH, LANES), 1)
    if row is None:
        return (lane == c - 48 * ((c * 43691) >> 21)).astype(F32).astype(BF)
    return (lane == 12 * row + c - 12 * ((c * 43691) >> 19)).astype(F32).astype(BF)


def mega_kernel(lengths, vec_in, qkv_in, out_in, up_in, down_in, x_in, og_in,
                enc_out, sgrad_out, oqkv, oout, oup, odown, ovec, *scratch):
    r = b = types.SimpleNamespace(**dict(zip([*SCRATCH, *BUFFERS, *SEMS], scratch)))
    here = position()
    me = member_of(here)
    sibling = hop(here, CORE)
    twin = hop(here, X2)
    dp = device_of(here)[0]
    weights = (r.wa, r.wb, r.wc)
    grads = (r.ga, r.wb, r.wc)
    rds = (r.act.at[pl.ds(0, 3)].reshape((2, 1, 4, 2, 2, UNIT, WIDTH)), r.rdb, r.rdc)
    slabs = [w.reshape(4, WIDTH, WIDTH) for w in weights]
    gslabs = [w.reshape(4, WIDTH, WIDTH) for w in grads]
    layer = Layer(slabs, gslabs, r.vec, lengths, r.x, r.x, r.x, r.gvec, b)

    def own_at(phase):
        ylow, z, x, yhigh = (s for s, n in own_box(here))
        return (ylow, here.core, z, x, yhigh) if phase < 2 else (z, x, yhigh, ylow, here.core)

    def mate_copy(which, k):
        mate = mates(here)[k]
        return remote(r.stage.at[which, member_of(mate)], r.landed.at[which, me],
                      r.mate_send.at[which, k], r.mate_recv.at[which, k], mate)

    def assemble(which):
        for k in range(3):
            mate_copy(which, k).wait()
        for i in range(4):
            @pl.when(me == i)
            def _():
                r.tall[which, 12 * i:12 * i + 12, :] = r.stage[which, i, 0:12, :]

            @pl.when(me != i)
            def _():
                r.tall[which, 12 * i:12 * i + 12, :] = r.landed[which, i, 0:12, :]
        weights[which][own_at(which)] = r.tall[which].astype(BF)

    def gather(phase, step):
        w = weights[phase]
        for part in range(PARTS):
            order = ORDERS[part]
            if step > 0:
                wait_units(w, phase, 1 << (step - 1), part, r.recv.at[phase, part, step - 1])
            if step < 5:
                there = hop(here, order[step])
                for box in boxes(here, order[:step]):
                    view = w.at[slices(phase, here.core, box, part)]
                    remote(view, view, r.send.at[phase, part, step], r.recv.at[phase, part, step], there).start()
            if step >= 4:
                new = boxes(here, order[:4]) if step == 4 else boxes(hop(here, order[4]), order[:4])
                for box in new:
                    view = w.at[slices(phase, here.core, box, part)]
                    remote(view, view, r.sib_send.at[phase, part], r.sib_recv.at[phase, part], sibling).start()

    def gathered(phase):
        for part in range(PARTS):
            wait_units(weights[phase], phase, 32, part, r.sib_recv.at[phase, part])

    def gather_sent(phase):
        for part in range(PARTS):
            wait_units(weights[phase], phase, 32, part, r.sib_send.at[phase, part])
            for s in range(5):
                wait_units(weights[phase], phase, 1 << s, part, r.send.at[phase, part, s])

    def vec_copy(k):
        n = 1 << k
        view = r.vt.at[pl.ds(dp // n * n, n)]
        return remote(view, view, r.vsend.at[k], r.vrecv.at[k], hop(here, VLINKS[k]))

    def vec_next(k):
        vec_copy(k - 1).wait()
        if k < 6:
            vec_copy(k).start()

    def expand():
        first = r.vt[:, 0, :].astype(BF)
        second = r.vt[:, 1, :].astype(BF)
        mask = owner_masks(None)
        for row in range(8):
            t = mm_nt(first, lane_picks(row))
            r.vec[row:row + 1, :] = jnp.sum(jnp.where(mask, t, 0.0), 0, keepdims=True)
        t = mm_nt(second, lane_picks(None))
        for j in range(4):
            r.vec[8 + j:9 + j, :] = jnp.sum(jnp.where(owner_masks(j), t, 0.0), 0, keepdims=True)

    def sib_slices(phase, part):
        cols = pl.ds(part * LANES, LANES)
        if phase < 2:
            return (slice(None), pl.ds(0, 1), slice(None), slice(None), slice(None), slice(None), cols)
        return (slice(None), slice(None), slice(None), slice(None), pl.ds(0, 1), slice(None), cols)

    def sib_copy(phase, part):
        return remote(grads[phase].at[slices(phase, 1 - here.core, EVERY, part)], rds[phase].at[sib_slices(phase, part)],
                      r.gsib_send.at[phase, part], r.gsib_recv.at[phase, part], sibling)

    def sib_add(phase, part):
        sib_copy(phase, part).wait()
        for z in range(4):
            box = ((0, 2), (z, 1), (0, 2), (0, 2))
            at = slices(phase, here.core, box, part)
            g = grads[phase]
            g[at] = g[at] + rds[phase][slices(phase, 0, box, part)]

    def hop_start(phase, part, step):
        order = ORDERS[part]
        there = hop(here, order[step])
        at = START[1 << step]
        for box in boxes(there, order[:step]):
            n = box_count(box)
            src = grads[phase].at[slices(phase, here.core, box, part)]
            dst = r.rk.at[phase, pl.ds(at, n)].reshape(src.shape[:5] + (UNIT, WIDTH)).at[:, :, :, :, :, :, pl.ds(part * LANES, LANES)]
            remote(src, dst, r.gsend.at[phase, part, step], r.grecv.at[phase, part, step], there).start()
            at += n

    def hop_add(phase, part, step):
        n = 1 << step
        at = START[n]
        cols = pl.ds(part * LANES, LANES)
        view = r.rk.at[phase, pl.ds(at, n), :, cols]
        pltpu.make_async_copy(view, view, r.grecv.at[phase, part, step]).wait()
        for box in boxes(here, ORDERS[part][:step]):
            m = box_count(box)
            g = grads[phase]
            where = slices(phase, here.core, box, part)
            old = g[where]
            g[where] = old + r.rk[phase, at:at + m, :, part * LANES:(part + 1) * LANES].reshape(old.shape)
            at += m

    def rep_copy(phase):
        return remote(grads[phase].at[own_at(phase)], r.rx.at[phase], r.rep_send.at[phase], r.rep_recv.at[phase], twin)

    def reduce_sib(phase):
        for part in range(PARTS):
            sib_copy(phase, part).start()

    def reduce_first(phase, parts=range(PARTS)):
        for part in parts:
            sib_add(phase, part)
            hop_start(phase, part, 4)

    def reduce(phase, step):
        for part in range(PARTS):
            hop_add(phase, part, step)
            if step > 0:
                hop_start(phase, part, step - 1)
        if step == 0:
            rep_copy(phase).start()

    def gmate_copy(which, k):
        mate = mates(here)[k]
        return remote(r.stage.at[which, member_of(mate)], r.landed.at[which, me],
                      r.gmate_send.at[which, k], r.gmate_recv.at[which, k], mate)

    def reduce_last(phase):
        rep_copy(phase).wait()
        total = grads[phase][own_at(phase)].astype(F32) + r.rx[phase].astype(F32)
        if phase == 2:
            odown[...] = total
            return
        r.tall[phase] = total
        for i in range(4):
            r.stage[phase, i, 0:12, :] = r.tall[phase, 12 * i:12 * i + 12, :]
        for k in range(3):
            gmate_copy(phase, k).start()

    def deliver(phase):
        for k in range(3):
            gmate_copy(phase, k).wait()
        for i in range(4):
            cols = pl.ds(i * WIDTH, WIDTH)
            dst = oup.at[:, cols] if phase else (oqkv.at[:, cols] if i < 3 else oout)

            @pl.when(me == i)
            def _():
                dst[...] = r.stage[phase, i, 0:12, :]

            @pl.when(me != i)
            def _():
                dst[...] = r.landed[phase, i, 0:12, :]

    def reduce_sent(phase):
        for part in range(PARTS):
            for step in range(5):
                n = 1 << step
                view = r.rk.at[phase, pl.ds(START[n], n), :, pl.ds(part * LANES, LANES)]
                pltpu.make_async_copy(view, view, r.gsend.at[phase, part, step]).wait()

    def pack_rows(rows):
        mask = owner_masks(None)
        first = jnp.zeros((64, LANES), F32)
        for row in rows:
            value = jnp.where(mask, jnp.broadcast_to(r.gvec[row:row + 1, :], (64, WIDTH)), 0.0)
            picks = lane_picks(row)
            for piece in split3(value):
                first = first + mm(piece, picks)
        return first

    def pack():
        second = jnp.zeros((64, LANES), F32)
        picks = lane_picks(None)
        for j in range(4):
            value = jnp.where(owner_masks(j), jnp.broadcast_to(r.gvec[8 + j:9 + j, :], (64, WIDTH)), 0.0)
            for piece in split3(value):
                second = second + mm(piece, picks)
        r.gv[:, 0, :] = pack_rows((VO, VAG, VAS, VD, VFG, VFS))
        r.gv[:, 1, :] = second

    def gvec_copy(k):
        if k < 6:
            n = 32 >> k
            there = hop(here, VLINKS[5 - k])
            to = device_of(there)[0]
            src, dst = r.gv.at[pl.ds(to // n * n, n)], r.rv.at[pl.ds(64 - 2 * n, n)]
        else:
            there, src, dst = twin, r.gv.at[pl.ds(dp, 1)], r.rv.at[pl.ds(63, 1)]
        return remote(src, dst, r.gvsend.at[k], r.gvrecv.at[k], there)

    def gvec_next(k):
        gvec_copy(k).wait()
        n = 32 >> k if k < 6 else 1
        lo = 64 - 2 * n if k < 6 else 63
        mine = pl.ds(dp // n * n, n)
        r.gv[mine] = r.gv[mine] + r.rv[lo:lo + n]
        if k < 6:
            gvec_copy(k + 1).start()

    x_load = pltpu.make_async_copy(x_in, r.x, r.loads.at[0])
    og_load = pltpu.make_async_copy(og_in, r.x, r.loads.at[1])
    x_load.start()
    near = [hop(here, link) for link in (Y1, Y3, Z1, Z3, X1, X3, CORE, X2)] + [mates(here)[2]]
    barrier = pltpu.get_barrier_semaphore()
    for place in near:
        pl.semaphore_signal(barrier, inc=1, device_id=device_of(place), device_id_type=MESH)
    for i in range(4):
        r.stage[0, i, 0:12, :] = (qkv_in[:, i * WIDTH:(i + 1) * WIDTH] if i < 3 else out_in[...]).astype(F32)
        r.stage[1, i, 0:12, :] = up_in[:, i * WIDTH:(i + 1) * WIDTH].astype(F32)
    r.vt[dp] = vec_in[...]
    weights[2][own_at(2)] = down_in[...]
    pl.semaphore_wait(barrier, len(near))
    for which in range(2):
        for k in range(3):
            mate_copy(which, k).start()
    vec_copy(0).start()
    assemble(0)
    gather(0, 0)
    assemble(1)
    gather(1, 0)
    vec_next(1)
    gather(2, 0)
    gather(0, 1)
    vec_next(2)
    gather(1, 1)
    gather(0, 2)
    vec_next(3)
    gather(2, 1)
    gather(0, 3)
    vec_next(4)
    gather(1, 2)
    gather(2, 2)
    gather(0, 4)
    vec_next(5)
    x_load.wait()
    b.xt[...] = r.x[...].T
    gather(1, 3)
    vec_next(6)
    expand()
    gather(0, 5)
    gathered(0)
    gather(1, 4)
    gather(2, 3)
    layer.project()
    gather(2, 4)
    layer.attend()
    gather(1, 5)
    layer.attn_out()
    og_load.start()
    b.nlt[...] = b.nl[...].T
    gather(2, 5)
    gathered(1)
    layer.feed()
    og_load.wait()
    gathered(2)
    layer.feed_out()
    enc_store = pltpu.make_async_copy(r.x, enc_out, r.loads.at[2])
    enc_store.start()
    layer.feed_back()
    gather_sent(2)
    layer.down_grads()
    reduce_sib(2)
    layer.norm1_back()
    reduce_first(2)
    layer.norm1_rows()
    gather_sent(1)
    layer.up_grads()
    reduce_sib(1)
    reduce(2, 4)
    layer.out_grads()
    reduce_first(1)
    reduce(2, 3)
    pack()
    for p in range(PARTS):
        layer.attend_back(p)
        sib_copy(0, p).start()
        if p > 0:
            reduce_first(0, (p - 1,))
        if p < 3:
            reduce(2, 2 - p)
        elif p == 3:
            reduce_last(2)
        if p < 5:
            reduce(1, 4 - p)
        else:
            reduce_last(1)
    layer.qkv_totals()
    r.gv[:, 0, :] = r.gv[:, 0, :] + pack_rows((VQ, VV))
    gvec_copy(0).start()
    layer.input_grad(0)
    reduce_first(0, (5,))
    layer.input_grad(1)
    gvec_next(0)
    layer.input_grad(2)
    sgrad_store = pltpu.make_async_copy(b.second, sgrad_out, r.loads.at[3])
    sgrad_store.start()
    for step in range(4, -1, -1):
        reduce(0, step)
        gvec_next(5 - step)
    deliver(1)
    reduce_last(0)
    gvec_next(6)
    ovec[...] = r.gv[dp]
    deliver(0)
    for phase in range(3):
        reduce_sent(phase)
    gather_sent(0)
    enc_store.wait()
    sgrad_store.wait()


def run_layer(lengths, vec_in, qkv, out, up, down, x, og):
    vm = pl.BlockSpec(memory_space=pltpu.VMEM)
    hb = pl.BlockSpec(memory_space=pl.ANY)
    return pl.pallas_call(
        mega_kernel,
        out_shape=[
            jax.ShapeDtypeStruct((TOKENS, WIDTH), BF), jax.ShapeDtypeStruct((TOKENS, WIDTH), F32),
            jax.ShapeDtypeStruct((12, 3 * WIDTH), F32), jax.ShapeDtypeStruct((12, WIDTH), F32),
            jax.ShapeDtypeStruct((12, 4 * WIDTH), F32), jax.ShapeDtypeStruct((UNIT, WIDTH), F32), jax.ShapeDtypeStruct((8, LANES), F32),
        ],
        in_specs=[pl.BlockSpec(memory_space=pltpu.SMEM)] + [vm] * 5 + [hb] * 2,
        out_specs=[hb, hb] + [vm] * 5,
        scratch_shapes=[pltpu.VMEM(s, d) for s, d in SCRATCH.values()] + [pltpu.VMEM(s, d) for s, d in BUFFERS.values()]
        + [pltpu.SemaphoreType.DMA(s) for s in SEMS.values()],
        compiler_params=pltpu.CompilerParams(collective_id=1, has_side_effects=True, vmem_limit_bytes=63 * 2**20),
    )(lengths, vec_in, qkv, out, up, down, x, og)


def local(states, qkv_weight, query_bias, value_bias, out_weight, out_bias, attn_gain, attn_shift, up_weight, up_bias,
          down_weight, down_bias, ffn_gain, ffn_shift, out_grad, lengths):
    short = (query_bias, value_bias, out_bias, attn_gain, attn_shift, down_bias, ffn_gain, ffn_shift)
    rows = jnp.stack([jnp.pad(jnp.concatenate(short), (0, 32)), jnp.pad(up_bias, (0, 80))])
    vec_in = jnp.pad(rows, ((0, 6), (0, 0))).astype(F32)
    enc, sgrad, oqkv, oout, oup, odown, ovec = run_layer(
        lengths, vec_in, qkv_weight, out_weight, up_weight, down_weight,
        states.reshape(TOKENS, WIDTH), out_grad.reshape(TOKENS, WIDTH))
    o = [ovec[0, 12 * i:12 * i + 12] for i in range(8)]
    return (enc.reshape(states.shape), sgrad.reshape(states.shape), oqkv, o[0], o[1], oout, o[2], o[3], o[4],
            oup, ovec[1, :48], odown, o[5], o[6], o[7])


def solution(mesh):
    return jax.shard_map(
        local,
        mesh=mesh,
        in_specs=(
            P(None, ("dp", "rep"), None, None),
            P("dp", None),
            P("dp"),
            P("dp"),
            P("dp", None),
            P("dp"),
            P("dp"),
            P("dp"),
            P("dp", None),
            P("dp"),
            P("dp", None),
            P("dp"),
            P("dp"),
            P("dp"),
            P(None, ("dp", "rep"), None, None),
            P(None, ("dp", "rep")),
        ),
        out_specs=(
            P(None, ("dp", "rep"), None, None),
            P(None, ("dp", "rep"), None, None),
            P("dp", None),
            P("dp"),
            P("dp"),
            P("dp", None),
            P("dp"),
            P("dp"),
            P("dp"),
            P("dp", None),
            P("dp"),
            P("dp", None),
            P("dp"),
            P("dp"),
            P("dp"),
        ),
        check_vma=False,
    )
```

```python
import collections
import math
import types

import jax
import jax.numpy as jnp
from jax import lax
from jax.experimental import pallas as pl
from jax.experimental.pallas import tpu as pltpu
from jax.sharding import PartitionSpec as P

Place = collections.namedtuple("Place", "core y z x")
MESH = pl.DeviceIdType.MESH
BF = jnp.bfloat16
F32 = jnp.float32
WIDTH = 768
UNIT = 48
LANES = 128
PARTS = 6

CORE, Y1, Y3, Z1, Z3, X1, X2, X3 = (0, 0), (1, 1), (1, 3), (2, 1), (2, 3), (3, 1), (3, 2), (3, 3)
Y2, Z2 = (1, 2), (2, 2)

ORDERS = (
    (Z1, Z3, Y1, Y3, X1),
    (Y1, Y3, Z1, Z3, X3),
    (Y3, Z1, Z3, X1, Y1),
    (Y1, Z3, X1, Z1, Y3),
    (Y1, Z3, X3, Y3, Z1),
    (Z1, Y3, X3, Y1, Z3),
)


def position():
    dp = lax.axis_index("dp")
    rep = lax.axis_index("rep")
    return Place(dp % 2, (dp // 2) % 4, dp // 16, rep * 2 + (dp // 8) % 2)


def device_of(place):
    dp = ((place.z * 2 + place.x % 2) * 4 + place.y) * 2 + place.core
    return (dp, place.x // 2)


def hop(place, link):
    axis, how = link
    p = place[axis]
    moved = (1 - p, p + 1 - 2 * (p % 2), (p + 2) % 4, 3 - p)[how]
    return Place(*(moved if i == axis else q for i, q in enumerate(place)))


def boxes(place, links):
    y, z, x = place.y, place.z, place.x % 2
    if Y1 in links and Y3 in links:
        ys = [((0, 2), (0, 2))]
    elif Y1 in links:
        ys = [((0, 2), (y // 2, 1))]
    elif Y3 in links:
        ys = [((y % 2, 1), (y // 2, 1)), ((1 - y % 2, 1), (1 - y // 2, 1))]
    else:
        ys = [((y % 2, 1), (y // 2, 1))]
    if Z1 in links and Z3 in links:
        zs = [(0, 4)]
    elif Z1 in links:
        zs = [((z // 2) * 2, 2)]
    elif Z3 in links:
        zs = [(z, 1), (3 - z, 1)]
    else:
        zs = [(z, 1)]
    xs = (0, 2) if X1 in links or X3 in links else (x, 1)
    return [(ylow, zz, xs, yhigh) for (ylow, yhigh) in ys for zz in zs]


def slices(phase, core, box, part):
    ylow, z, x, yhigh = (pl.ds(*s) for s in box)
    cols = pl.ds(part * LANES, LANES)
    if phase < 2:
        return (ylow, pl.ds(core, 1), z, x, yhigh, slice(None), cols)
    return (z, x, yhigh, ylow, pl.ds(core, 1), slice(None), cols)


SHAPES = (
    (2, 2, 4, 2, 2, UNIT, WIDTH),
    (2, 2, 4, 2, 2, UNIT, WIDTH),
    (4, 2, 2, 2, 2, UNIT, WIDTH),
)


def size_box(count):
    sizes = {1: (1, 1, 1, 1), 2: (1, 1, 1, 2), 4: (1, 1, 2, 2), 8: (1, 2, 2, 2), 16: (1, 4, 2, 2), 32: (2, 4, 2, 2)}[count]
    return tuple((0, n) for n in sizes)


def wait_units(ref, phase, count, part, sem):
    view = ref.at[slices(phase, 0, size_box(count), part)]
    pltpu.make_async_copy(view, view, sem).wait()


def remote(src, dst, send_sem, recv_sem, place):
    return pltpu.make_async_remote_copy(
        src_ref=src, dst_ref=dst, send_sem=send_sem, recv_sem=recv_sem,
        device_id=device_of(place), device_id_type=MESH,
    )


def greet(places):
    barrier = pltpu.get_barrier_semaphore()
    for place in places:
        pl.semaphore_signal(barrier, inc=1, device_id=device_of(place), device_id_type=MESH)
    pl.semaphore_wait(barrier, len(places))


def member_of(place):
    return (place.y % 2) * 2 + place.core


def mates(here):
    return [hop(here, CORE), hop(here, Y1), hop(hop(here, CORE), Y1)]


def own_box(here):
    return boxes(here, ())[0]


def trio(place, order):
    a, b = hop(place, order[0]), hop(place, order[1])
    return a, b, hop(a, order[1])


def halves(found):
    if len(found) == 2:
        return [found[:1], found[1:]]
    ylow, (start, n), x, yhigh = found[0]
    return [[(ylow, (start, n // 2), x, yhigh)], [(ylow, (start + n // 2, n // 2), x, yhigh)]]


HALF = 256
SEQ = 256
TOKENS = 512
epsilon = 1e-05
NT = (((1,), (1,)), ((), ()))
TN = (((0,), (0,)), ((), ()))
VQ, VV, VO, VAG, VAS, VD, VFG, VFS, VUP = range(9)


def mm(left, right):
    return jnp.dot(left, right, preferred_element_type=F32)


def mm_nt(left, right):
    return lax.dot_general(left, right, NT, preferred_element_type=F32)


def mm_tn(left, right):
    return lax.dot_general(left, right, TN, preferred_element_type=F32)


def normalise(value):
    center = value - jnp.mean(value, -1, keepdims=True)
    scale = lax.rsqrt(jnp.mean(center * center, -1, keepdims=True) + epsilon)
    return center * scale, scale


def norm_back(cot, gain, n, scale):
    e = cot * gain
    return scale * (e - jnp.mean(e, -1, keepdims=True) - n * jnp.mean(e * n, -1, keepdims=True))


def half_masks():
    lane = lax.broadcasted_iota(jnp.int32, (1, LANES), 1)
    low = (lane < 64).astype(F32).astype(BF)
    return low, (1.0 - low.astype(F32)).astype(BF)


def column_total(ref_rows):
    return jnp.sum(ref_rows.astype(F32), 0, keepdims=True)


class Layer:
    def __init__(self, slabs, grads, vec, lengths, x, og, enc, gvec, b):
        self.slabs, self.grads, self.vec, self.lengths, self.x, self.og = slabs, grads, vec, lengths, x, og
        self.enc, self.gvec, self.b = enc, gvec, b

    def v(self, row):
        return self.vec[row:row + 1, :]

    def project(self, j):
        b = self.b
        dst, row = ((b.q, VQ), (b.k, None), (b.v, VV))[j]
        for n in range(3):
            cols = slice(n * 256, n * 256 + 256)
            acc = mm(self.x[...], self.slabs[0].at[j][:, cols])
            if row is not None:
                acc = acc + self.vec[row:row + 1, cols]
            low = acc.astype(BF)
            if j == 0:
                low = (low.astype(F32) * 0.125).astype(BF)
            dst[:, cols] = low

    def attend(self):
        b = self.b
        masks = half_masks()

        def body(i, _):
            s, p = i // 6, i % 6
            rows = pl.ds(pl.multiple_of(s * SEQ, SEQ), SEQ)
            cols = pl.ds(pl.multiple_of(p * LANES, LANES), LANES)
            q, k, v = b.q[rows, cols], b.k[rows, cols], b.v[rows, cols]
            length = self.lengths[0, s]
            key = lax.broadcasted_iota(jnp.int32, (SEQ, SEQ), 0)
            out = None
            for a in range(2):
                st = mm_nt(k * masks[a], q)
                st = jnp.where(key < length, st, -1e9)
                e = jnp.exp(st - jnp.max(st, 0, keepdims=True))
                att = e * (1.0 / jnp.sum(e, 0, keepdims=True))
                b.p[i * 2 + a] = att
                o = mm_tn(v * masks[a], att.astype(BF))
                out = o if out is None else out + o
            b.mixed[rows, cols] = out.T.astype(BF)
            return 0

        lax.fori_loop(0, 12, body, 0)

    def attn_out(self):
        b = self.b
        for n in range(3):
            cols = slice(n * 256, n * 256 + 256)
            acc = mm(b.mixed[...], self.slabs[0].at[3][:, cols]) + self.vec[VO:VO + 1, cols]
            b.n1[:, cols] = self.x[:, cols].astype(F32) + acc

        def body(r, _):
            rows = pl.ds(pl.multiple_of(r * 32, 32), 32)
            n, scale = normalise(b.n1[rows, :])
            b.n1[rows, :] = n
            b.r1[rows, :] = jnp.broadcast_to(scale, (32, LANES))
            b.nl[rows, :] = (n * self.v(VAG) + self.v(VAS)).astype(BF)
            return 0

        lax.fori_loop(0, TOKENS // 32, body, 0)

    def feed(self):
        b = self.b

        def body(j, _):
            w = self.slabs[1].at[j]
            for n in range(3):
                cols = slice(n * 256, n * 256 + 256)
                bias = self.vec[pl.ds(VUP + j, 1), cols]
                for h in range(2):
                    rows = slice(h * 256, h * 256 + 256)
                    pre = mm(b.nl[rows, :], w[:, cols]) + bias
                    cdf = 0.5 * (1.0 + lax.erf(pre * (1.0 / math.sqrt(2.0))))
                    pdf = jnp.exp(pre * pre * -0.5) * (1.0 / math.sqrt(2.0 * math.pi))
                    b.act[j, rows, cols] = (pre * cdf).astype(BF)
                    b.gp[j, rows, cols] = cdf + pre * pdf
            return 0

        lax.fori_loop(0, 4, body, 0)

    def feed_out(self):
        b = self.b
        for n in range(3):
            cols = slice(n * 256, n * 256 + 256)
            acc = self.b.n1[:, cols] * self.vec[VAG:VAG + 1, cols] + self.vec[VAS:VAS + 1, cols] + self.vec[VD:VD + 1, cols]
            for j in range(4):
                acc = acc + mm(b.act[j], self.slabs[2].at[j][:, cols])
            b.second[:, cols] = acc

        def body(r, sums):
            rows = pl.ds(pl.multiple_of(r * 32, 32), 32)
            n, scale = normalise(b.second[rows, :])
            c = self.og[rows, :].astype(F32)
            self.enc[rows, :] = (n * self.v(VFG) + self.v(VFS)).astype(BF)
            g = norm_back(c, self.v(VFG), n, scale)
            b.second[rows, :] = g
            low = g.astype(BF)
            b.nl[rows, :] = low
            return sums[0] + column_total(c * n), sums[1] + column_total(c), sums[2] + column_total(low)

        zero = jnp.zeros((1, WIDTH), F32)
        sums = lax.fori_loop(0, TOKENS // 32, body, (zero, zero, zero))
        self.gvec[VFG:VFG + 1, :], self.gvec[VFS:VFS + 1, :], self.gvec[VD:VD + 1, :] = sums

    def down_grads(self, j):
        b = self.b
        for n in range(3):
            cols = slice(n * 256, n * 256 + 256)
            self.grads[2][j, :, cols] = mm_tn(b.act[j], b.nl[:, cols]).astype(BF)

    def feed_back(self, j):
        b = self.b
        w = self.slabs[2].at[j]
        for n in range(3):
            cols = slice(n * 256, n * 256 + 256)
            total = jnp.zeros((1, 256), F32)
            for h in range(2):
                rows = slice(h * 256, h * 256 + 256)
                acc = mm_nt(b.nl[rows, :], w[cols, :])
                low = (acc * b.gp[j, rows, cols]).astype(BF)
                b.gpre[j, rows, cols] = low
                total = total + column_total(low)
            self.gvec[pl.ds(VUP + j, 1), cols] = total

    def up_grads(self, j):
        b = self.b
        for n in range(3):
            cols = slice(n * 256, n * 256 + 256)
            self.grads[1][j, :, cols] = mm(b.nlt[...], b.gpre[j, :, cols]).astype(BF)

    def norm1_back(self, n):
        b = self.b
        cols = slice(n * 256, n * 256 + 256)
        acc = b.second[:, cols]
        for j in range(4):
            acc = acc + mm_nt(b.gpre[j], self.slabs[1].at[j][cols, :])
        b.second[:, cols] = acc

    def norm1_rows(self):
        b = self.b

        def body(r, sums):
            rows = pl.ds(pl.multiple_of(r * 32, 32), 32)
            c = b.second[rows, :]
            n = b.n1[rows, :]
            g = norm_back(c, self.v(VAG), n, b.r1[rows, 0:1])
            b.second[rows, :] = g
            low = g.astype(BF)
            b.nl[rows, :] = low
            return sums[0] + column_total(c * n), sums[1] + column_total(c), sums[2] + column_total(low)

        zero = jnp.zeros((1, WIDTH), F32)
        sums = lax.fori_loop(0, TOKENS // 32, body, (zero, zero, zero))
        self.gvec[VAG:VAG + 1, :], self.gvec[VAS:VAS + 1, :], self.gvec[VO:VO + 1, :] = sums

    def out_grads(self):
        b = self.b
        for n in range(3):
            cols = slice(n * 256, n * 256 + 256)
            self.grads[0][3, :, cols] = mm_tn(b.mixed[...], b.nl[:, cols]).astype(BF)

    def out_back(self):
        b = self.b
        for n in range(3):
            cols = slice(n * 256, n * 256 + 256)
            b.mixed[:, cols] = mm_nt(b.nl[...], self.slabs[0].at[3][cols, :]).astype(BF)

    def attend_back(self, p):
        b = self.b
        masks = half_masks()
        cols = slice(p * LANES, p * LANES + LANES)

        def body(s, _):
            rows = pl.ds(pl.multiple_of(s * SEQ, SEQ), SEQ)
            q, k, v, do = b.q[rows, cols], b.k[rows, cols], b.v[rows, cols], b.mixed[rows, cols]
            dq = dk = dv = 0.0
            for a in range(2):
                att = b.p[s * 12 + p * 2 + a]
                do_a = do * masks[a]
                dv = dv + mm(att.astype(BF), do_a)
                dp = mm_nt(v, do_a)
                ds = (att * (dp - jnp.sum(att * dp, 0, keepdims=True))).astype(BF)
                dk = dk + mm(ds, q * masks[a])
                dq = dq + mm_tn(k * masks[a], ds)
            b.gpre[0, rows, cols] = (dq.T * 0.125).astype(BF)
            b.gpre[1, rows, cols] = dk.astype(BF)
            b.gpre[2, rows, cols] = dv.astype(BF)
            return 0

        lax.fori_loop(0, 2, body, 0)
        both = mm(b.xt[...], jnp.concatenate([b.gpre[0, :, cols], b.gpre[1, :, cols]], 1))
        self.grads[0][0, :, cols] = both[:, :LANES].astype(BF)
        self.grads[0][1, :, cols] = both[:, LANES:].astype(BF)
        self.grads[0][2, :, cols] = mm(b.xt[...], b.gpre[2, :, cols]).astype(BF)
        self.gvec[VQ:VQ + 1, cols] = column_total(b.gpre[0, :, cols])
        self.gvec[VV:VV + 1, cols] = column_total(b.gpre[2, :, cols])

    def input_grad(self, n):
        b = self.b
        cols = slice(n * 256, n * 256 + 256)
        acc = b.second[:, cols]
        for j in range(3):
            acc = acc + mm_nt(b.gpre[j], self.slabs[0].at[j][cols, :])
        b.second[:, cols] = acc


BUFFERS = dict(
    q=((TOKENS, WIDTH), BF), k=((TOKENS, WIDTH), BF), v=((TOKENS, WIDTH), BF), p=((24, SEQ, SEQ), F32),
    mixed=((TOKENS, WIDTH), BF), n1=((TOKENS, WIDTH), F32), r1=((TOKENS, LANES), F32), nl=((TOKENS, WIDTH), BF),
    act=((4, TOKENS, WIDTH), BF), gp=((4, TOKENS, WIDTH), F32), second=((TOKENS, WIDTH), F32),
    gpre=((4, TOKENS, WIDTH), BF), xt=((WIDTH, TOKENS), BF), nlt=((WIDTH, TOKENS), BF),
)


START = {16: 0, 8: 16, 4: 24}
VLINKS = (CORE, Y1, Y3, X1, Z1, Z3)
EVERY = ((0, 2), (0, 4), (0, 2), (0, 2))
SCRATCH = dict(
    wa=(SHAPES[0], BF), wb=(SHAPES[1], BF), wc=(SHAPES[2], BF), ga=(SHAPES[0], BF),
    rdb=((2, 1, 4, 2, 2, UNIT, WIDTH), BF), rdc=((4, 2, 2, 2, 1, UNIT, WIDTH), BF),
    rk=((3, 31, UNIT, WIDTH), BF), rx=((3, UNIT, WIDTH), BF), tall=((2, UNIT, WIDTH), F32),
    stage=((2, 4, 16, WIDTH), F32), landed=((2, 4, 16, WIDTH), F32),
    vt=((64, 2, LANES), F32), gv=((64, 2, LANES), F32), rv=((64, 2, LANES), F32),
    vec=((16, WIDTH), F32), gvec=((16, WIDTH), F32),
    x=((TOKENS, WIDTH), BF), qkv_in=((12, 3 * WIDTH), BF), out_in=((12, WIDTH), BF), up_in=((12, 4 * WIDTH), BF),
)
SEMS = dict(
    loads=(8,), mate_send=(2, 3), mate_recv=(2, 3), send=(3, PARTS, 7), recv=(3, PARTS, 7),
    sib_send=(3, PARTS), sib_recv=(3, PARTS), vsend=(6,), vrecv=(6,),
    gsib_send=(3, PARTS), gsib_recv=(3, PARTS), gsend=(3, PARTS, 6), grecv=(3, PARTS, 6),
    rep_send=(3,), rep_recv=(3,), gmate_send=(2, 3), gmate_recv=(2, 3), gvsend=(7,), gvrecv=(7,),
)


def box_count(box):
    return box[0][1] * box[1][1] * box[2][1] * box[3][1]


def split3(value):
    high = value.astype(BF)
    rest = value - high.astype(F32)
    mid = rest.astype(BF)
    return high, mid, (rest - mid.astype(F32)).astype(BF)


def owner_masks(block):
    d = lax.broadcasted_iota(jnp.int32, (64, WIDTH), 0)
    c = lax.broadcasted_iota(jnp.int32, (64, WIDTH), 1)
    if block is None:
        return d == (c * 43691) >> 19
    return d == 16 * block + ((c * 43691) >> 21)


def lane_picks(row):
    c = lax.broadcasted_iota(jnp.int32, (WIDTH, LANES), 0)
    lane = lax.broadcasted_iota(jnp.int32, (WIDTH, LANES), 1)
    if row is None:
        return (lane == c - 48 * ((c * 43691) >> 21)).astype(F32).astype(BF)
    return (lane == 12 * row + c - 12 * ((c * 43691) >> 19)).astype(F32).astype(BF)


def mega_kernel(lengths, *refs):
    vecs_in, (qkv_in, out_in, up_in, down_in, x_in, og_in,
               enc_out, sgrad_out, oqkv, oout, oup, odown, ovec), scratch = refs[:9], refs[9:22], refs[22:]
    r = b = types.SimpleNamespace(**dict(zip([*SCRATCH, *BUFFERS, *SEMS], scratch)))
    here = position()
    me = member_of(here)
    sibling = hop(here, CORE)
    twin = hop(here, X2)
    dp = device_of(here)[0]
    weights = (r.wa, r.wb, r.wc)
    grads = (r.ga, r.wb, r.wc)
    rds = (r.act.at[pl.ds(0, 3)].reshape((2, 1, 4, 2, 2, UNIT, WIDTH)), r.rdb, r.rdc)
    slabs = [w.reshape(4, WIDTH, WIDTH) for w in weights]
    gslabs = [w.reshape(4, WIDTH, WIDTH) for w in grads]
    layer = Layer(slabs, gslabs, r.vec, lengths, r.x, r.x, r.x, r.gvec, b)

    def own_at(phase):
        ylow, z, x, yhigh = (s for s, n in own_box(here))
        return (ylow, here.core, z, x, yhigh) if phase < 2 else (z, x, yhigh, ylow, here.core)

    def mate_copy(which, k):
        mate = mates(here)[k]
        return remote(r.stage.at[which, member_of(mate)], r.landed.at[which, me],
                      r.mate_send.at[which, k], r.mate_recv.at[which, k], mate)

    def assemble(which):
        for k in range(3):
            mate_copy(which, k).wait()
        for i in range(4):
            @pl.when(me == i)
            def _():
                r.tall[which, 12 * i:12 * i + 12, :] = r.stage[which, i, 0:12, :]

            @pl.when(me != i)
            def _():
                r.tall[which, 12 * i:12 * i + 12, :] = r.landed[which, i, 0:12, :]
        weights[which][own_at(which)] = r.tall[which].astype(BF)

    def push(phase, part, found, slot, there):
        w = weights[phase]
        for box in found:
            view = w.at[slices(phase, here.core, box, part)]
            remote(view, view, r.send.at[phase, part, slot], r.recv.at[phase, part, slot], there).start()

    def share(phase, part, found):
        w = weights[phase]
        for box in found:
            view = w.at[slices(phase, here.core, box, part)]
            remote(view, view, r.sib_send.at[phase, part], r.sib_recv.at[phase, part], sibling).start()

    def gather_first(phase):
        for part in range(PARTS):
            for slot, there in enumerate(trio(here, ORDERS[part])):
                push(phase, part, boxes(here, ()), slot, there)

    def gather(phase, step):
        w = weights[phase]
        for part in range(PARTS):
            order = ORDERS[part]
            if step == 2:
                for slot in range(3):
                    wait_units(w, phase, 1, part, r.recv.at[phase, part, slot])
            else:
                wait_units(w, phase, 1 << (step - 1), part, r.recv.at[phase, part, step])
            there = hop(here, order[step])
            if step < 4:
                push(phase, part, boxes(here, order[:step]), step + 1, there)
            else:
                for half, found in enumerate(halves(boxes(here, order[:4]))):
                    push(phase, part, found, 5 + half, there)
                share(phase, part, boxes(here, order[:4]))

    def gather_last(phase, half):
        for part in range(PARTS):
            order = ORDERS[part]
            wait_units(weights[phase], phase, 8, part, r.recv.at[phase, part, 5 + half])
            share(phase, part, halves(boxes(hop(here, order[4]), order[:4]))[half])

    def gathered(phase):
        for part in range(PARTS):
            wait_units(weights[phase], phase, 32, part, r.sib_recv.at[phase, part])

    def gather_sent(phase):
        for part in range(PARTS):
            wait_units(weights[phase], phase, 32, part, r.sib_send.at[phase, part])
            for slot, n in enumerate((1, 1, 1, 4, 8, 8, 8)):
                wait_units(weights[phase], phase, n, part, r.send.at[phase, part, slot])

    def vec_copy(k):
        n = 1 << k
        view = r.vt.at[pl.ds(dp // n * n, n)]
        return remote(view, view, r.vsend.at[k], r.vrecv.at[k], hop(here, VLINKS[k]))

    def vec_next(k):
        vec_copy(k - 1).wait()
        if k < 6:
            vec_copy(k).start()

    def expand():
        first = r.vt[:, 0, :].astype(BF)
        second = r.vt[:, 1, :].astype(BF)
        mask = owner_masks(None)
        for row in range(8):
            t = mm_nt(first, lane_picks(row))
            r.vec[row:row + 1, :] = jnp.sum(jnp.where(mask, t, 0.0), 0, keepdims=True)
        t = mm_nt(second, lane_picks(None))
        for j in range(4):
            r.vec[8 + j:9 + j, :] = jnp.sum(jnp.where(owner_masks(j), t, 0.0), 0, keepdims=True)

    def sib_copy(phase, k):
        g, rd = grads[phase], rds[phase]
        if phase == 0:
            cols = pl.ds(k * LANES, LANES)
            src = g.at[:, pl.ds(sibling.core, 1), :, :, :, :, cols]
            dst = rd.at[:, :, :, :, :, :, cols]
        elif phase == 1:
            src, dst = g.at[k, sibling.core], rd.at[k, 0]
        else:
            src, dst = g.at[k, :, :, :, pl.ds(sibling.core, 1)], rd.at[k]
        return remote(src, dst, r.gsib_send.at[phase, k], r.gsib_recv.at[phase, k], sibling)

    def sib_add(phase, k):
        sib_copy(phase, k).wait()
        g, rd = grads[phase], rds[phase]
        for i in range(4):
            if phase == 0:
                at = slices(0, here.core, ((0, 2), (i, 1), (0, 2), (0, 2)), k)
                g[at] = g[at] + rd[slices(0, 0, ((0, 2), (i, 1), (0, 2), (0, 2)), k)]
            elif phase == 1:
                g[k, here.core, i] = g[k, here.core, i] + rd[k, 0, i]
            else:
                at = (k, i // 2, i % 2, slice(None), pl.ds(here.core, 1))
                g[at] = g[at] + rd[k, i // 2, i % 2]

    def hop_start(phase, part, step):
        order = ORDERS[part]
        cols = pl.ds(part * LANES, LANES)
        if step == 1:
            for slot, there in enumerate(trio(here, order)):
                src = grads[phase].at[slices(phase, here.core, boxes(there, ())[0], part)]
                dst = r.rk.at[phase, pl.ds(28 + slot, 1)].reshape(src.shape[:5] + (UNIT, WIDTH)).at[:, :, :, :, :, :, cols]
                remote(src, dst, r.gsend.at[phase, part, slot], r.grecv.at[phase, part, slot], there).start()
            return
        there = hop(here, order[step])
        at = START[1 << step]
        for box in boxes(there, order[:step]):
            n = box_count(box)
            src = grads[phase].at[slices(phase, here.core, box, part)]
            dst = r.rk.at[phase, pl.ds(at, n)].reshape(src.shape[:5] + (UNIT, WIDTH)).at[:, :, :, :, :, :, cols]
            remote(src, dst, r.gsend.at[phase, part, step + 1], r.grecv.at[phase, part, step + 1], there).start()
            at += n

    def hop_add(phase, part, step):
        g = grads[phase]
        cols = slice(part * LANES, part * LANES + LANES)
        if step == 1:
            where = slices(phase, here.core, boxes(here, ())[0], part)
            total = g[where].astype(F32)
            for slot in range(3):
                view = r.rk.at[phase, 28 + slot, :, cols]
                pltpu.make_async_copy(view, view, r.grecv.at[phase, part, slot]).wait()
                total = total + view[...].astype(F32).reshape(total.shape)
            g[where] = total.astype(BF)
            return
        n = 1 << step
        at = START[n]
        view = r.rk.at[phase, pl.ds(at, n), :, cols]
        pltpu.make_async_copy(view, view, r.grecv.at[phase, part, step + 1]).wait()
        for box in boxes(here, ORDERS[part][:step]):
            m = box_count(box)
            where = slices(phase, here.core, box, part)
            old = g[where]
            g[where] = old + r.rk[phase, at:at + m, :, cols].reshape(old.shape)
            at += m

    def rep_copy(phase):
        return remote(grads[phase].at[own_at(phase)], r.rx.at[phase], r.rep_send.at[phase], r.rep_recv.at[phase], twin)

    def reduce_first(phase):
        for k in range(2 if phase == 1 else 4):
            sib_add(phase, k)
        for part in range(PARTS):
            hop_start(phase, part, 4)

    def move(phase, part, step):
        hop_add(phase, part, step)
        if step > 1:
            hop_start(phase, part, step - 1)

    def reduce(phase, step):
        for part in range(PARTS):
            move(phase, part, step)
        if step == 1:
            rep_copy(phase).start()

    def first_part(part):
        sib_add(0, part)
        hop_start(0, part, 4)

    def gmate_copy(which, k):
        mate = mates(here)[k]
        return remote(r.stage.at[which, member_of(mate)], r.landed.at[which, me],
                      r.gmate_send.at[which, k], r.gmate_recv.at[which, k], mate)

    def reduce_last(phase):
        rep_copy(phase).wait()
        total = grads[phase][own_at(phase)].astype(F32) + r.rx[phase].astype(F32)
        if phase == 2:
            odown[...] = total
            return
        r.tall[phase] = total
        for i in range(4):
            r.stage[phase, i, 0:12, :] = r.tall[phase, 12 * i:12 * i + 12, :]
        for k in range(3):
            gmate_copy(phase, k).start()

    def deliver(phase):
        for k in range(3):
            gmate_copy(phase, k).wait()
        for i in range(4):
            cols = pl.ds(i * WIDTH, WIDTH)
            dst = oup.at[:, cols] if phase else (oqkv.at[:, cols] if i < 3 else oout)

            @pl.when(me == i)
            def _():
                dst[...] = r.stage[phase, i, 0:12, :]

            @pl.when(me != i)
            def _():
                dst[...] = r.landed[phase, i, 0:12, :]

    def reduce_sent(phase):
        for part in range(PARTS):
            cols = pl.ds(part * LANES, LANES)
            for slot, n in enumerate((1, 1, 1, 4, 8, 16)):
                view = r.rk.at[phase, pl.ds(0, n), :, cols]
                pltpu.make_async_copy(view, view, r.gsend.at[phase, part, slot]).wait()

    def pack_rows(rows):
        mask = owner_masks(None)
        first = jnp.zeros((64, LANES), F32)
        for row in rows:
            value = jnp.where(mask, jnp.broadcast_to(r.gvec[row:row + 1, :], (64, WIDTH)), 0.0)
            picks = lane_picks(row)
            for piece in split3(value):
                first = first + mm(piece, picks)
        return first

    def pack():
        second = jnp.zeros((64, LANES), F32)
        picks = lane_picks(None)
        for j in range(4):
            value = jnp.where(owner_masks(j), jnp.broadcast_to(r.gvec[8 + j:9 + j, :], (64, WIDTH)), 0.0)
            for piece in split3(value):
                second = second + mm(piece, picks)
        r.gv[:, 0, :] = pack_rows((VO, VAG, VAS, VD, VFG, VFS))
        r.gv[:, 1, :] = second

    def gvec_copy(k):
        if k < 6:
            n = 32 >> k
            there = hop(here, VLINKS[5 - k])
            to = device_of(there)[0]
            src, dst = r.gv.at[pl.ds(to // n * n, n)], r.rv.at[pl.ds(64 - 2 * n, n)]
        else:
            there, src, dst = twin, r.gv.at[pl.ds(dp, 1)], r.rv.at[pl.ds(63, 1)]
        return remote(src, dst, r.gvsend.at[k], r.gvrecv.at[k], there)

    def gvec_next(k):
        gvec_copy(k).wait()
        n = 32 >> k if k < 6 else 1
        lo = 64 - 2 * n if k < 6 else 63
        mine = pl.ds(dp // n * n, n)
        r.gv[mine] = r.gv[mine] + r.rv[lo:lo + n]
        if k < 6:
            gvec_copy(k + 1).start()

    near = [hop(here, link) for link in (Y1, Y3, Z1, Z3, X1, X3, CORE, X2, Y2, Z2)]
    near += [mates(here)[2], hop(hop(here, Y3), Z1), hop(hop(here, Y1), Z3)]
    barrier = pltpu.get_barrier_semaphore()
    for place in near:
        pl.semaphore_signal(barrier, inc=1, device_id=device_of(place), device_id_type=MESH)
    loads = [pltpu.make_async_copy(src, dst, r.loads.at[i]) for i, (src, dst) in enumerate((
        (qkv_in, r.qkv_in), (out_in, r.out_in), (up_in, r.up_in), (down_in, weights[2].at[own_at(2)]), (x_in, r.x)))]
    for load in loads:
        load.start()
    og_load = pltpu.make_async_copy(og_in, r.x, r.loads.at[5])
    r.vt[dp] = jnp.zeros((2, LANES), F32)
    for i in range(8):
        r.vt[dp, 0:1, 12 * i:12 * i + 12] = vecs_in[i][...].astype(F32)
    r.vt[dp, 1:2, 0:48] = vecs_in[8][...].astype(F32)
    for load in loads[:4]:
        load.wait()
    for i in range(4):
        r.stage[0, i, 0:12, :] = (r.qkv_in[:, i * WIDTH:(i + 1) * WIDTH] if i < 3 else r.out_in[...]).astype(F32)
        r.stage[1, i, 0:12, :] = r.up_in[:, i * WIDTH:(i + 1) * WIDTH].astype(F32)
    pl.semaphore_wait(barrier, len(near))
    for which in range(2):
        for k in range(3):
            mate_copy(which, k).start()
    vec_copy(0).start()
    gather_first(2)
    loads[4].wait()
    b.xt[...] = r.x[...].T
    assemble(0)
    gather_first(0)
    assemble(1)
    vec_next(1)
    gather_first(1)
    gather(0, 2)
    vec_next(2)
    gather(2, 2)
    gather(0, 3)
    vec_next(3)
    gather(1, 2)
    gather(0, 4)
    vec_next(4)
    gather(1, 3)
    vec_next(5)
    gather(2, 3)
    vec_next(6)
    expand()
    gather_last(0, 0)
    gather_last(0, 1)
    gathered(0)
    layer.project(0)
    gather(1, 4)
    layer.project(1)
    layer.project(2)
    gather(2, 4)
    layer.attend()
    gather_last(1, 0)
    gather_last(1, 1)
    layer.attn_out()
    og_load.start()
    b.nlt[...] = b.nl[...].T
    gather_last(2, 0)
    gather_last(2, 1)
    gathered(1)
    layer.feed()
    og_load.wait()
    gathered(2)
    layer.feed_out()
    enc_store = pltpu.make_async_copy(r.x, enc_out, r.loads.at[6])
    enc_store.start()
    gather_sent(2)

    def down_body(j, _):
        layer.feed_back(j)
        layer.down_grads(j)
        sib_copy(2, j).start()
        return 0

    lax.fori_loop(0, 4, down_body, 0)
    for n in range(3):
        layer.norm1_back(n)
    reduce_first(2)
    gather_sent(1)

    def up_body(i, _):
        layer.up_grads(i * 2 + sibling.core)
        sib_copy(1, i).start()
        return 0

    def up_own(i, _):
        layer.up_grads(i * 2 + here.core)
        return 0

    lax.fori_loop(0, 2, up_body, 0)
    lax.fori_loop(0, 2, up_own, 0)
    layer.norm1_rows()
    reduce_first(1)
    layer.out_grads()
    reduce(2, 4)
    layer.out_back()
    pack()
    layer.attend_back(0)
    sib_copy(0, 0).start()
    layer.attend_back(1)
    sib_copy(0, 1).start()
    reduce(1, 4)
    first_part(0)
    layer.attend_back(2)
    sib_copy(0, 2).start()
    reduce(2, 3)
    first_part(1)
    layer.attend_back(3)
    sib_copy(0, 3).start()
    reduce(1, 3)
    first_part(2)
    layer.attend_back(4)
    sib_copy(0, 4).start()
    reduce(2, 2)
    first_part(3)
    layer.attend_back(5)
    sib_copy(0, 5).start()
    first_part(4)
    r.gv[:, 0, :] = r.gv[:, 0, :] + pack_rows((VQ, VV))
    gvec_copy(0).start()
    reduce(1, 2)
    layer.input_grad(0)
    first_part(5)
    move(0, 0, 4)
    layer.input_grad(1)
    move(0, 1, 4)
    gvec_next(0)
    layer.input_grad(2)
    sgrad_store = pltpu.make_async_copy(b.second, sgrad_out, r.loads.at[7])
    sgrad_store.start()
    reduce(2, 1)
    move(0, 2, 4)
    move(0, 0, 3)
    gvec_next(1)
    move(0, 3, 4)
    move(0, 1, 3)
    reduce(1, 1)
    gvec_next(2)
    move(0, 4, 4)
    move(0, 2, 3)
    move(0, 0, 2)
    reduce_last(2)
    move(0, 5, 4)
    move(0, 3, 3)
    move(0, 1, 2)
    gvec_next(3)
    move(0, 4, 3)
    move(0, 2, 2)
    reduce_last(1)
    move(0, 5, 3)
    move(0, 3, 2)
    move(0, 4, 2)
    gvec_next(4)
    move(0, 5, 2)
    deliver(1)
    gvec_next(5)
    reduce(0, 1)
    gvec_next(6)
    ovec[...] = r.gv[dp]
    reduce_last(0)
    for phase in range(1, 3):
        reduce_sent(phase)
    gather_sent(0)
    deliver(0)
    reduce_sent(0)
    enc_store.wait()
    sgrad_store.wait()


def run_layer(lengths, vecs, qkv, out, up, down, x, og):
    vm = pl.BlockSpec(memory_space=pltpu.VMEM)
    hb = pl.BlockSpec(memory_space=pl.ANY)
    return pl.pallas_call(
        mega_kernel,
        out_shape=[
            jax.ShapeDtypeStruct((TOKENS, WIDTH), BF), jax.ShapeDtypeStruct((TOKENS, WIDTH), F32),
            jax.ShapeDtypeStruct((12, 3 * WIDTH), F32), jax.ShapeDtypeStruct((12, WIDTH), F32),
            jax.ShapeDtypeStruct((12, 4 * WIDTH), F32), jax.ShapeDtypeStruct((UNIT, WIDTH), F32), jax.ShapeDtypeStruct((2, LANES), F32),
        ],
        in_specs=[pl.BlockSpec(memory_space=pltpu.SMEM)] + [vm] * 9 + [hb] * 6,
        out_specs=[hb, hb] + [vm] * 5,
        scratch_shapes=[pltpu.VMEM(s, d) for s, d in SCRATCH.values()] + [pltpu.VMEM(s, d) for s, d in BUFFERS.values()]
        + [pltpu.SemaphoreType.DMA(s) for s in SEMS.values()],
        compiler_params=pltpu.CompilerParams(collective_id=1, has_side_effects=True, vmem_limit_bytes=63 * 2**20),
    )(lengths, *vecs, qkv, out, up, down, x, og)


def finish_kernel(*refs):
    srcs, vec, dsts, vec_outs, held, sems = refs[:6], refs[6], refs[7:13], refs[13:22], refs[22:28], refs[28]
    loads = [pltpu.make_async_copy(src, mid, sems.at[0, i]) for i, (src, mid) in enumerate(zip(srcs, held))]
    stores = [pltpu.make_async_copy(mid, dst, sems.at[1, i]) for i, (mid, dst) in enumerate(zip(held, dsts))]
    for load in loads:
        load.start()
    for i in range(8):
        vec_outs[i][...] = vec[0:1, 12 * i:12 * i + 12]
    vec_outs[8][...] = vec[1:2, 0:48]
    for load, store in zip(loads, stores):
        load.wait()
        store.start()
    for store in stores:
        store.wait()


def finish(results):
    vm = pl.BlockSpec(memory_space=pltpu.VMEM)
    hb = pl.BlockSpec(memory_space=pl.ANY)
    return pl.pallas_call(
        finish_kernel,
        out_shape=[jax.ShapeDtypeStruct(a.shape, a.dtype) for a in results[:6]]
        + [jax.ShapeDtypeStruct((1, n), F32) for n in [12] * 8 + [48]],
        in_specs=[hb] * 6 + [vm],
        out_specs=[hb] * 6 + [vm] * 9,
        scratch_shapes=[pltpu.VMEM(a.shape, a.dtype) for a in results[:6]] + [pltpu.SemaphoreType.DMA((2, 6))],
        compiler_params=pltpu.CompilerParams(vmem_limit_bytes=63 * 2**20),
    )(*results)


def local(states, qkv_weight, query_bias, value_bias, out_weight, out_bias, attn_gain, attn_shift, up_weight, up_bias,
          down_weight, down_bias, ffn_gain, ffn_shift, out_grad, lengths):
    vecs = [v.reshape(1, -1) for v in (query_bias, value_bias, out_bias, attn_gain, attn_shift, down_bias, ffn_gain, ffn_shift, up_bias)]
    results = run_layer(
        lengths.reshape(1, 2), vecs, qkv_weight, out_weight, up_weight, down_weight,
        states.reshape(TOKENS, WIDTH), out_grad.reshape(TOKENS, WIDTH))
    enc, sgrad, oqkv, oout, oup, odown, *o = finish(results)
    o = [v.reshape(-1) for v in o]
    return (enc.reshape(states.shape), sgrad.reshape(states.shape), oqkv, o[0], o[1], oout, o[2], o[3], o[4],
            oup, o[8], odown, o[5], o[6], o[7])


def solution(mesh):
    return jax.shard_map(
        local,
        mesh=mesh,
        in_specs=(
            P(None, ("dp", "rep"), None, None),
            P("dp", None),
            P("dp"),
            P("dp"),
            P("dp", None),
            P("dp"),
            P("dp"),
            P("dp"),
            P("dp", None),
            P("dp"),
            P("dp", None),
            P("dp"),
            P("dp"),
            P("dp"),
            P(None, ("dp", "rep"), None, None),
            P(None, ("dp", "rep")),
        ),
        out_specs=(
            P(None, ("dp", "rep"), None, None),
            P(None, ("dp", "rep"), None, None),
            P("dp", None),
            P("dp"),
            P("dp"),
            P("dp", None),
            P("dp"),
            P("dp"),
            P("dp"),
            P("dp", None),
            P("dp"),
            P("dp", None),
            P("dp"),
            P("dp"),
            P("dp"),
        ),
        check_vma=False,
    )
```

```python
import collections
import math
import types

import jax
import jax.numpy as jnp
from jax import lax
from jax.experimental import pallas as pl
from jax.experimental.pallas import tpu as pltpu
from jax.sharding import PartitionSpec as P

Place = collections.namedtuple("Place", "core y z x")
MESH = pl.DeviceIdType.MESH
BF = jnp.bfloat16
F32 = jnp.float32
WIDTH = 768
UNIT = 48
LANES = 128
PARTS = 6

CORE, Y1, Y3, Z1, Z3, X1, X2, X3 = (0, 0), (1, 1), (1, 3), (2, 1), (2, 3), (3, 1), (3, 2), (3, 3)
Y2, Z2 = (1, 2), (2, 2)

ORDERS = (
    (Z1, Z3, Y1, Y3, X1),
    (Y1, Y3, Z1, Z3, X3),
    (Y3, Z1, Z3, X1, Y1),
    (Y1, Z3, X1, Z1, Y3),
    (Y1, Z3, X3, Y3, Z1),
    (Z1, Y3, X3, Y1, Z3),
)


def position():
    dp = lax.axis_index("dp")
    rep = lax.axis_index("rep")
    return Place(dp % 2, (dp // 2) % 4, dp // 16, rep * 2 + (dp // 8) % 2)


def device_of(place):
    dp = ((place.z * 2 + place.x % 2) * 4 + place.y) * 2 + place.core
    return (dp, place.x // 2)


def hop(place, link):
    axis, how = link
    p = place[axis]
    moved = (1 - p, p + 1 - 2 * (p % 2), (p + 2) % 4, 3 - p)[how]
    return Place(*(moved if i == axis else q for i, q in enumerate(place)))


def boxes(place, links):
    y, z, x = place.y, place.z, place.x % 2
    if Y1 in links and Y3 in links:
        ys = [((0, 2), (0, 2))]
    elif Y1 in links:
        ys = [((0, 2), (y // 2, 1))]
    elif Y3 in links:
        ys = [((y % 2, 1), (y // 2, 1)), ((1 - y % 2, 1), (1 - y // 2, 1))]
    else:
        ys = [((y % 2, 1), (y // 2, 1))]
    if Z1 in links and Z3 in links:
        zs = [(0, 4)]
    elif Z1 in links:
        zs = [((z // 2) * 2, 2)]
    elif Z3 in links:
        zs = [(z, 1), (3 - z, 1)]
    else:
        zs = [(z, 1)]
    xs = (0, 2) if X1 in links or X3 in links else (x, 1)
    return [(ylow, zz, xs, yhigh) for (ylow, yhigh) in ys for zz in zs]


def slices(phase, core, box, part):
    ylow, z, x, yhigh = (pl.ds(*s) for s in box)
    cols = pl.ds(part * LANES, LANES)
    if phase < 2:
        return (ylow, pl.ds(core, 1), z, x, yhigh, slice(None), cols)
    return (z, x, yhigh, ylow, pl.ds(core, 1), slice(None), cols)


SHAPES = (
    (2, 2, 4, 2, 2, UNIT, WIDTH),
    (2, 2, 4, 2, 2, UNIT, WIDTH),
    (4, 2, 2, 2, 2, UNIT, WIDTH),
)


def size_box(count):
    sizes = {1: (1, 1, 1, 1), 2: (1, 1, 1, 2), 4: (1, 1, 2, 2), 8: (1, 2, 2, 2), 16: (1, 4, 2, 2), 32: (2, 4, 2, 2)}[count]
    return tuple((0, n) for n in sizes)


def wait_units(ref, phase, count, part, sem):
    view = ref.at[slices(phase, 0, size_box(count), part)]
    pltpu.make_async_copy(view, view, sem).wait()


def remote(src, dst, send_sem, recv_sem, place):
    return pltpu.make_async_remote_copy(
        src_ref=src, dst_ref=dst, send_sem=send_sem, recv_sem=recv_sem,
        device_id=device_of(place), device_id_type=MESH,
    )


def greet(places):
    barrier = pltpu.get_barrier_semaphore()
    for place in places:
        pl.semaphore_signal(barrier, inc=1, device_id=device_of(place), device_id_type=MESH)
    pl.semaphore_wait(barrier, len(places))


def member_of(place):
    return (place.y % 2) * 2 + place.core


def mates(here):
    return [hop(here, CORE), hop(here, Y1), hop(hop(here, CORE), Y1)]


def own_box(here):
    return boxes(here, ())[0]


def trio(place, order):
    a, b = hop(place, order[0]), hop(place, order[1])
    return a, b, hop(a, order[1])


def halves(found):
    if len(found) == 2:
        return [found[:1], found[1:]]
    ylow, (start, n), x, yhigh = found[0]
    return [[(ylow, (start, n // 2), x, yhigh)], [(ylow, (start + n // 2, n // 2), x, yhigh)]]


HALF = 256
SEQ = 256
TOKENS = 512
ROWS = 64
epsilon = 1e-05
NT = (((1,), (1,)), ((), ()))
TN = (((0,), (0,)), ((), ()))
VQ, VV, VO, VAG, VAS, VD, VFG, VFS, VUP = range(9)


def mm(left, right):
    return jnp.dot(left, right, preferred_element_type=F32)


def mm_nt(left, right):
    return lax.dot_general(left, right, NT, preferred_element_type=F32)


def mm_tn(left, right):
    return lax.dot_general(left, right, TN, preferred_element_type=F32)


def normalise(value):
    center = value - jnp.mean(value, -1, keepdims=True)
    scale = lax.rsqrt(jnp.mean(center * center, -1, keepdims=True) + epsilon)
    return center * scale, scale


def norm_back(cot, gain, n, scale):
    e = cot * gain
    return scale * (e - jnp.mean(e, -1, keepdims=True) - n * jnp.mean(e * n, -1, keepdims=True))


def half_masks():
    lane = lax.broadcasted_iota(jnp.int32, (1, LANES), 1)
    low = (lane < 64).astype(F32).astype(BF)
    return low, (1.0 - low.astype(F32)).astype(BF)


def column_total(ref_rows):
    return jnp.sum(ref_rows.astype(F32), 0, keepdims=True)


class Layer:
    def __init__(self, slabs, grads, vec, lengths, x, og, enc, gvec, b):
        self.slabs, self.grads, self.vec, self.lengths, self.x, self.og = slabs, grads, vec, lengths, x, og
        self.enc, self.gvec, self.b = enc, gvec, b

    def v(self, row):
        return self.vec[row:row + 1, :]

    def project(self, j):
        b = self.b
        dst, row = ((b.q, VQ), (b.k, None), (b.v, VV))[j]
        for n in range(3):
            cols = slice(n * 256, n * 256 + 256)
            acc = mm(self.x[...], self.slabs[0].at[j][:, cols])
            if row is not None:
                acc = acc + self.vec[row:row + 1, cols]
            low = acc.astype(BF)
            if j == 0:
                low = (low.astype(F32) * 0.125).astype(BF)
            dst[:, cols] = low

    def attend(self):
        b = self.b
        masks = half_masks()
        key = lax.broadcasted_iota(jnp.int32, (SEQ, SEQ), 0)

        def body(p, _):
            cols = pl.ds(pl.multiple_of(p * LANES, LANES), LANES)
            for s in range(2):
                rows = slice(s * SEQ, s * SEQ + SEQ)
                q, k, v = b.q[rows, cols], b.k[rows, cols], b.v[rows, cols]
                length = self.lengths[0, s]
                out = None
                for a in range(2):
                    st = mm_nt(k * masks[a], q)
                    st = jnp.where(key < length, st, -1e9)
                    e = jnp.exp(st - jnp.max(st, 0, keepdims=True))
                    att = e * (1.0 / jnp.sum(e, 0, keepdims=True))
                    b.p[s * 12 + p * 2 + a] = att
                    o = mm_tn(v * masks[a], att.astype(BF))
                    out = o if out is None else out + o
                b.mixed[rows, cols] = out.T.astype(BF)
            return 0

        lax.fori_loop(0, 6, body, 0)

    def attn_out(self):
        b = self.b
        for n in range(3):
            cols = slice(n * 256, n * 256 + 256)
            acc = mm(b.mixed[...], self.slabs[0].at[3][:, cols]) + self.vec[VO:VO + 1, cols]
            b.n1[:, cols] = self.x[:, cols].astype(F32) + acc

        def body(r, _):
            rows = pl.ds(pl.multiple_of(r * ROWS, ROWS), ROWS)
            n, scale = normalise(b.n1[rows, :])
            b.n1[rows, :] = n
            b.r1[rows, :] = jnp.broadcast_to(scale, (ROWS, LANES))
            b.nl[rows, :] = (n * self.v(VAG) + self.v(VAS)).astype(BF)
            return 0

        lax.fori_loop(0, TOKENS // ROWS, body, 0)

    def feed(self):
        b = self.b

        def body(j, _):
            w = self.slabs[1].at[j]
            for n in range(3):
                cols = slice(n * 256, n * 256 + 256)
                bias = self.vec[pl.ds(VUP + j, 1), cols]
                for h in range(2):
                    rows = slice(h * 256, h * 256 + 256)
                    pre = mm(b.nl[rows, :], w[:, cols]) + bias
                    cdf = 0.5 * (1.0 + lax.erf(pre * (1.0 / math.sqrt(2.0))))
                    pdf = jnp.exp(pre * pre * -0.5) * (1.0 / math.sqrt(2.0 * math.pi))
                    b.act[j, rows, cols] = (pre * cdf).astype(BF)
                    b.gp[j, rows, cols] = cdf + pre * pdf
            return 0

        lax.fori_loop(0, 4, body, 0)

    def feed_out(self):
        b = self.b
        for n in range(3):
            cols = slice(n * 256, n * 256 + 256)
            acc = self.b.n1[:, cols] * self.vec[VAG:VAG + 1, cols] + self.vec[VAS:VAS + 1, cols] + self.vec[VD:VD + 1, cols]
            for j in range(4):
                acc = acc + mm(b.act[j], self.slabs[2].at[j][:, cols])
            b.second[:, cols] = acc

        def body(r, sums):
            rows = pl.ds(pl.multiple_of(r * ROWS, ROWS), ROWS)
            n, scale = normalise(b.second[rows, :])
            c = self.og[rows, :].astype(F32)
            self.enc[rows, :] = (n * self.v(VFG) + self.v(VFS)).astype(BF)
            g = norm_back(c, self.v(VFG), n, scale)
            b.second[rows, :] = g
            low = g.astype(BF)
            b.nl[rows, :] = low
            return sums[0] + column_total(c * n), sums[1] + column_total(c), sums[2] + column_total(low)

        zero = jnp.zeros((1, WIDTH), F32)
        sums = lax.fori_loop(0, TOKENS // ROWS, body, (zero, zero, zero))
        self.gvec[VFG:VFG + 1, :], self.gvec[VFS:VFS + 1, :], self.gvec[VD:VD + 1, :] = sums

    def down_grads(self, j):
        b = self.b
        left = b.act[j].T
        for n in range(3):
            cols = slice(n * 256, n * 256 + 256)
            self.grads[2][j, :, cols] = mm(left, b.nl[:, cols]).astype(BF)

    def feed_back(self, j):
        b = self.b
        w = self.slabs[2].at[j]
        for n in range(3):
            cols = slice(n * 256, n * 256 + 256)
            total = jnp.zeros((1, 256), F32)
            for h in range(2):
                rows = slice(h * 256, h * 256 + 256)
                acc = mm_nt(b.nl[rows, :], w[cols, :])
                low = (acc * b.gp[j, rows, cols]).astype(BF)
                b.gpre[j, rows, cols] = low
                total = total + column_total(low)
            self.gvec[pl.ds(VUP + j, 1), cols] = total

    def up_grads(self, j):
        b = self.b
        for n in range(3):
            cols = slice(n * 256, n * 256 + 256)
            self.grads[1][j, :, cols] = mm(b.nlt[...], b.gpre[j, :, cols]).astype(BF)

    def norm1_back(self, n):
        b = self.b
        cols = slice(n * 256, n * 256 + 256)
        acc = b.second[:, cols]
        for j in range(4):
            acc = acc + mm_nt(b.gpre[j], self.slabs[1].at[j][cols, :])
        b.second[:, cols] = acc

    def norm1_rows(self):
        b = self.b

        def body(r, sums):
            rows = pl.ds(pl.multiple_of(r * ROWS, ROWS), ROWS)
            c = b.second[rows, :]
            n = b.n1[rows, :]
            g = norm_back(c, self.v(VAG), n, b.r1[rows, 0:1])
            b.second[rows, :] = g
            low = g.astype(BF)
            b.nl[rows, :] = low
            return sums[0] + column_total(c * n), sums[1] + column_total(c), sums[2] + column_total(low)

        zero = jnp.zeros((1, WIDTH), F32)
        sums = lax.fori_loop(0, TOKENS // ROWS, body, (zero, zero, zero))
        self.gvec[VAG:VAG + 1, :], self.gvec[VAS:VAS + 1, :], self.gvec[VO:VO + 1, :] = sums

    def out_grads(self):
        b = self.b
        left = b.mixed[...].T
        for n in range(3):
            cols = slice(n * 256, n * 256 + 256)
            self.grads[0][3, :, cols] = mm(left, b.nl[:, cols]).astype(BF)

    def out_back(self):
        b = self.b
        for n in range(3):
            cols = slice(n * 256, n * 256 + 256)
            b.mixed[:, cols] = mm_nt(b.nl[...], self.slabs[0].at[3][cols, :]).astype(BF)

    def attend_back(self, p):
        b = self.b
        masks = half_masks()
        cols = slice(p * LANES, p * LANES + LANES)

        for s in range(2):
            rows = slice(s * SEQ, s * SEQ + SEQ)
            q, k, v, do = b.q[rows, cols], b.k[rows, cols], b.v[rows, cols], b.mixed[rows, cols]
            dq = dk = dv = 0.0
            for a in range(2):
                att = b.p[s * 12 + p * 2 + a]
                do_a = do * masks[a]
                dv = dv + mm(att.astype(BF), do_a)
                dp = mm_nt(v, do_a)
                ds = (att * (dp - jnp.sum(att * dp, 0, keepdims=True))).astype(BF)
                dk = dk + mm(ds, q * masks[a])
                dq = dq + mm_tn(k * masks[a], ds)
            b.gpre[0, rows, cols] = (dq.T * 0.125).astype(BF)
            b.gpre[1, rows, cols] = dk.astype(BF)
            b.gpre[2, rows, cols] = dv.astype(BF)
        both = mm(b.xt[...], jnp.concatenate([b.gpre[0, :, cols], b.gpre[1, :, cols]], 1))
        self.grads[0][0, :, cols] = both[:, :LANES].astype(BF)
        self.grads[0][1, :, cols] = both[:, LANES:].astype(BF)
        self.grads[0][2, :, cols] = mm(b.xt[...], b.gpre[2, :, cols]).astype(BF)
        self.gvec[VQ:VQ + 1, cols] = column_total(b.gpre[0, :, cols])
        self.gvec[VV:VV + 1, cols] = column_total(b.gpre[2, :, cols])

    def input_grad(self, n):
        b = self.b
        cols = slice(n * 256, n * 256 + 256)
        acc = b.second[:, cols]
        for j in range(3):
            acc = acc + mm_nt(b.gpre[j], self.slabs[0].at[j][cols, :])
        b.second[:, cols] = acc


BUFFERS = dict(
    q=((TOKENS, WIDTH), BF), k=((TOKENS, WIDTH), BF), v=((TOKENS, WIDTH), BF), p=((24, SEQ, SEQ), F32),
    mixed=((TOKENS, WIDTH), BF), n1=((TOKENS, WIDTH), F32), r1=((TOKENS, LANES), F32), nl=((TOKENS, WIDTH), BF),
    act=((4, TOKENS, WIDTH), BF), gp=((4, TOKENS, WIDTH), F32), second=((TOKENS, WIDTH), F32),
    gpre=((4, TOKENS, WIDTH), BF), xt=((WIDTH, TOKENS), BF), nlt=((WIDTH, TOKENS), BF),
)


START = {16: 0, 8: 16, 4: 24}
WHOLE = tuple((part, 0, UNIT, ORDERS[part]) for part in range(PARTS))
CUT = WHOLE[:4] + tuple((4 + i // 3, 16 * (i % 3), 16, ORDERS[i]) for i in range(6))
CHAINS = (CUT, WHOLE, WHOLE)
EVERY = ((0, 2), (0, 4), (0, 2), (0, 2))
SCRATCH = dict(
    wa=(SHAPES[0], BF), wb=(SHAPES[1], BF), wc=(SHAPES[2], BF), ga=(SHAPES[0], BF),
    rdb=((2, 1, 4, 2, 2, UNIT, WIDTH), BF), rdc=((4, 2, 2, 2, 1, UNIT, WIDTH), BF),
    rk=((3, 31, UNIT, WIDTH), BF), rx=((UNIT, WIDTH), BF), tall=((UNIT, WIDTH), F32),
    stage=((2, 4, 16, WIDTH), BF), final=((2, 2, 4, 16, WIDTH), BF),
    vt=((4, 2, 8, 2, LANES), F32), gv=((4, 2, 8, 2, LANES), F32),
    rv2=((3, 2, 8, 2, LANES), F32), rv1=((3, 4, 2, LANES), F32), rv0=((7, 2, LANES), F32),
    vec=((16, WIDTH), F32), gvec=((16, WIDTH), F32),
    x=((TOKENS, WIDTH), BF), qkv_in=((12, 3 * WIDTH), BF), out_in=((12, WIDTH), BF), up_in=((12, 4 * WIDTH), BF),
)
SEMS = dict(
    loads=(8,), mate_send=(2, 3), mate_recv=(2, 3), send=(3, PARTS, 7), recv=(3, PARTS, 7),
    sib_send=(3, PARTS), sib_recv=(3, PARTS), vsend=(9,), vrecv=(9,),
    gsib_send=(3, PARTS), gsib_recv=(3, PARTS), gsend=(3, 10, 6), grecv=(3, 10, 6),
    rep_send=(1,), rep_recv=(1,), gmate_send=(2, 7), gmate_recv=(2, 7), gvsend=(13,), gvrecv=(13,),
)


def box_count(box):
    return box[0][1] * box[1][1] * box[2][1] * box[3][1]


def split3(value):
    high = value.astype(BF)
    rest = value - high.astype(F32)
    mid = rest.astype(BF)
    return high, mid, (rest - mid.astype(F32)).astype(BF)


def owner_masks(block):
    d = lax.broadcasted_iota(jnp.int32, (64, WIDTH), 0)
    c = lax.broadcasted_iota(jnp.int32, (64, WIDTH), 1)
    if block is None:
        return d == (c * 43691) >> 19
    return d == 16 * block + ((c * 43691) >> 21)


def lane_picks(row):
    c = lax.broadcasted_iota(jnp.int32, (WIDTH, LANES), 0)
    lane = lax.broadcasted_iota(jnp.int32, (WIDTH, LANES), 1)
    if row is None:
        return (lane == c - 48 * ((c * 43691) >> 21)).astype(F32).astype(BF)
    return (lane == 12 * row + c - 12 * ((c * 43691) >> 19)).astype(F32).astype(BF)


def mega_kernel(lengths, *refs):
    vecs_in, (qkv_in, out_in, up_in, down_in, x_in, og_in,
               enc_out, sgrad_out, oqkv, oout, oup, odown, ovec), scratch = refs[:9], refs[9:22], refs[22:]
    r = b = types.SimpleNamespace(**dict(zip([*SCRATCH, *BUFFERS, *SEMS], scratch)))
    here = position()
    me = member_of(here)
    sibling = hop(here, CORE)
    twin = hop(here, X2)
    weights = (r.wa, r.wb, r.wc)
    grads = (r.ga, r.wb, r.wc)
    rds = (r.act.at[pl.ds(0, 3)].reshape((2, 1, 4, 2, 2, UNIT, WIDTH)), r.rdb, r.rdc)
    slabs = [w.reshape(4, WIDTH, WIDTH) for w in weights]
    gslabs = [w.reshape(4, WIDTH, WIDTH) for w in grads]
    layer = Layer(slabs, gslabs, r.vec, lengths, r.x, r.x, r.x, r.gvec, b)

    def own_at(phase):
        ylow, z, x, yhigh = (s for s, n in own_box(here))
        return (ylow, here.core, z, x, yhigh) if phase < 2 else (z, x, yhigh, ylow, here.core)

    def mate_copy(which, k):
        mate = mates(here)[k]
        return remote(r.stage.at[which, member_of(mate)], r.final.at[which, 0, me],
                      r.mate_send.at[which, k], r.mate_recv.at[which, k], mate)

    def assemble(which):
        for k in range(3):
            mate_copy(which, k).wait()
        r.final[which, 0, me] = r.stage[which, me]
        for i in range(4):
            r.tall[12 * i:12 * i + 12, :] = r.final[which, 0, i, 0:12, :].astype(F32)
        weights[which][own_at(which)] = r.tall[...].astype(BF)

    def push(phase, part, found, slot, there):
        w = weights[phase]
        for box in found:
            view = w.at[slices(phase, here.core, box, part)]
            remote(view, view, r.send.at[phase, part, slot], r.recv.at[phase, part, slot], there).start()

    def share(phase, part, found):
        w = weights[phase]
        for box in found:
            view = w.at[slices(phase, here.core, box, part)]
            remote(view, view, r.sib_send.at[phase, part], r.sib_recv.at[phase, part], sibling).start()

    def gather_first(phase):
        for part in range(PARTS):
            for slot, there in enumerate(trio(here, ORDERS[part])):
                push(phase, part, boxes(here, ()), slot, there)

    def gather(phase, step):
        w = weights[phase]
        for part in range(PARTS):
            order = ORDERS[part]
            if step == 2:
                for slot in range(3):
                    wait_units(w, phase, 1, part, r.recv.at[phase, part, slot])
            else:
                wait_units(w, phase, 1 << (step - 1), part, r.recv.at[phase, part, step])
            there = hop(here, order[step])
            if step < 4:
                push(phase, part, boxes(here, order[:step]), step + 1, there)
            else:
                for half, found in enumerate(halves(boxes(here, order[:4]))):
                    push(phase, part, found, 5 + half, there)
                share(phase, part, boxes(here, order[:4]))

    def gather_last(phase, half):
        for part in range(PARTS):
            order = ORDERS[part]
            wait_units(weights[phase], phase, 8, part, r.recv.at[phase, part, 5 + half])
            share(phase, part, halves(boxes(hop(here, order[4]), order[:4]))[half])

    def gathered(phase):
        for part in range(PARTS):
            wait_units(weights[phase], phase, 32, part, r.sib_recv.at[phase, part])

    def gather_sent(phase):
        for part in range(PARTS):
            wait_units(weights[phase], phase, 32, part, r.sib_send.at[phase, part])
            for slot, n in enumerate((1, 1, 1, 4, 8, 8, 8)):
                wait_units(weights[phase], phase, n, part, r.send.at[phase, part, slot])

    def vec_tile(place):
        return (place.z, place.x % 2, place.y * 2 + place.core)

    def vec_pair(place):
        return (place.z, place.x % 2, pl.ds(place.y // 2 * 4, 4))

    def vec_ring(place):
        return (pl.ds(place.z // 2 * 2, 2), place.x % 2)

    def vec_peers(k):
        return (mates(here), trio(here, (Y3, Z1)), trio(here, (Z3, X1)))[k]

    def vec_copies(k):
        view = r.vt.at[(vec_tile, vec_pair, vec_ring)[k](here)]
        return [remote(view, view, r.vsend.at[3 * k + i], r.vrecv.at[3 * k + i], there) for i, there in enumerate(vec_peers(k))]

    def vec_start(k):
        for copy in vec_copies(k):
            copy.start()

    def vec_wait(k):
        for copy in vec_copies(k):
            copy.wait()

    def expand():
        first = r.vt[:, :, :, 0, :].reshape(64, LANES).astype(BF)
        second = r.vt[:, :, :, 1, :].reshape(64, LANES).astype(BF)
        mask = owner_masks(None)
        for row in range(8):
            t = mm_nt(first, lane_picks(row))
            r.vec[row:row + 1, :] = jnp.sum(jnp.where(mask, t, 0.0), 0, keepdims=True)
        t = mm_nt(second, lane_picks(None))
        for j in range(4):
            r.vec[8 + j:9 + j, :] = jnp.sum(jnp.where(owner_masks(j), t, 0.0), 0, keepdims=True)

    def sib_copy(phase, k):
        g, rd = grads[phase], rds[phase]
        if phase == 0:
            cols = pl.ds(k * LANES, LANES)
            src = g.at[:, pl.ds(sibling.core, 1), :, :, :, :, cols]
            dst = rd.at[:, :, :, :, :, :, cols]
        elif phase == 1:
            src, dst = g.at[k, sibling.core], rd.at[k, 0]
        else:
            src, dst = g.at[k, :, :, :, pl.ds(sibling.core, 1)], rd.at[k]
        return remote(src, dst, r.gsib_send.at[phase, k], r.gsib_recv.at[phase, k], sibling)

    def sib_add(phase, k):
        sib_copy(phase, k).wait()
        g, rd = grads[phase], rds[phase]
        for i in range(4):
            if phase == 0:
                at = slices(0, here.core, ((0, 2), (i, 1), (0, 2), (0, 2)), k)
                g[at] = g[at] + rd[slices(0, 0, ((0, 2), (i, 1), (0, 2), (0, 2)), k)]
            elif phase == 1:
                g[k, here.core, i] = g[k, here.core, i] + rd[k, 0, i]
            else:
                at = (k, i // 2, i % 2, slice(None), pl.ds(here.core, 1))
                g[at] = g[at] + rd[k, i // 2, i % 2]

    def unit_slices(phase, box, chain):
        part, row, rows, _ = chain
        return slices(phase, here.core, box, part)[:5] + (slice(row, row + rows), slice(part * LANES, part * LANES + LANES))

    def hop_start(phase, c, step):
        chain = CHAINS[phase][c]
        order = chain[3]

        def send(box, at, slot, there):
            n = box_count(box)
            src = grads[phase].at[slices(phase, here.core, box, chain[0])[:5]]
            dst = r.rk.at[phase, pl.ds(at, n)].reshape(src.shape)
            at5 = (slice(None),) * 5 + (pl.ds(chain[1], chain[2]), pl.ds(chain[0] * LANES, LANES))
            remote(src.at[at5], dst.at[at5], r.gsend.at[phase, c, slot], r.grecv.at[phase, c, slot], there).start()
            return at + n

        if step == 1:
            for slot, there in enumerate(trio(here, order)):
                send(boxes(there, ())[0], 28 + slot, slot, there)
            return
        there = hop(here, order[step])
        at = START[1 << step]
        for box in boxes(there, order[:step]):
            at = send(box, at, step + 1, there)

    def landing(phase, c, at, n):
        part, row, rows, _ = CHAINS[phase][c]
        return r.rk.at[phase, pl.ds(at, n), pl.ds(row, rows), pl.ds(part * LANES, LANES)]

    def hop_add(phase, c, step):
        g = grads[phase]
        chain = CHAINS[phase][c]
        if step == 1:
            where = unit_slices(phase, boxes(here, ())[0], chain)
            total = g[where].astype(F32)
            for slot in range(3):
                view = landing(phase, c, 28 + slot, 1)
                pltpu.make_async_copy(view, view, r.grecv.at[phase, c, slot]).wait()
                total = total + view[...].astype(F32).reshape(total.shape)
            g[where] = total.astype(BF)
            return
        n = 1 << step
        at = START[n]
        view = landing(phase, c, at, n)
        pltpu.make_async_copy(view, view, r.grecv.at[phase, c, step + 1]).wait()
        for box in boxes(here, chain[3][:step]):
            m = box_count(box)
            where = unit_slices(phase, box, chain)
            old = g[where]
            g[where] = old + landing(phase, c, at, m)[...].reshape(old.shape)
            at += m

    def rep_copy():
        return remote(grads[2].at[own_at(2)], r.rx, r.rep_send.at[0], r.rep_recv.at[0], twin)

    def reduce_first(phase):
        for k in range(2 if phase == 1 else 4):
            sib_add(phase, k)
        for part in range(PARTS):
            hop_start(phase, part, 4)

    def move(phase, c, step):
        hop_add(phase, c, step)
        if step > 1:
            hop_start(phase, c, step - 1)

    def reduce(phase, step):
        for part in range(PARTS):
            move(phase, part, step)

    def first_part(part):
        sib_add(0, part)
        for c, chain in enumerate(CUT):
            if chain[0] == part:
                hop_start(0, c, 4)

    def move_part(part, step):
        for c, chain in enumerate(CUT):
            if chain[0] == part:
                move(0, c, step)

    def gmate_copy(which, k):
        others = mates(here)
        there = (others + [twin] + [hop(mate, X2) for mate in others])[k]
        return remote(r.stage.at[which, member_of(there)], r.final.at[which, k // 3 if k < 6 else 1, me],
                      r.gmate_send.at[which, k], r.gmate_recv.at[which, k], there)

    def hand_over(phase):
        r.tall[...] = grads[phase][own_at(phase)].astype(F32)
        for i in range(4):
            r.stage[phase, i, 0:12, :] = r.tall[12 * i:12 * i + 12, :].astype(BF)
        for k in range(7):
            gmate_copy(phase, k).start()

    def deliver(phase):
        for k in range(7):
            gmate_copy(phase, k).wait()
        r.final[phase, 0, me] = r.stage[phase, me]
        for i in range(4):
            cols = pl.ds(i * WIDTH, WIDTH)
            dst = oup.at[:, cols] if phase else (oqkv.at[:, cols] if i < 3 else oout)
            dst[...] = r.final[phase, 0, i, 0:12, :].astype(F32) + r.final[phase, 1, i, 0:12, :].astype(F32)

    def deliver_down():
        rep_copy().wait()
        odown[...] = grads[2][own_at(2)].astype(F32) + r.rx[...].astype(F32)

    def reduce_sent(phase):
        for c in range(len(CHAINS[phase])):
            for slot, n in enumerate((1, 1, 1, 4, 8, 16)):
                view = landing(phase, c, 0, n)
                pltpu.make_async_copy(view, view, r.gsend.at[phase, c, slot]).wait()

    def pack_rows(rows):
        mask = owner_masks(None)
        first = jnp.zeros((64, LANES), F32)
        for row in rows:
            value = jnp.where(mask, jnp.broadcast_to(r.gvec[row:row + 1, :], (64, WIDTH)), 0.0)
            picks = lane_picks(row)
            for piece in split3(value):
                first = first + mm(piece, picks)
        return first.reshape(4, 2, 8, LANES)

    def pack():
        second = jnp.zeros((64, LANES), F32)
        picks = lane_picks(None)
        for j in range(4):
            value = jnp.where(owner_masks(j), jnp.broadcast_to(r.gvec[8 + j:9 + j, :], (64, WIDTH)), 0.0)
            for piece in split3(value):
                second = second + mm(piece, picks)
        r.gv[:, :, :, 0, :] = pack_rows((VO, VAG, VAS, VD, VFG, VFS))
        r.gv[:, :, :, 1, :] = second.reshape(4, 2, 8, LANES)

    def gvec_copies(k):
        if k == 0:
            peers = mates(here) + [twin] + [hop(mate, X2) for mate in mates(here)]
        else:
            peers = vec_peers(k)
        part, landing_ref = ((vec_tile, r.rv0), (vec_pair, r.rv1), (vec_ring, r.rv2))[k]
        base = (6, 3, 0)[k]
        return [remote(r.gv.at[part(there)], landing_ref.at[i], r.gvsend.at[base + i], r.gvrecv.at[base + i], there)
                for i, there in enumerate(peers)]

    def gvec_start(k):
        for copy in gvec_copies(k):
            copy.start()

    def gvec_add(k):
        part, landing_ref = ((vec_tile, r.rv0), (vec_pair, r.rv1), (vec_ring, r.rv2))[k]
        at = part(here)
        total = r.gv[at]
        for i, copy in enumerate(gvec_copies(k)):
            copy.wait()
            total = total + landing_ref[i].reshape(total.shape)
        r.gv[at] = total

    near = [hop(here, link) for link in (Y1, Y3, Z1, Z3, X1, X3, CORE, X2, Y2, Z2)]
    near += [mates(here)[2], hop(hop(here, Y3), Z1), hop(hop(here, Y1), Z3)]
    near += [hop(mate, X2) for mate in mates(here)] + [hop(hop(here, Z3), X1)]
    loads = [pltpu.make_async_copy(src, dst, r.loads.at[i]) for i, (src, dst) in enumerate((
        (qkv_in, r.qkv_in), (out_in, r.out_in), (up_in, r.up_in), (down_in, weights[2].at[own_at(2)]), (x_in, r.x)))]
    for load in loads:
        load.start()
    barrier = pltpu.get_barrier_semaphore()
    for place in near:
        pl.semaphore_signal(barrier, inc=1, device_id=device_of(place), device_id_type=MESH)
    og_load = pltpu.make_async_copy(og_in, r.x, r.loads.at[5])
    own = vec_tile(here)
    r.vt[own] = jnp.zeros((2, LANES), F32)
    for i in range(8):
        r.vt[own + (slice(0, 1), slice(12 * i, 12 * i + 12))] = vecs_in[i][...].astype(F32)
    r.vt[own + (slice(1, 2), slice(0, 48))] = vecs_in[8][...].astype(F32)
    for load in loads[:4]:
        load.wait()
    for i in range(4):
        r.stage[0, i, 0:12, :] = r.qkv_in[:, i * WIDTH:(i + 1) * WIDTH] if i < 3 else r.out_in[...]
        r.stage[1, i, 0:12, :] = r.up_in[:, i * WIDTH:(i + 1) * WIDTH]
    pl.semaphore_wait(barrier, len(near))
    for k in range(3):
        mate_copy(0, k).start()
    vec_start(0)
    for k in range(3):
        mate_copy(1, k).start()
    gather_first(2)
    loads[4].wait()
    b.xt[...] = r.x[...].T
    assemble(0)
    vec_wait(0)
    vec_start(1)
    gather_first(0)
    assemble(1)
    gather_first(1)
    vec_wait(1)
    vec_start(2)
    gather(0, 2)
    gather(2, 2)
    gather(1, 2)
    gather(0, 3)
    vec_wait(2)
    expand()
    gather(0, 4)
    gather(1, 3)
    gather(2, 3)
    gather_last(0, 0)
    gather_last(0, 1)
    gathered(0)
    layer.project(0)
    gather(1, 4)
    layer.project(1)
    layer.project(2)
    gather(2, 4)
    layer.attend()
    gather_last(1, 0)
    gather_last(1, 1)
    layer.attn_out()
    og_load.start()
    b.nlt[...] = b.nl[...].T
    gather_last(2, 0)
    gather_last(2, 1)
    gathered(1)
    layer.feed()
    og_load.wait()
    gathered(2)
    layer.feed_out()
    enc_store = pltpu.make_async_copy(r.x, enc_out, r.loads.at[6])
    enc_store.start()
    gather_sent(2)

    def down_body(j, _):
        layer.feed_back(j)
        layer.down_grads(j)
        sib_copy(2, j).start()
        return 0

    lax.fori_loop(0, 4, down_body, 0)
    for n in range(3):
        layer.norm1_back(n)
    reduce_first(2)
    gather_sent(1)

    def up_body(i, _):
        layer.up_grads(i * 2 + sibling.core)
        sib_copy(1, i).start()
        return 0

    def up_own(i, _):
        layer.up_grads(i * 2 + here.core)
        return 0

    lax.fori_loop(0, 2, up_body, 0)
    lax.fori_loop(0, 2, up_own, 0)
    layer.norm1_rows()
    reduce_first(1)
    layer.out_grads()
    reduce(2, 4)
    layer.out_back()
    pack()
    layer.attend_back(0)
    sib_copy(0, 0).start()
    layer.attend_back(1)
    sib_copy(0, 1).start()
    reduce(1, 4)
    first_part(0)
    layer.attend_back(2)
    sib_copy(0, 2).start()
    reduce(2, 3)
    first_part(1)
    layer.attend_back(3)
    sib_copy(0, 3).start()
    reduce(1, 3)
    first_part(2)
    layer.attend_back(4)
    sib_copy(0, 4).start()
    reduce(2, 2)
    first_part(3)
    move_part(0, 4)
    layer.attend_back(5)
    sib_copy(0, 5).start()
    first_part(4)
    r.gv[:, :, :, 0, :] = r.gv[:, :, :, 0, :] + pack_rows((VQ, VV))
    gvec_start(2)
    move_part(1, 4)
    layer.input_grad(0)
    first_part(5)
    reduce(1, 2)
    layer.input_grad(1)
    move_part(2, 4)
    move_part(0, 3)
    layer.input_grad(2)
    sgrad_store = pltpu.make_async_copy(b.second, sgrad_out, r.loads.at[7])
    sgrad_store.start()
    reduce(2, 1)
    rep_copy().start()
    move_part(4, 4)
    gvec_add(2)
    gvec_start(1)
    move_part(3, 4)
    move_part(5, 4)
    move_part(1, 3)
    move_part(0, 2)
    move_part(2, 3)
    move_part(4, 3)
    reduce(1, 1)
    hand_over(1)
    move_part(5, 3)
    move_part(3, 3)
    move_part(1, 2)
    move_part(2, 2)
    move_part(4, 2)
    gvec_add(1)
    gvec_start(0)
    move_part(3, 2)
    move_part(5, 2)
    deliver_down()
    for part in range(PARTS):
        move_part(part, 1)
    hand_over(0)
    deliver(1)
    gvec_add(0)
    ovec[...] = r.gv[vec_tile(here)]
    for phase in range(1, 3):
        reduce_sent(phase)
    gather_sent(0)
    reduce_sent(0)
    enc_store.wait()
    sgrad_store.wait()
    deliver(0)


def run_layer(lengths, vecs, qkv, out, up, down, x, og):
    vm = pl.BlockSpec(memory_space=pltpu.VMEM)
    hb = pl.BlockSpec(memory_space=pl.ANY)
    return pl.pallas_call(
        mega_kernel,
        out_shape=[
            jax.ShapeDtypeStruct((TOKENS, WIDTH), BF), jax.ShapeDtypeStruct((TOKENS, WIDTH), F32),
            jax.ShapeDtypeStruct((12, 3 * WIDTH), F32), jax.ShapeDtypeStruct((12, WIDTH), F32),
            jax.ShapeDtypeStruct((12, 4 * WIDTH), F32), jax.ShapeDtypeStruct((UNIT, WIDTH), F32), jax.ShapeDtypeStruct((2, LANES), F32),
        ],
        in_specs=[pl.BlockSpec(memory_space=pltpu.SMEM)] + [vm] * 9 + [hb] * 6,
        out_specs=[hb, hb] + [vm] * 5,
        scratch_shapes=[pltpu.VMEM(s, d) for s, d in SCRATCH.values()] + [pltpu.VMEM(s, d) for s, d in BUFFERS.values()]
        + [pltpu.SemaphoreType.DMA(s) for s in SEMS.values()],
        compiler_params=pltpu.CompilerParams(collective_id=1, has_side_effects=True, vmem_limit_bytes=63 * 2**20),
    )(lengths, *vecs, qkv, out, up, down, x, og)


def finish_kernel(*refs):
    srcs, vec, dsts, vec_outs, held, sems = refs[:6], refs[6], refs[7:13], refs[13:22], refs[22:28], refs[28]
    loads = [pltpu.make_async_copy(src, mid, sems.at[0, i]) for i, (src, mid) in enumerate(zip(srcs, held))]
    stores = [pltpu.make_async_copy(mid, dst, sems.at[1, i]) for i, (mid, dst) in enumerate(zip(held, dsts))]
    for load in loads:
        load.start()
    for i in range(8):
        vec_outs[i][...] = vec[0:1, 12 * i:12 * i + 12]
    vec_outs[8][...] = vec[1:2, 0:48]
    for load, store in zip(loads, stores):
        load.wait()
        store.start()
    for store in stores:
        store.wait()


def finish(results):
    vm = pl.BlockSpec(memory_space=pltpu.VMEM)
    hb = pl.BlockSpec(memory_space=pl.ANY)
    return pl.pallas_call(
        finish_kernel,
        out_shape=[jax.ShapeDtypeStruct(a.shape, a.dtype) for a in results[:6]]
        + [jax.ShapeDtypeStruct((1, n), F32) for n in [12] * 8 + [48]],
        in_specs=[hb] * 6 + [vm],
        out_specs=[hb] * 6 + [vm] * 9,
        scratch_shapes=[pltpu.VMEM(a.shape, a.dtype) for a in results[:6]] + [pltpu.SemaphoreType.DMA((2, 6))],
        compiler_params=pltpu.CompilerParams(vmem_limit_bytes=63 * 2**20),
    )(*results)


def local(states, qkv_weight, query_bias, value_bias, out_weight, out_bias, attn_gain, attn_shift, up_weight, up_bias,
          down_weight, down_bias, ffn_gain, ffn_shift, out_grad, lengths):
    vecs = [v.reshape(1, -1) for v in (query_bias, value_bias, out_bias, attn_gain, attn_shift, down_bias, ffn_gain, ffn_shift, up_bias)]
    results = run_layer(
        lengths.reshape(1, 2), vecs, qkv_weight, out_weight, up_weight, down_weight,
        states.reshape(TOKENS, WIDTH), out_grad.reshape(TOKENS, WIDTH))
    enc, sgrad, oqkv, oout, oup, odown, *o = finish(results)
    o = [v.reshape(-1) for v in o]
    return (enc.reshape(states.shape), sgrad.reshape(states.shape), oqkv, o[0], o[1], oout, o[2], o[3], o[4],
            oup, o[8], odown, o[5], o[6], o[7])


def solution(mesh):
    return jax.shard_map(
        local,
        mesh=mesh,
        in_specs=(
            P(None, ("dp", "rep"), None, None),
            P("dp", None),
            P("dp"),
            P("dp"),
            P("dp", None),
            P("dp"),
            P("dp"),
            P("dp"),
            P("dp", None),
            P("dp"),
            P("dp", None),
            P("dp"),
            P("dp"),
            P("dp"),
            P(None, ("dp", "rep"), None, None),
            P(None, ("dp", "rep")),
        ),
        out_specs=(
            P(None, ("dp", "rep"), None, None),
            P(None, ("dp", "rep"), None, None),
            P("dp", None),
            P("dp"),
            P("dp"),
            P("dp", None),
            P("dp"),
            P("dp"),
            P("dp"),
            P("dp", None),
            P("dp"),
            P("dp", None),
            P("dp"),
            P("dp"),
            P("dp"),
        ),
        check_vma=False,
    )
```

```python
import collections
import math
import types

import jax
import jax.numpy as jnp
from jax import lax
from jax.experimental import pallas as pl
from jax.experimental.pallas import tpu as pltpu
from jax.sharding import PartitionSpec as P

Place = collections.namedtuple("Place", "core y z x")
MESH = pl.DeviceIdType.MESH
BF = jnp.bfloat16
F32 = jnp.float32
WIDTH = 768
UNIT = 48
LANES = 128
PARTS = 6

CORE, Y1, Y3, Z1, Z3, X1, X2, X3 = (0, 0), (1, 1), (1, 3), (2, 1), (2, 3), (3, 1), (3, 2), (3, 3)
Y2, Z2 = (1, 2), (2, 2)

ORDERS = (
    (Z1, Z3, Y1, Y3, X1),
    (Y1, Y3, Z1, Z3, X3),
    (Y3, Z1, Z3, X1, Y1),
    (Y1, Z3, X1, Z1, Y3),
    (Y1, Z3, X3, Y3, Z1),
    (Z1, Y3, X3, Y1, Z3),
)


def position():
    dp = lax.axis_index("dp")
    rep = lax.axis_index("rep")
    return Place(dp % 2, (dp // 2) % 4, dp // 16, rep * 2 + (dp // 8) % 2)


def device_of(place):
    dp = ((place.z * 2 + place.x % 2) * 4 + place.y) * 2 + place.core
    return (dp, place.x // 2)


def hop(place, link):
    axis, how = link
    p = place[axis]
    moved = (1 - p, p + 1 - 2 * (p % 2), (p + 2) % 4, 3 - p)[how]
    return Place(*(moved if i == axis else q for i, q in enumerate(place)))


def boxes(place, links):
    y, z, x = place.y, place.z, place.x % 2
    if Y1 in links and Y3 in links:
        ys = [((0, 2), (0, 2))]
    elif Y1 in links:
        ys = [((0, 2), (y // 2, 1))]
    elif Y3 in links:
        ys = [((y % 2, 1), (y // 2, 1)), ((1 - y % 2, 1), (1 - y // 2, 1))]
    else:
        ys = [((y % 2, 1), (y // 2, 1))]
    if Z1 in links and Z3 in links:
        zs = [(0, 4)]
    elif Z1 in links:
        zs = [((z // 2) * 2, 2)]
    elif Z3 in links:
        zs = [(z, 1), (3 - z, 1)]
    else:
        zs = [(z, 1)]
    xs = (0, 2) if X1 in links or X3 in links else (x, 1)
    return [(ylow, zz, xs, yhigh) for (ylow, yhigh) in ys for zz in zs]


def slices(phase, core, box, part):
    ylow, z, x, yhigh = (pl.ds(*s) for s in box)
    cols = pl.ds(part * LANES, LANES)
    if phase < 2:
        return (ylow, pl.ds(core, 1), z, x, yhigh, slice(None), cols)
    return (z, x, yhigh, ylow, pl.ds(core, 1), slice(None), cols)


SHAPES = (
    (2, 2, 4, 2, 2, UNIT, WIDTH),
    (2, 2, 4, 2, 2, UNIT, WIDTH),
    (4, 2, 2, 2, 2, UNIT, WIDTH),
)


def size_box(count):
    sizes = {1: (1, 1, 1, 1), 2: (1, 1, 1, 2), 4: (1, 1, 2, 2), 8: (1, 2, 2, 2), 16: (1, 4, 2, 2), 32: (2, 4, 2, 2)}[count]
    return tuple((0, n) for n in sizes)


def wait_units(ref, phase, count, part, sem):
    view = ref.at[slices(phase, 0, size_box(count), part)]
    pltpu.make_async_copy(view, view, sem).wait()


def remote(src, dst, send_sem, recv_sem, place):
    return pltpu.make_async_remote_copy(
        src_ref=src, dst_ref=dst, send_sem=send_sem, recv_sem=recv_sem,
        device_id=device_of(place), device_id_type=MESH,
    )


def greet(places):
    barrier = pltpu.get_barrier_semaphore()
    for place in places:
        pl.semaphore_signal(barrier, inc=1, device_id=device_of(place), device_id_type=MESH)
    pl.semaphore_wait(barrier, len(places))


def member_of(place):
    return (place.y % 2) * 2 + place.core


def mates(here):
    return [hop(here, CORE), hop(here, Y1), hop(hop(here, CORE), Y1)]


def own_box(here):
    return boxes(here, ())[0]


def trio(place, order):
    a, b = hop(place, order[0]), hop(place, order[1])
    return a, b, hop(a, order[1])


def halves(found):
    if len(found) == 2:
        return [found[:1], found[1:]]
    ylow, (start, n), x, yhigh = found[0]
    return [[(ylow, (start, n // 2), x, yhigh)], [(ylow, (start + n // 2, n // 2), x, yhigh)]]


HALF = 256
SEQ = 256
TOKENS = 512
ROWS = 64
epsilon = 1e-05
NT = (((1,), (1,)), ((), ()))
TN = (((0,), (0,)), ((), ()))
VQ, VV, VO, VAG, VAS, VD, VFG, VFS, VUP = range(9)


def mm(left, right):
    return jnp.dot(left, right, preferred_element_type=F32)


def mm_nt(left, right):
    return lax.dot_general(left, right, NT, preferred_element_type=F32)


def mm_tn(left, right):
    return lax.dot_general(left, right, TN, preferred_element_type=F32)


def normalise(value):
    center = value - jnp.mean(value, -1, keepdims=True)
    scale = lax.rsqrt(jnp.mean(center * center, -1, keepdims=True) + epsilon)
    return center * scale, scale


def norm_back(cot, gain, n, scale):
    e = cot * gain
    return scale * (e - jnp.mean(e, -1, keepdims=True) - n * jnp.mean(e * n, -1, keepdims=True))


def half_masks():
    lane = lax.broadcasted_iota(jnp.int32, (1, LANES), 1)
    low = (lane < 64).astype(F32).astype(BF)
    return low, (1.0 - low.astype(F32)).astype(BF)


def row_masks():
    row = lax.broadcasted_iota(jnp.int32, (LANES, SEQ), 0)
    low = (row < 64).astype(F32).astype(BF)
    return low, (1.0 - low.astype(F32)).astype(BF)


def column_total(ref_rows):
    return jnp.sum(ref_rows.astype(F32), 0, keepdims=True)


class Layer:
    def __init__(self, slabs, grads, vec, lengths, x, og, enc, gvec, b):
        self.slabs, self.grads, self.vec, self.lengths, self.x, self.og = slabs, grads, vec, lengths, x, og
        self.enc, self.gvec, self.b = enc, gvec, b

    def v(self, row):
        return self.vec[row:row + 1, :]

    def project(self, j):
        b = self.b
        dst, row = ((b.q, VQ), (b.k, None), (b.v, VV))[j]
        for n in range(3):
            cols = slice(n * 256, n * 256 + 256)
            acc = mm(self.x[...], self.slabs[0].at[j][:, cols])
            if row is not None:
                acc = acc + self.vec[row:row + 1, cols]
            low = acc.astype(BF)
            if j == 0:
                low = (low.astype(F32) * 0.125).astype(BF)
            dst[:, cols] = low

    def attend(self):
        b = self.b
        masks, tall = half_masks(), row_masks()
        key = lax.broadcasted_iota(jnp.int32, (SEQ, SEQ), 0)

        def body(p, _):
            cols = pl.ds(pl.multiple_of(p * LANES, LANES), LANES)
            rows = [slice(s * SEQ, s * SEQ + SEQ) for s in range(2)]
            scores = [[mm_nt(b.k[rows[s], cols] * masks[a], b.q[rows[s], cols]) for a in range(2)] for s in range(2)]
            low = [[None, None], [None, None]]
            for s in range(2):
                length = self.lengths[0, s]
                for a in range(2):
                    st = jnp.where(key < length, scores[s][a], -1e9)
                    e = jnp.exp(st - jnp.max(st, 0, keepdims=True))
                    att = e * (1.0 / jnp.sum(e, 0, keepdims=True))
                    b.p[s * 12 + p * 2 + a] = att
                    low[s][a] = att.astype(BF)
            for s in range(2):
                vt = b.v[rows[s], cols].T
                out = mm(jnp.concatenate([vt * tall[0], vt * tall[1]], 1), jnp.concatenate(low[s], 0))
                b.mixed[rows[s], cols] = out.T.astype(BF)
            return 0

        lax.fori_loop(0, 6, body, 0)

    def attn_out(self):
        b = self.b
        for n in range(3):
            cols = slice(n * 256, n * 256 + 256)
            acc = mm(b.mixed[...], self.slabs[0].at[3][:, cols]) + self.vec[VO:VO + 1, cols]
            b.n1[:, cols] = self.x[:, cols].astype(F32) + acc

        def body(r, _):
            rows = pl.ds(pl.multiple_of(r * ROWS, ROWS), ROWS)
            n, scale = normalise(b.n1[rows, :])
            b.n1[rows, :] = n
            b.r1[rows, :] = jnp.broadcast_to(scale, (ROWS, LANES))
            b.nl[rows, :] = (n * self.v(VAG) + self.v(VAS)).astype(BF)
            return 0

        lax.fori_loop(0, TOKENS // ROWS, body, 0)

    def feed(self):
        b = self.b

        def body(j, _):
            w = self.slabs[1].at[j]
            for n in range(3):
                cols = slice(n * 256, n * 256 + 256)
                bias = self.vec[pl.ds(VUP + j, 1), cols]
                for h in range(2):
                    rows = slice(h * 256, h * 256 + 256)
                    pre = mm(b.nl[rows, :], w[:, cols]) + bias
                    cdf = 0.5 * (1.0 + lax.erf(pre * (1.0 / math.sqrt(2.0))))
                    pdf = jnp.exp(pre * pre * -0.5) * (1.0 / math.sqrt(2.0 * math.pi))
                    b.act[j, rows, cols] = (pre * cdf).astype(BF)
                    b.gp[j, rows, cols] = cdf + pre * pdf
            return 0

        lax.fori_loop(0, 4, body, 0)

    def feed_out(self):
        b = self.b
        for n in range(3):
            cols = slice(n * 256, n * 256 + 256)
            acc = self.b.n1[:, cols] * self.vec[VAG:VAG + 1, cols] + self.vec[VAS:VAS + 1, cols] + self.vec[VD:VD + 1, cols]
            for j in range(4):
                acc = acc + mm(b.act[j], self.slabs[2].at[j][:, cols])
            b.second[:, cols] = acc

        def body(r, sums):
            rows = pl.ds(pl.multiple_of(r * ROWS, ROWS), ROWS)
            n, scale = normalise(b.second[rows, :])
            c = self.og[rows, :].astype(F32)
            self.enc[rows, :] = (n * self.v(VFG) + self.v(VFS)).astype(BF)
            g = norm_back(c, self.v(VFG), n, scale)
            b.second[rows, :] = g
            low = g.astype(BF)
            b.nl[rows, :] = low
            return sums[0] + column_total(c * n), sums[1] + column_total(c), sums[2] + column_total(low)

        zero = jnp.zeros((1, WIDTH), F32)
        sums = lax.fori_loop(0, TOKENS // ROWS, body, (zero, zero, zero))
        self.gvec[VFG:VFG + 1, :], self.gvec[VFS:VFS + 1, :], self.gvec[VD:VD + 1, :] = sums

    def down_grads(self, j):
        b = self.b
        left = b.act[j].T
        for n in range(3):
            cols = slice(n * 256, n * 256 + 256)
            self.grads[2][j, :, cols] = mm(left, b.nl[:, cols]).astype(BF)

    def feed_back(self, j):
        b = self.b
        w = self.slabs[2].at[j]
        for n in range(3):
            cols = slice(n * 256, n * 256 + 256)
            total = jnp.zeros((1, 256), F32)
            for h in range(2):
                rows = slice(h * 256, h * 256 + 256)
                acc = mm_nt(b.nl[rows, :], w[cols, :])
                low = (acc * b.gp[j, rows, cols]).astype(BF)
                b.gpre[j, rows, cols] = low
                total = total + column_total(low)
            self.gvec[pl.ds(VUP + j, 1), cols] = total

    def up_grads(self, j):
        b = self.b
        for n in range(3):
            cols = slice(n * 256, n * 256 + 256)
            self.grads[1][j, :, cols] = mm(b.nlt[...], b.gpre[j, :, cols]).astype(BF)

    def norm1_back(self, n):
        b = self.b
        cols = slice(n * 256, n * 256 + 256)
        acc = b.second[:, cols]
        for j in range(4):
            acc = acc + mm_nt(b.gpre[j], self.slabs[1].at[j][cols, :])
        b.second[:, cols] = acc

    def norm1_rows(self):
        b = self.b

        def body(r, sums):
            rows = pl.ds(pl.multiple_of(r * ROWS, ROWS), ROWS)
            c = b.second[rows, :]
            n = b.n1[rows, :]
            g = norm_back(c, self.v(VAG), n, b.r1[rows, 0:1])
            b.second[rows, :] = g
            low = g.astype(BF)
            b.nl[rows, :] = low
            return sums[0] + column_total(c * n), sums[1] + column_total(c), sums[2] + column_total(low)

        zero = jnp.zeros((1, WIDTH), F32)
        sums = lax.fori_loop(0, TOKENS // ROWS, body, (zero, zero, zero))
        self.gvec[VAG:VAG + 1, :], self.gvec[VAS:VAS + 1, :], self.gvec[VO:VO + 1, :] = sums

    def out_grads(self):
        b = self.b
        left = b.mixed[...].T
        for n in range(3):
            cols = slice(n * 256, n * 256 + 256)
            self.grads[0][3, :, cols] = mm(left, b.nl[:, cols]).astype(BF)

    def out_back(self):
        b = self.b
        for n in range(3):
            cols = slice(n * 256, n * 256 + 256)
            b.mixed[:, cols] = mm_nt(b.nl[...], self.slabs[0].at[3][cols, :]).astype(BF)

    def attend_back(self, p):
        b = self.b
        masks, tall = half_masks(), row_masks()
        cols = slice(p * LANES, p * LANES + LANES)
        rows = [slice(s * SEQ, s * SEQ + SEQ) for s in range(2)]
        dos = [[b.mixed[rows[s], cols] * masks[a] for a in range(2)] for s in range(2)]
        dps = [[mm_nt(b.v[rows[s], cols], dos[s][a]) for a in range(2)] for s in range(2)]
        low = [[None, None], [None, None]]
        for s in range(2):
            atts = []
            for a in range(2):
                att = b.p[s * 12 + p * 2 + a]
                atts.append(att.astype(BF))
                dp = dps[s][a]
                low[s][a] = (att * (dp - jnp.sum(att * dp, 0, keepdims=True))).astype(BF)
            b.gpre[2, rows[s], cols] = mm(jnp.concatenate(atts, 1), jnp.concatenate(dos[s], 0)).astype(BF)
        for s in range(2):
            q, kt = b.q[rows[s], cols], b.k[rows[s], cols].T
            dk = mm(jnp.concatenate(low[s], 1), jnp.concatenate([q * masks[0], q * masks[1]], 0))
            b.gpre[1, rows[s], cols] = dk.astype(BF)
            dq = mm(jnp.concatenate([kt * tall[0], kt * tall[1]], 1), jnp.concatenate(low[s], 0))
            b.gpre[0, rows[s], cols] = (dq.T * 0.125).astype(BF)
        both = mm(b.xt[...], jnp.concatenate([b.gpre[0, :, cols], b.gpre[1, :, cols]], 1))
        self.grads[0][0, :, cols] = both[:, :LANES].astype(BF)
        self.grads[0][1, :, cols] = both[:, LANES:].astype(BF)
        self.grads[0][2, :, cols] = mm(b.xt[...], b.gpre[2, :, cols]).astype(BF)
        self.gvec[VQ:VQ + 1, cols] = column_total(b.gpre[0, :, cols])
        self.gvec[VV:VV + 1, cols] = column_total(b.gpre[2, :, cols])

    def input_grad(self, n):
        b = self.b
        cols = slice(n * 256, n * 256 + 256)
        acc = b.second[:, cols]
        for j in range(3):
            acc = acc + mm_nt(b.gpre[j], self.slabs[0].at[j][cols, :])
        b.second[:, cols] = acc


BUFFERS = dict(
    q=((TOKENS, WIDTH), BF), k=((TOKENS, WIDTH), BF), v=((TOKENS, WIDTH), BF), p=((24, SEQ, SEQ), F32),
    mixed=((TOKENS, WIDTH), BF), n1=((TOKENS, WIDTH), F32), r1=((TOKENS, LANES), F32), nl=((TOKENS, WIDTH), BF),
    act=((4, TOKENS, WIDTH), BF), gp=((4, TOKENS, WIDTH), F32), second=((TOKENS, WIDTH), F32),
    gpre=((4, TOKENS, WIDTH), BF), xt=((WIDTH, TOKENS), BF), nlt=((WIDTH, TOKENS), BF),
)


START = {16: 0, 8: 16, 4: 24}
WHOLE = tuple((part, 0, UNIT, ORDERS[part]) for part in range(PARTS))
CUT = tuple((i // 3, 16 * (i % 3), 16, ORDERS[i % 6]) for i in range(3 * PARTS))
CHAINS = (CUT, WHOLE, WHOLE)
FIRST = (0, 18, 24)
EVERY = ((0, 2), (0, 4), (0, 2), (0, 2))
VECTORS = "v0 v1 v2 v3".split() + "v4 v5 v6 v7".split()
SCRATCH = dict(
    wa=(SHAPES[0], BF), wb=(SHAPES[1], BF), wc=(SHAPES[2], BF), ga=(SHAPES[0], BF),
    rdb=((2, 1, 4, 2, 2, UNIT, WIDTH), BF), rdc=((4, 2, 2, 2, 1, UNIT, WIDTH), BF),
    rk=((3, 31, UNIT, WIDTH), BF), rx=((UNIT, WIDTH), BF), tall=((UNIT, WIDTH), F32),
    stage=((2, 4, 16, WIDTH), BF), final=((2, 2, 4, 16, WIDTH), BF),
    vt=((4, 2, 8, 2, LANES), F32), gv=((4, 2, 8, 2, LANES), F32),
    rv2=((3, 2, 8, 2, LANES), F32), rv1=((3, 4, 2, LANES), F32), rv0=((7, 2, LANES), F32),
    vec=((16, WIDTH), F32), gvec=((16, WIDTH), F32),
    x=((TOKENS, WIDTH), BF), qkv_in=((12, 3 * WIDTH), BF), out_in=((12, WIDTH), BF), up_in=((12, 4 * WIDTH), BF),
    **{name: ((1, 12), BF) for name in VECTORS}, v8=((1, 48), BF),
)
SEMS = dict(
    loads=(17,), mate_send=(2, 3), mate_recv=(2, 3), send=(3, PARTS, 7), recv=(3, PARTS, 7),
    sib_send=(3, PARTS), sib_recv=(3, PARTS), vsend=(9,), vrecv=(9,),
    gsib_send=(3, PARTS), gsib_recv=(3, PARTS), gsend=(30, 7), grecv=(30, 7),
    rep_send=(1,), rep_recv=(1,), gmate_send=(3, 7), gmate_recv=(3, 7), gvsend=(13,), gvrecv=(13,),
)


def box_count(box):
    return box[0][1] * box[1][1] * box[2][1] * box[3][1]


def split3(value):
    high = value.astype(BF)
    rest = value - high.astype(F32)
    mid = rest.astype(BF)
    return high, mid, (rest - mid.astype(F32)).astype(BF)


def owner_masks(block):
    d = lax.broadcasted_iota(jnp.int32, (64, WIDTH), 0)
    c = lax.broadcasted_iota(jnp.int32, (64, WIDTH), 1)
    if block is None:
        return d == (c * 43691) >> 19
    return d == 16 * block + ((c * 43691) >> 21)


def lane_picks(row):
    c = lax.broadcasted_iota(jnp.int32, (WIDTH, LANES), 0)
    lane = lax.broadcasted_iota(jnp.int32, (WIDTH, LANES), 1)
    if row is None:
        return (lane == c - 48 * ((c * 43691) >> 21)).astype(F32).astype(BF)
    return (lane == 12 * row + c - 12 * ((c * 43691) >> 19)).astype(F32).astype(BF)


def mega_kernel(lengths, *refs):
    vecs_in, (qkv_in, out_in, up_in, down_in, x_in, og_in,
               enc_out, sgrad_out, oqkv, oout, oup, odown, ovec), scratch = refs[:9], refs[9:22], refs[22:]
    r = b = types.SimpleNamespace(**dict(zip([*SCRATCH, *BUFFERS, *SEMS], scratch)))
    here = position()
    me = member_of(here)
    sibling = hop(here, CORE)
    twin = hop(here, X2)
    weights = (r.wa, r.wb, r.wc)
    grads = (r.ga, r.wb, r.wc)
    rds = (r.act.at[pl.ds(0, 3)].reshape((2, 1, 4, 2, 2, UNIT, WIDTH)), r.rdb, r.rdc)
    slabs = [w.reshape(4, WIDTH, WIDTH) for w in weights]
    gslabs = [w.reshape(4, WIDTH, WIDTH) for w in grads]
    layer = Layer(slabs, gslabs, r.vec, lengths, r.x, r.x, r.x, r.gvec, b)

    def own_at(phase):
        ylow, z, x, yhigh = (s for s, n in own_box(here))
        return (ylow, here.core, z, x, yhigh) if phase < 2 else (z, x, yhigh, ylow, here.core)

    def mate_copy(which, k):
        mate = mates(here)[k]
        return remote(r.stage.at[which, member_of(mate)], r.final.at[which, 0, me],
                      r.mate_send.at[which, k], r.mate_recv.at[which, k], mate)

    def assemble(which):
        for k in range(3):
            mate_copy(which, k).wait()
        r.final[which, 0, me] = r.stage[which, me]
        for i in range(4):
            r.tall[12 * i:12 * i + 12, :] = r.final[which, 0, i, 0:12, :].astype(F32)
        weights[which][own_at(which)] = r.tall[...].astype(BF)

    def push(phase, part, found, slot, there):
        w = weights[phase]
        for box in found:
            view = w.at[slices(phase, here.core, box, part)]
            remote(view, view, r.send.at[phase, part, slot], r.recv.at[phase, part, slot], there).start()

    def share(phase, part, found):
        w = weights[phase]
        for box in found:
            view = w.at[slices(phase, here.core, box, part)]
            remote(view, view, r.sib_send.at[phase, part], r.sib_recv.at[phase, part], sibling).start()

    def gather_first(phase):
        for part in range(PARTS):
            for slot, there in enumerate(trio(here, ORDERS[part])):
                push(phase, part, boxes(here, ()), slot, there)

    def gather(phase, step):
        w = weights[phase]
        for part in range(PARTS):
            order = ORDERS[part]
            if step == 2:
                for slot in range(3):
                    wait_units(w, phase, 1, part, r.recv.at[phase, part, slot])
            else:
                wait_units(w, phase, 1 << (step - 1), part, r.recv.at[phase, part, step])
            there = hop(here, order[step])
            if step < 4:
                push(phase, part, boxes(here, order[:step]), step + 1, there)
            else:
                for half, found in enumerate(halves(boxes(here, order[:4]))):
                    push(phase, part, found, 5 + half, there)
                share(phase, part, boxes(here, order[:4]))

    def gather_last(phase, half):
        for part in range(PARTS):
            order = ORDERS[part]
            wait_units(weights[phase], phase, 8, part, r.recv.at[phase, part, 5 + half])
            share(phase, part, halves(boxes(hop(here, order[4]), order[:4]))[half])

    def gathered(phase):
        for part in range(PARTS):
            wait_units(weights[phase], phase, 32, part, r.sib_recv.at[phase, part])

    def gather_sent(phase):
        for part in range(PARTS):
            wait_units(weights[phase], phase, 32, part, r.sib_send.at[phase, part])
            for slot, n in enumerate((1, 1, 1, 4, 8, 8, 8)):
                wait_units(weights[phase], phase, n, part, r.send.at[phase, part, slot])

    def vec_tile(place):
        return (place.z, place.x % 2, place.y * 2 + place.core)

    def vec_pair(place):
        return (place.z, place.x % 2, pl.ds(place.y // 2 * 4, 4))

    def vec_ring(place):
        return (pl.ds(place.z // 2 * 2, 2), place.x % 2)

    def vec_peers(k):
        return (mates(here), trio(here, (Y3, Z1)), trio(here, (Z3, X1)))[k]

    def vec_copies(k):
        view = r.vt.at[(vec_tile, vec_pair, vec_ring)[k](here)]
        return [remote(view, view, r.vsend.at[3 * k + i], r.vrecv.at[3 * k + i], there) for i, there in enumerate(vec_peers(k))]

    def vec_start(k):
        for copy in vec_copies(k):
            copy.start()

    def vec_wait(k):
        for copy in vec_copies(k):
            copy.wait()

    def expand():
        first = r.vt[:, :, :, 0, :].reshape(64, LANES)
        second = r.vt[:, :, :, 1, :].reshape(64, LANES).astype(BF)
        mask = owner_masks(None)
        turned = [first] + [pltpu.roll(first, LANES - 12 * row, 1) for row in range(1, 8)]
        t = mm_nt(jnp.concatenate(turned, 0).astype(BF), lane_picks(0)).reshape(8, 64, WIDTH)
        for row in range(8):
            r.vec[row:row + 1, :] = jnp.sum(jnp.where(mask, t[row], 0.0), 0, keepdims=True)
        t = mm_nt(second, lane_picks(None))
        for j in range(4):
            r.vec[8 + j:9 + j, :] = jnp.sum(jnp.where(owner_masks(j), t, 0.0), 0, keepdims=True)

    def sib_copy(phase, k):
        g, rd = grads[phase], rds[phase]
        if phase == 0:
            cols = pl.ds(k * LANES, LANES)
            src = g.at[:, pl.ds(sibling.core, 1), :, :, :, :, cols]
            dst = rd.at[:, :, :, :, :, :, cols]
        elif phase == 1:
            src, dst = g.at[k, sibling.core], rd.at[k, 0]
        else:
            src, dst = g.at[k, :, :, :, pl.ds(sibling.core, 1)], rd.at[k]
        return remote(src, dst, r.gsib_send.at[phase, k], r.gsib_recv.at[phase, k], sibling)

    def sib_add(phase, k):
        sib_copy(phase, k).wait()
        g, rd = grads[phase], rds[phase]
        for i in range(4):
            if phase == 0:
                at = slices(0, here.core, ((0, 2), (i, 1), (0, 2), (0, 2)), k)
                g[at] = g[at] + rd[slices(0, 0, ((0, 2), (i, 1), (0, 2), (0, 2)), k)]
            elif phase == 1:
                g[k, here.core, i] = g[k, here.core, i] + rd[k, 0, i]
            else:
                at = (k, i // 2, i % 2, slice(None), pl.ds(here.core, 1))
                g[at] = g[at] + rd[k, i // 2, i % 2]

    def unit_slices(phase, box, chain):
        part, row, rows, _ = chain
        return slices(phase, here.core, box, part)[:5] + (slice(row, row + rows), slice(part * LANES, part * LANES + LANES))

    def hop_start(phase, c, step):
        chain = CHAINS[phase][c]
        order = chain[3]

        def send(box, at, slot, there):
            n = box_count(box)
            src = grads[phase].at[slices(phase, here.core, box, chain[0])[:5]]
            dst = r.rk.at[phase, pl.ds(at, n)].reshape(src.shape)
            at5 = (slice(None),) * 5 + (pl.ds(chain[1], chain[2]), pl.ds(chain[0] * LANES, LANES))
            remote(src.at[at5], dst.at[at5], r.gsend.at[FIRST[phase] + c, slot], r.grecv.at[FIRST[phase] + c, slot], there).start()
            return at + n

        if step == 1:
            for slot, there in enumerate(trio(here, order)):
                send(boxes(there, ())[0], 28 + slot, slot, there)
            return
        if phase == 0 and step == 3:
            for i, there in enumerate(trio(here, order[2:])):
                at = 16 + 4 * i
                for box in boxes(there, order[:2]):
                    at = send(box, at, 3 + i, there)
            return
        there = hop(here, order[step])
        at = START[1 << step]
        for box in boxes(there, order[:step]):
            at = send(box, at, step + 2, there)

    def landing(phase, c, at, n):
        part, row, rows, _ = CHAINS[phase][c]
        return r.rk.at[phase, pl.ds(at, n), pl.ds(row, rows), pl.ds(part * LANES, LANES)]

    def hop_add(phase, c, step):
        g = grads[phase]
        chain = CHAINS[phase][c]
        if step == 1:
            where = unit_slices(phase, boxes(here, ())[0], chain)
            total = g[where].astype(F32)
            for slot in range(3):
                view = landing(phase, c, 28 + slot, 1)
                pltpu.make_async_copy(view, view, r.grecv.at[FIRST[phase] + c, slot]).wait()
                total = total + view[...].astype(F32).reshape(total.shape)
            g[where] = total.astype(BF)
            return
        if phase == 0 and step == 3:
            for i in range(3):
                view = landing(phase, c, 16 + 4 * i, 4)
                pltpu.make_async_copy(view, view, r.grecv.at[FIRST[phase] + c, 3 + i]).wait()
            at = 16
            for box in boxes(here, chain[3][:2]):
                m = box_count(box)
                where = unit_slices(phase, box, chain)
                total = g[where].astype(F32)
                for i in range(3):
                    total = total + landing(phase, c, at + 4 * i, m)[...].astype(F32).reshape(total.shape)
                g[where] = total.astype(BF)
                at += m
            return
        n = 1 << step
        at = START[n]
        view = landing(phase, c, at, n)
        pltpu.make_async_copy(view, view, r.grecv.at[FIRST[phase] + c, step + 2]).wait()
        for box in boxes(here, chain[3][:step]):
            m = box_count(box)
            where = unit_slices(phase, box, chain)
            old = g[where]
            g[where] = old + landing(phase, c, at, m)[...].reshape(old.shape)
            at += m

    def rep_copy():
        return remote(grads[2].at[own_at(2)], r.rx, r.rep_send.at[0], r.rep_recv.at[0], twin)

    def reduce_first(phase):
        for k in range(2 if phase == 1 else 4):
            sib_add(phase, k)
        for part in range(PARTS):
            hop_start(phase, part, 4)

    def move(phase, c, step):
        hop_add(phase, c, step)
        if step > 1:
            hop_start(phase, c, 1 if phase == 0 and step == 3 else step - 1)

    def reduce(phase, step):
        for part in range(PARTS):
            move(phase, part, step)

    def first_part(part):
        sib_add(0, part)
        for c, chain in enumerate(CUT):
            if chain[0] == part:
                hop_start(0, c, 4)

    def move_part(part, step):
        for c, chain in enumerate(CUT):
            if chain[0] == part:
                move(0, c, step)

    def gmate_copy(which, k):
        others = mates(here)
        there = (others + [twin] + [hop(mate, X2) for mate in others])[k]
        cols = (pl.ds(0, 512), pl.ds(0, WIDTH), pl.ds(512, 256))[which]
        phase = which % 2
        return remote(r.stage.at[phase, member_of(there), :, cols], r.final.at[phase, k // 3 if k < 6 else 1, me, :, cols],
                      r.gmate_send.at[which, k], r.gmate_recv.at[which, k], there)

    def hand_over(which):
        phase = which % 2
        cols = (slice(0, 512), slice(0, WIDTH), slice(512, WIDTH))[which]
        r.tall[:, cols] = grads[phase][own_at(phase) + (slice(None), cols)].astype(F32)
        for i in range(4):
            r.stage[phase, i, 0:12, cols] = r.tall[12 * i:12 * i + 12, cols].astype(BF)
        for k in range(7):
            gmate_copy(which, k).start()

    def deliver(which):
        phase = which % 2
        cols = (slice(0, 512), slice(0, WIDTH), slice(512, WIDTH))[which]
        for k in range(7):
            gmate_copy(which, k).wait()
        r.final[phase, 0, me, :, cols] = r.stage[phase, me, :, cols]
        for i in range(4):
            at = slice(i * WIDTH + cols.start, i * WIDTH + cols.stop)
            dst = oup.at[:, at] if phase else (oqkv.at[:, at] if i < 3 else oout.at[:, cols])
            dst[...] = r.final[phase, 0, i, 0:12, cols].astype(F32) + r.final[phase, 1, i, 0:12, cols].astype(F32)

    def deliver_down():
        rep_copy().wait()
        odown[...] = grads[2][own_at(2)].astype(F32) + r.rx[...].astype(F32)

    def reduce_sent(phase):
        for c in range(len(CHAINS[phase])):
            for slot, n in enumerate((1, 1, 1, 4, 4, 4, 16) if phase == 0 else (1, 1, 1, 0, 4, 8, 16)):
                if n == 0:
                    continue
                view = landing(phase, c, 0, n)
                pltpu.make_async_copy(view, view, r.gsend.at[FIRST[phase] + c, slot]).wait()

    def pack_rows(first, count):
        mask = owner_masks(None).astype(F32).astype(BF)
        pieces = split3(r.gvec[first:first + count, :])
        spread = [piece[i:i + 1, :] * mask for piece in pieces for i in range(count)]
        out = mm(jnp.concatenate(spread, 0), lane_picks(0)).reshape(3, count, 64, LANES)
        out = out[0] + out[1] + out[2]
        total = out[0] if first == 0 else pltpu.roll(out[0], 12 * first, 1)
        for i in range(1, count):
            total = total + pltpu.roll(out[i], 12 * (first + i), 1)
        return total.reshape(4, 2, 8, LANES)

    def pack():
        pieces = split3(r.gvec[8:12, :])
        masks = [owner_masks(j).astype(F32).astype(BF) for j in range(4)]
        spread = [piece[j:j + 1, :] * masks[j] for piece in pieces for j in range(4)]
        out = mm(jnp.concatenate(spread, 0), lane_picks(None)).reshape(12, 64, LANES)
        r.gv[:, :, :, 0, :] = pack_rows(2, 6)
        r.gv[:, :, :, 1, :] = jnp.sum(out, 0).reshape(4, 2, 8, LANES)

    def gvec_copies(k):
        if k == 0:
            peers = mates(here) + [twin] + [hop(mate, X2) for mate in mates(here)]
        else:
            peers = vec_peers(k)
        part, landing_ref = ((vec_tile, r.rv0), (vec_pair, r.rv1), (vec_ring, r.rv2))[k]
        base = (6, 3, 0)[k]
        return [remote(r.gv.at[part(there)], landing_ref.at[i], r.gvsend.at[base + i], r.gvrecv.at[base + i], there)
                for i, there in enumerate(peers)]

    def gvec_start(k):
        for copy in gvec_copies(k):
            copy.start()

    def gvec_add(k):
        part, landing_ref = ((vec_tile, r.rv0), (vec_pair, r.rv1), (vec_ring, r.rv2))[k]
        at = part(here)
        total = r.gv[at]
        for i, copy in enumerate(gvec_copies(k)):
            copy.wait()
            total = total + landing_ref[i].reshape(total.shape)
        r.gv[at] = total

    near = [hop(here, link) for link in (Y1, Y3, Z1, Z3, X1, X3, CORE, X2, Y2, Z2)]
    near += [mates(here)[2], hop(hop(here, Y3), Z1), hop(hop(here, Y1), Z3)]
    near += [hop(mate, X2) for mate in mates(here)]
    near += [hop(hop(here, a), c) for a, c in ((Z3, X1), (X1, Z1), (X3, Y3), (X3, Y1))]
    loads = [pltpu.make_async_copy(src, dst, r.loads.at[i]) for i, (src, dst) in enumerate((
        (qkv_in, r.qkv_in), (out_in, r.out_in), (up_in, r.up_in), (down_in, weights[2].at[own_at(2)]), (x_in, r.x)))]
    held = [getattr(r, name) for name in VECTORS] + [r.v8]
    vec_loads = [pltpu.make_async_copy(src, dst, r.loads.at[8 + i]) for i, (src, dst) in enumerate(zip(vecs_in, held))]
    for load in loads[:4] + vec_loads + loads[4:]:
        load.start()
    barrier = pltpu.get_barrier_semaphore()
    for place in near:
        pl.semaphore_signal(barrier, inc=1, device_id=device_of(place), device_id_type=MESH)
    og_load = pltpu.make_async_copy(og_in, r.x, r.loads.at[5])
    own = vec_tile(here)
    r.vt[own] = jnp.zeros((2, LANES), F32)
    for load in loads[:4] + vec_loads:
        load.wait()
    for i in range(8):
        r.vt[own + (slice(0, 1), slice(12 * i, 12 * i + 12))] = held[i][...].astype(F32)
    r.vt[own + (slice(1, 2), slice(0, 48))] = held[8][...].astype(F32)
    for i in range(4):
        r.stage[0, i, 0:12, :] = r.qkv_in[:, i * WIDTH:(i + 1) * WIDTH] if i < 3 else r.out_in[...]
        r.stage[1, i, 0:12, :] = r.up_in[:, i * WIDTH:(i + 1) * WIDTH]
    pl.semaphore_wait(barrier, len(near))
    for k in range(3):
        mate_copy(0, k).start()
    vec_start(0)
    for k in range(3):
        mate_copy(1, k).start()
    gather_first(2)
    assemble(0)
    vec_wait(0)
    vec_start(1)
    gather_first(0)
    assemble(1)
    gather_first(1)
    loads[4].wait()
    b.xt[...] = r.x[...].T
    vec_wait(1)
    vec_start(2)
    gather(0, 2)
    gather(2, 2)
    gather(1, 2)
    gather(0, 3)
    vec_wait(2)
    expand()
    gather(0, 4)
    gather(1, 3)
    gather(2, 3)
    gather_last(0, 0)
    gather_last(0, 1)
    gathered(0)
    layer.project(0)
    gather(1, 4)
    layer.project(1)
    layer.project(2)
    gather(2, 4)
    layer.attend()
    gather_last(1, 0)
    gather_last(1, 1)
    layer.attn_out()
    og_load.start()
    b.nlt[...] = b.nl[...].T
    gather_last(2, 0)
    gather_last(2, 1)
    gathered(1)
    layer.feed()
    og_load.wait()
    gathered(2)
    layer.feed_out()
    enc_store = pltpu.make_async_copy(r.x, enc_out, r.loads.at[6])
    enc_store.start()
    gather_sent(2)

    def down_body(j, _):
        layer.feed_back(j)
        layer.down_grads(j)
        sib_copy(2, j).start()
        return 0

    lax.fori_loop(0, 4, down_body, 0)
    for n in range(3):
        layer.norm1_back(n)
    reduce_first(2)
    gather_sent(1)

    def up_body(i, _):
        layer.up_grads(i * 2 + sibling.core)
        sib_copy(1, i).start()
        return 0

    def up_own(i, _):
        layer.up_grads(i * 2 + here.core)
        return 0

    lax.fori_loop(0, 2, up_body, 0)
    lax.fori_loop(0, 2, up_own, 0)
    layer.norm1_rows()
    layer.out_grads()
    reduce(2, 4)
    reduce_first(1)
    layer.out_back()
    pack()
    layer.attend_back(0)
    sib_copy(0, 0).start()
    reduce(2, 3)
    layer.attend_back(1)
    sib_copy(0, 1).start()
    first_part(0)
    layer.attend_back(2)
    sib_copy(0, 2).start()
    reduce(1, 4)
    first_part(1)
    layer.attend_back(3)
    sib_copy(0, 3).start()
    reduce(2, 2)
    first_part(2)
    move_part(0, 4)
    layer.attend_back(4)
    sib_copy(0, 4).start()
    reduce(1, 3)
    first_part(3)
    move_part(1, 4)
    layer.attend_back(5)
    sib_copy(0, 5).start()
    first_part(4)
    r.gv[:, :, :, 0, :] = r.gv[:, :, :, 0, :] + pack_rows(VQ, 2)
    gvec_start(2)
    reduce(2, 1)
    rep_copy().start()
    move_part(0, 3)
    move_part(2, 4)
    layer.input_grad(0)
    first_part(5)
    layer.input_grad(1)
    reduce(1, 2)
    move_part(3, 4)
    layer.input_grad(2)
    sgrad_store = pltpu.make_async_copy(b.second, sgrad_out, r.loads.at[7])
    sgrad_store.start()
    move_part(1, 3)
    move_part(4, 4)
    gvec_add(2)
    gvec_start(1)
    move_part(2, 3)
    move_part(5, 4)
    reduce(1, 1)
    hand_over(1)
    move_part(0, 1)
    move_part(3, 3)
    move_part(4, 3)
    gvec_add(1)
    gvec_start(0)
    move_part(1, 1)
    deliver_down()
    move_part(5, 3)
    move_part(2, 1)
    move_part(3, 1)
    hand_over(0)
    move_part(4, 1)
    deliver(1)
    move_part(5, 1)
    hand_over(2)
    gvec_add(0)
    ovec[...] = r.gv[vec_tile(here)]
    for phase in range(1, 3):
        reduce_sent(phase)
    gather_sent(0)
    reduce_sent(0)
    enc_store.wait()
    sgrad_store.wait()
    deliver(0)
    deliver(2)


def run_layer(lengths, vecs, qkv, out, up, down, x, og):
    vm = pl.BlockSpec(memory_space=pltpu.VMEM)
    hb = pl.BlockSpec(memory_space=pl.ANY)
    return pl.pallas_call(
        mega_kernel,
        out_shape=[
            jax.ShapeDtypeStruct((TOKENS, WIDTH), BF), jax.ShapeDtypeStruct((TOKENS, WIDTH), F32),
            jax.ShapeDtypeStruct((12, 3 * WIDTH), F32), jax.ShapeDtypeStruct((12, WIDTH), F32),
            jax.ShapeDtypeStruct((12, 4 * WIDTH), F32), jax.ShapeDtypeStruct((UNIT, WIDTH), F32), jax.ShapeDtypeStruct((2, LANES), F32),
        ],
        in_specs=[pl.BlockSpec(memory_space=pltpu.SMEM)] + [hb] * 15,
        out_specs=[hb, hb] + [vm] * 5,
        scratch_shapes=[pltpu.VMEM(s, d) for s, d in SCRATCH.values()] + [pltpu.VMEM(s, d) for s, d in BUFFERS.values()]
        + [pltpu.SemaphoreType.DMA(s) for s in SEMS.values()],
        compiler_params=pltpu.CompilerParams(collective_id=1, has_side_effects=True, vmem_limit_bytes=63 * 2**20),
    )(lengths, *vecs, qkv, out, up, down, x, og)


def finish_kernel(*refs):
    srcs, dsts, vec_outs, held, parts, sems = refs[:7], refs[7:13], refs[13:22], refs[22:29], refs[29:38], refs[38]
    loads = [pltpu.make_async_copy(src, mid, sems.at[0, i]) for i, (src, mid) in enumerate(zip(srcs, held))]
    stores = [pltpu.make_async_copy(mid, dst, sems.at[1, i]) for i, (mid, dst) in enumerate(zip(held, dsts))]
    vec_stores = [pltpu.make_async_copy(mid, dst, sems.at[1, 6 + i]) for i, (mid, dst) in enumerate(zip(parts, vec_outs))]
    for load in loads[::-1]:
        load.start()
    loads[6].wait()
    vec = held[6]
    for i in range(8):
        parts[i][...] = vec[0:1, 12 * i:12 * i + 12]
    parts[8][...] = vec[1:2, 0:48]
    for store in vec_stores:
        store.start()
    for load, store in list(zip(loads, stores))[::-1]:
        load.wait()
        store.start()
    for store in vec_stores + stores:
        store.wait()


def finish(results):
    hb = pl.BlockSpec(memory_space=pl.ANY)
    small = [(1, n) for n in [12] * 8 + [48]]
    return pl.pallas_call(
        finish_kernel,
        out_shape=[jax.ShapeDtypeStruct(a.shape, a.dtype) for a in results[:6]] + [jax.ShapeDtypeStruct(n, F32) for n in small],
        in_specs=[hb] * 7,
        out_specs=[hb] * 15,
        scratch_shapes=[pltpu.VMEM(a.shape, a.dtype) for a in results] + [pltpu.VMEM(n, F32) for n in small]
        + [pltpu.SemaphoreType.DMA((2, 15))],
        compiler_params=pltpu.CompilerParams(vmem_limit_bytes=63 * 2**20),
    )(*results)


def local(states, qkv_weight, query_bias, value_bias, out_weight, out_bias, attn_gain, attn_shift, up_weight, up_bias,
          down_weight, down_bias, ffn_gain, ffn_shift, out_grad, lengths):
    vecs = [v.reshape(1, -1) for v in (query_bias, value_bias, out_bias, attn_gain, attn_shift, down_bias, ffn_gain, ffn_shift, up_bias)]
    results = run_layer(
        lengths.reshape(1, 2), vecs, qkv_weight, out_weight, up_weight, down_weight,
        states.reshape(TOKENS, WIDTH), out_grad.reshape(TOKENS, WIDTH))
    enc, sgrad, oqkv, oout, oup, odown, *o = finish(results)
    o = [v.reshape(-1) for v in o]
    return (enc.reshape(states.shape), sgrad.reshape(states.shape), oqkv, o[0], o[1], oout, o[2], o[3], o[4],
            oup, o[8], odown, o[5], o[6], o[7])


def solution(mesh):
    return jax.shard_map(
        local,
        mesh=mesh,
        in_specs=(
            P(None, ("dp", "rep"), None, None),
            P("dp", None),
            P("dp"),
            P("dp"),
            P("dp", None),
            P("dp"),
            P("dp"),
            P("dp"),
            P("dp", None),
            P("dp"),
            P("dp", None),
            P("dp"),
            P("dp"),
            P("dp"),
            P(None, ("dp", "rep"), None, None),
            P(None, ("dp", "rep")),
        ),
        out_specs=(
            P(None, ("dp", "rep"), None, None),
            P(None, ("dp", "rep"), None, None),
            P("dp", None),
            P("dp"),
            P("dp"),
            P("dp", None),
            P("dp"),
            P("dp"),
            P("dp"),
            P("dp", None),
            P("dp"),
            P("dp", None),
            P("dp"),
            P("dp"),
            P("dp"),
        ),
        check_vma=False,
    )
```

```python
import collections
import math
import types

import jax
import jax.numpy as jnp
from jax import lax
from jax.experimental import pallas as pl
from jax.experimental.pallas import tpu as pltpu
from jax.sharding import PartitionSpec as P

Place = collections.namedtuple("Place", "core y z x")
MESH = pl.DeviceIdType.MESH
BF = jnp.bfloat16
F32 = jnp.float32
WIDTH = 768
UNIT = 48
LANES = 128
PARTS = 6

CORE, Y1, Y3, Z1, Z3, X1, X2, X3 = (0, 0), (1, 1), (1, 3), (2, 1), (2, 3), (3, 1), (3, 2), (3, 3)
Y2, Z2 = (1, 2), (2, 2)

ORDERS = (
    (Z1, Z3, Y1, Y3, X1),
    (Y1, Y3, Z1, Z3, X3),
    (Y3, Z1, Z3, X1, Y1),
    (Y1, Z3, X1, Z1, Y3),
    (Y1, Z3, X3, Y3, Z1),
    (Z1, Y3, X3, Y1, Z3),
)


def position():
    dp = lax.axis_index("dp")
    rep = lax.axis_index("rep")
    return Place(dp % 2, (dp // 2) % 4, dp // 16, rep * 2 + (dp // 8) % 2)


def device_of(place):
    dp = ((place.z * 2 + place.x % 2) * 4 + place.y) * 2 + place.core
    return (dp, place.x // 2)


def hop(place, link):
    axis, how = link
    p = place[axis]
    moved = (1 - p, p + 1 - 2 * (p % 2), (p + 2) % 4, 3 - p)[how]
    return Place(*(moved if i == axis else q for i, q in enumerate(place)))


def boxes(place, links):
    y, z, x = place.y, place.z, place.x % 2
    if Y1 in links and Y3 in links:
        ys = [((0, 2), (0, 2))]
    elif Y1 in links:
        ys = [((0, 2), (y // 2, 1))]
    elif Y3 in links:
        ys = [((y % 2, 1), (y // 2, 1)), ((1 - y % 2, 1), (1 - y // 2, 1))]
    else:
        ys = [((y % 2, 1), (y // 2, 1))]
    if Z1 in links and Z3 in links:
        zs = [(0, 4)]
    elif Z1 in links:
        zs = [((z // 2) * 2, 2)]
    elif Z3 in links:
        zs = [(z, 1), (3 - z, 1)]
    else:
        zs = [(z, 1)]
    xs = (0, 2) if X1 in links or X3 in links else (x, 1)
    return [(ylow, zz, xs, yhigh) for (ylow, yhigh) in ys for zz in zs]


def slices(phase, core, box, part):
    ylow, z, x, yhigh = (pl.ds(*s) for s in box)
    cols = pl.ds(part * LANES, LANES)
    if phase < 2:
        return (ylow, pl.ds(core, 1), z, x, yhigh, slice(None), cols)
    return (z, x, yhigh, ylow, pl.ds(core, 1), slice(None), cols)


SHAPES = (
    (2, 2, 4, 2, 2, UNIT, WIDTH),
    (2, 2, 4, 2, 2, UNIT, WIDTH),
    (4, 2, 2, 2, 2, UNIT, WIDTH),
)


def size_box(count):
    sizes = {1: (1, 1, 1, 1), 2: (1, 1, 1, 2), 4: (1, 1, 2, 2), 8: (1, 2, 2, 2), 16: (1, 4, 2, 2), 32: (2, 4, 2, 2)}[count]
    return tuple((0, n) for n in sizes)


def wait_units(ref, phase, count, part, sem):
    view = ref.at[slices(phase, 0, size_box(count), part)]
    pltpu.make_async_copy(view, view, sem).wait()


def remote(src, dst, send_sem, recv_sem, place):
    return pltpu.make_async_remote_copy(
        src_ref=src, dst_ref=dst, send_sem=send_sem, recv_sem=recv_sem,
        device_id=device_of(place), device_id_type=MESH,
    )


def greet(places):
    barrier = pltpu.get_barrier_semaphore()
    for place in places:
        pl.semaphore_signal(barrier, inc=1, device_id=device_of(place), device_id_type=MESH)
    pl.semaphore_wait(barrier, len(places))


def member_of(place):
    return (place.y % 2) * 2 + place.core


def mates(here):
    return [hop(here, CORE), hop(here, Y1), hop(hop(here, CORE), Y1)]


def own_box(here):
    return boxes(here, ())[0]


def trio(place, order):
    a, b = hop(place, order[0]), hop(place, order[1])
    return a, b, hop(a, order[1])


def halves(found):
    if len(found) == 2:
        return [found[:1], found[1:]]
    ylow, (start, n), x, yhigh = found[0]
    return [[(ylow, (start, n // 2), x, yhigh)], [(ylow, (start + n // 2, n // 2), x, yhigh)]]


HALF = 256
SEQ = 256
TOKENS = 512
ROWS = 128
epsilon = 1e-05
NT = (((1,), (1,)), ((), ()))
TN = (((0,), (0,)), ((), ()))
VQ, VV, VO, VAG, VAS, VD, VFG, VFS, VUP = range(9)


def mm(left, right):
    return jnp.dot(left, right, preferred_element_type=F32)


def mm_nt(left, right):
    return lax.dot_general(left, right, NT, preferred_element_type=F32)


def mm_tn(left, right):
    return lax.dot_general(left, right, TN, preferred_element_type=F32)


def normalise(value):
    center = value - jnp.mean(value, -1, keepdims=True)
    scale = lax.rsqrt(jnp.mean(center * center, -1, keepdims=True) + epsilon)
    return center * scale, scale


def norm_back(cot, gain, n, scale):
    e = cot * gain
    return scale * (e - jnp.mean(e, -1, keepdims=True) - n * jnp.mean(e * n, -1, keepdims=True))


def half_masks():
    lane = lax.broadcasted_iota(jnp.int32, (1, LANES), 1)
    low = (lane < 64).astype(F32).astype(BF)
    return low, (1.0 - low.astype(F32)).astype(BF)


def row_masks():
    row = lax.broadcasted_iota(jnp.int32, (LANES, SEQ), 0)
    low = (row < 64).astype(F32).astype(BF)
    return low, (1.0 - low.astype(F32)).astype(BF)


def column_total(ref_rows):
    return jnp.sum(ref_rows.astype(F32), 0, keepdims=True)


class Layer:
    def __init__(self, slabs, grads, vec, lengths, x, og, enc, gvec, b):
        self.slabs, self.grads, self.vec, self.lengths, self.x, self.og = slabs, grads, vec, lengths, x, og
        self.enc, self.gvec, self.b = enc, gvec, b

    def v(self, row):
        return self.vec[row:row + 1, :]

    def project(self, n):
        b = self.b
        cols = slice(n * 256, n * 256 + 256)
        x = self.x[...]
        b.q[:, cols] = ((mm(x, self.slabs[0].at[0][:, cols]) + self.vec[VQ:VQ + 1, cols]).astype(BF).astype(F32) * 0.125).astype(BF)
        b.k[:, cols] = mm(x, self.slabs[0].at[1][:, cols]).astype(BF)
        b.v[:, cols] = (mm(x, self.slabs[0].at[2][:, cols]) + self.vec[VV:VV + 1, cols]).astype(BF)

    def attend(self):
        b = self.b
        masks, tall = half_masks(), row_masks()
        key = lax.broadcasted_iota(jnp.int32, (SEQ, SEQ), 0)

        def body(p, _):
            cols = pl.ds(pl.multiple_of(p * LANES, LANES), LANES)
            rows = [slice(s * SEQ, s * SEQ + SEQ) for s in range(2)]
            scores = [[mm_nt(b.k[rows[s], cols] * masks[a], b.q[rows[s], cols]) for a in range(2)] for s in range(2)]
            low = [[None, None], [None, None]]
            for s in range(2):
                length = self.lengths[0, s]
                for a in range(2):
                    st = jnp.where(key < length, scores[s][a], -1e9)
                    e = jnp.exp(st - jnp.max(st, 0, keepdims=True))
                    att = e * (1.0 / jnp.sum(e, 0, keepdims=True))
                    b.p[s * 12 + p * 2 + a] = att
                    low[s][a] = att.astype(BF)
            for s in range(2):
                vt = b.v[rows[s], cols].T
                out = mm(jnp.concatenate([vt * tall[0], vt * tall[1]], 1), jnp.concatenate(low[s], 0))
                b.mixed[rows[s], cols] = out.T.astype(BF)
            return 0

        lax.fori_loop(0, 6, body, 0)

    def attn_out(self):
        b = self.b
        for n in range(3):
            cols = slice(n * 256, n * 256 + 256)
            acc = mm(b.mixed[...], self.slabs[0].at[3][:, cols]) + self.vec[VO:VO + 1, cols]
            b.n1[:, cols] = self.x[:, cols].astype(F32) + acc

        def body(r, _):
            rows = pl.ds(pl.multiple_of(r * ROWS, ROWS), ROWS)
            n, scale = normalise(b.n1[rows, :])
            b.n1[rows, :] = n
            b.r1[rows, :] = jnp.broadcast_to(scale, (ROWS, LANES))
            b.nl[rows, :] = (n * self.v(VAG) + self.v(VAS)).astype(BF)
            return 0

        lax.fori_loop(0, TOKENS // ROWS, body, 0)

    def feed(self):
        b = self.b

        def body(j, _):
            w = self.slabs[1].at[j]
            for n in range(3):
                cols = slice(n * 256, n * 256 + 256)
                bias = self.vec[pl.ds(VUP + j, 1), cols]
                for h in range(2):
                    rows = slice(h * 256, h * 256 + 256)
                    pre = mm(b.nl[rows, :], w[:, cols]) + bias
                    cdf = 0.5 * (1.0 + lax.erf(pre * (1.0 / math.sqrt(2.0))))
                    pdf = jnp.exp(pre * pre * -0.5) * (1.0 / math.sqrt(2.0 * math.pi))
                    b.act[j, rows, cols] = (pre * cdf).astype(BF)
                    b.gp[j, rows, cols] = cdf + pre * pdf
            return 0

        lax.fori_loop(0, 4, body, 0)

    def feed_out(self):
        b = self.b
        for n in range(3):
            cols = slice(n * 256, n * 256 + 256)
            acc = self.b.n1[:, cols] * self.vec[VAG:VAG + 1, cols] + self.vec[VAS:VAS + 1, cols] + self.vec[VD:VD + 1, cols]
            for j in range(4):
                acc = acc + mm(b.act[j], self.slabs[2].at[j][:, cols])
            b.second[:, cols] = acc

        def body(r, sums):
            rows = pl.ds(pl.multiple_of(r * ROWS, ROWS), ROWS)
            n, scale = normalise(b.second[rows, :])
            c = self.og[rows, :].astype(F32)
            self.enc[rows, :] = (n * self.v(VFG) + self.v(VFS)).astype(BF)
            g = norm_back(c, self.v(VFG), n, scale)
            b.second[rows, :] = g
            low = g.astype(BF)
            b.nl[rows, :] = low
            return sums[0] + column_total(c * n), sums[1] + column_total(c), sums[2] + column_total(low)

        zero = jnp.zeros((1, WIDTH), F32)
        sums = lax.fori_loop(0, TOKENS // ROWS, body, (zero, zero, zero))
        self.gvec[VFG:VFG + 1, :], self.gvec[VFS:VFS + 1, :], self.gvec[VD:VD + 1, :] = sums

    def down_grads(self, j):
        b = self.b
        left = b.act[j].T
        for n in range(3):
            cols = slice(n * 256, n * 256 + 256)
            self.grads[2][j, :, cols] = mm(left, b.nl[:, cols]).astype(BF)

    def feed_back(self, j):
        b = self.b
        w = self.slabs[2].at[j]
        for n in range(3):
            cols = slice(n * 256, n * 256 + 256)
            total = jnp.zeros((1, 256), F32)
            for h in range(2):
                rows = slice(h * 256, h * 256 + 256)
                acc = mm_nt(b.nl[rows, :], w[cols, :])
                low = (acc * b.gp[j, rows, cols]).astype(BF)
                b.gpre[j, rows, cols] = low
                total = total + column_total(low)
            self.gvec[pl.ds(VUP + j, 1), cols] = total

    def up_grads(self, j):
        b = self.b
        for n in range(3):
            cols = slice(n * 256, n * 256 + 256)
            self.grads[1][j, :, cols] = mm(b.nlt[...], b.gpre[j, :, cols]).astype(BF)

    def norm1_back(self, n):
        b = self.b
        cols = slice(n * 256, n * 256 + 256)
        acc = b.second[:, cols]
        for j in range(4):
            acc = acc + mm_nt(b.gpre[j], self.slabs[1].at[j][cols, :])
        b.second[:, cols] = acc

    def norm1_rows(self):
        b = self.b

        def body(r, sums):
            rows = pl.ds(pl.multiple_of(r * ROWS, ROWS), ROWS)
            c = b.second[rows, :]
            n = b.n1[rows, :]
            g = norm_back(c, self.v(VAG), n, b.r1[rows, 0:1])
            b.second[rows, :] = g
            low = g.astype(BF)
            b.nl[rows, :] = low
            return sums[0] + column_total(c * n), sums[1] + column_total(c), sums[2] + column_total(low)

        zero = jnp.zeros((1, WIDTH), F32)
        sums = lax.fori_loop(0, TOKENS // ROWS, body, (zero, zero, zero))
        self.gvec[VAG:VAG + 1, :], self.gvec[VAS:VAS + 1, :], self.gvec[VO:VO + 1, :] = sums

    def out_grads(self):
        b = self.b
        left = b.mixed[...].T
        for n in range(3):
            cols = slice(n * 256, n * 256 + 256)
            self.grads[0][3, :, cols] = mm(left, b.nl[:, cols]).astype(BF)

    def out_back(self):
        b = self.b
        for n in range(3):
            cols = slice(n * 256, n * 256 + 256)
            b.mixed[:, cols] = mm_nt(b.nl[...], self.slabs[0].at[3][cols, :]).astype(BF)

    def attend_back(self, p):
        b = self.b
        masks, tall = half_masks(), row_masks()
        cols = slice(p * LANES, p * LANES + LANES)
        rows = [slice(s * SEQ, s * SEQ + SEQ) for s in range(2)]
        dos = [[b.mixed[rows[s], cols] * masks[a] for a in range(2)] for s in range(2)]
        dps = [[mm_nt(b.v[rows[s], cols], dos[s][a]) for a in range(2)] for s in range(2)]
        low = [[None, None], [None, None]]
        for s in range(2):
            atts = []
            for a in range(2):
                att = b.p[s * 12 + p * 2 + a]
                atts.append(att.astype(BF))
                dp = dps[s][a]
                low[s][a] = (att * (dp - jnp.sum(att * dp, 0, keepdims=True))).astype(BF)
            b.gpre[2, rows[s], cols] = mm(jnp.concatenate(atts, 1), jnp.concatenate(dos[s], 0)).astype(BF)
        for s in range(2):
            q, kt = b.q[rows[s], cols], b.k[rows[s], cols].T
            dk = mm(jnp.concatenate(low[s], 1), jnp.concatenate([q * masks[0], q * masks[1]], 0))
            b.gpre[1, rows[s], cols] = dk.astype(BF)
            dq = mm(jnp.concatenate([kt * tall[0], kt * tall[1]], 1), jnp.concatenate(low[s], 0))
            b.gpre[0, rows[s], cols] = (dq.T * 0.125).astype(BF)

    def qkv_grads(self, start, count):
        b = self.b
        cols = slice(start, start + count)
        if count == LANES:
            both = mm(b.xt[...], jnp.concatenate([b.gpre[0, :, cols], b.gpre[1, :, cols]], 1))
            self.grads[0][0, :, cols] = both[:, :LANES].astype(BF)
            self.grads[0][1, :, cols] = both[:, LANES:].astype(BF)
        else:
            self.grads[0][0, :, cols] = mm(b.xt[...], b.gpre[0, :, cols]).astype(BF)
            self.grads[0][1, :, cols] = mm(b.xt[...], b.gpre[1, :, cols]).astype(BF)
        self.grads[0][2, :, cols] = mm(b.xt[...], b.gpre[2, :, cols]).astype(BF)
        self.gvec[VQ:VQ + 1, cols] = column_total(b.gpre[0, :, cols])
        self.gvec[VV:VV + 1, cols] = column_total(b.gpre[2, :, cols])

    def input_grad(self, n):
        b = self.b
        cols = slice(n * 256, n * 256 + 256)
        acc = b.second[:, cols]
        for j in range(3):
            acc = acc + mm_nt(b.gpre[j], self.slabs[0].at[j][cols, :])
        b.second[:, cols] = acc


BUFFERS = dict(
    q=((TOKENS, WIDTH), BF), k=((TOKENS, WIDTH), BF), v=((TOKENS, WIDTH), BF), p=((24, SEQ, SEQ), F32),
    mixed=((TOKENS, WIDTH), BF), n1=((TOKENS, WIDTH), F32), r1=((TOKENS, LANES), F32), nl=((TOKENS, WIDTH), BF),
    act=((4, TOKENS, WIDTH), BF), gp=((4, TOKENS, WIDTH), F32), second=((TOKENS, WIDTH), F32),
    gpre=((4, TOKENS, WIDTH), BF), xt=((WIDTH, TOKENS), BF), nlt=((WIDTH, TOKENS), BF),
)


START = {16: 0, 8: 16, 4: 24}
WHOLE = tuple((part, part * LANES, LANES, 0, UNIT, ORDERS[part]) for part in range(PARTS))
STRIPS = (
    ((Z1, Z3, Y1, Y3, X1), (Z1, Z3, X1, Y1, Y3), (Y1, Y3, X3, Z3, Z1)),
    ((Y1, Y3, Z1, Z3, X3), (Z1, Z3, X1, Y3, Y1), (Y1, Y3, X3, Z1, Z3)),
)
COLUMNS = ((0, 256), (256, 256), (512, LANES), (640, LANES))
CUT = tuple((part,) + COLUMNS[part] + (16 * i, 16, STRIPS[part % 2][i]) for part in range(4) for i in range(3))
CHAINS = (CUT, WHOLE, WHOLE)
FIRST = (0, 12, 18)
EVERY = ((0, 2), (0, 4), (0, 2), (0, 2))
VECTORS = "v0 v1 v2 v3".split() + "v4 v5 v6 v7".split()
SCRATCH = dict(
    wa=(SHAPES[0], BF), wb=(SHAPES[1], BF), wc=(SHAPES[2], BF), ga=(SHAPES[0], BF),
    rdb=((2, 1, 4, 2, 2, UNIT, WIDTH), BF), rdc=((4, 2, 2, 2, 1, UNIT, WIDTH), BF),
    rk=((3, 31, UNIT, WIDTH), BF), rx=((UNIT, WIDTH), BF), tall=((UNIT, WIDTH), F32),
    stage=((2, 4, 16, WIDTH), BF), final=((2, 2, 4, 16, WIDTH), BF),
    vt=((4, 2, 8, 2, LANES), F32), gv=((4, 2, 8, 2, LANES), F32),
    rv2=((3, 2, 8, 2, LANES), F32), rv1=((3, 4, 2, LANES), F32), rv0=((7, 2, LANES), F32),
    vec=((16, WIDTH), F32), gvec=((16, WIDTH), F32),
    x=((TOKENS, WIDTH), BF), qkv_in=((12, 3 * WIDTH), BF), out_in=((12, WIDTH), BF), up_in=((12, 4 * WIDTH), BF),
    **{name: ((1, 12), BF) for name in VECTORS}, v8=((1, 48), BF),
)
SEMS = dict(
    loads=(17,), mate_send=(2, 3), mate_recv=(2, 3), send=(3, PARTS, 7), recv=(3, PARTS, 7),
    sib_send=(3, PARTS), sib_recv=(3, PARTS), vsend=(9,), vrecv=(9,),
    gsib_send=(3, PARTS), gsib_recv=(3, PARTS), gsend=(24, 7), grecv=(24, 7),
    rep_send=(1,), rep_recv=(1,), gmate_send=(3, 7), gmate_recv=(3, 7), gvsend=(13,), gvrecv=(13,),
)


def box_count(box):
    return box[0][1] * box[1][1] * box[2][1] * box[3][1]


def split3(value):
    high = value.astype(BF)
    rest = value - high.astype(F32)
    mid = rest.astype(BF)
    return high, mid, (rest - mid.astype(F32)).astype(BF)


def owner_masks(block):
    d = lax.broadcasted_iota(jnp.int32, (64, WIDTH), 0)
    c = lax.broadcasted_iota(jnp.int32, (64, WIDTH), 1)
    if block is None:
        return d == (c * 43691) >> 19
    return d == 16 * block + ((c * 43691) >> 21)


def lane_picks(row):
    c = lax.broadcasted_iota(jnp.int32, (WIDTH, LANES), 0)
    lane = lax.broadcasted_iota(jnp.int32, (WIDTH, LANES), 1)
    if row is None:
        return (lane == c - 48 * ((c * 43691) >> 21)).astype(F32).astype(BF)
    return (lane == 12 * row + c - 12 * ((c * 43691) >> 19)).astype(F32).astype(BF)


def mega_kernel(lengths, *refs):
    vecs_in, (qkv_in, out_in, up_in, down_in, x_in, og_in,
               enc_out, sgrad_out, oqkv, oout, oup, odown, ovec), scratch = refs[:9], refs[9:22], refs[22:]
    r = b = types.SimpleNamespace(**dict(zip([*SCRATCH, *BUFFERS, *SEMS], scratch)))
    here = position()
    me = member_of(here)
    sibling = hop(here, CORE)
    twin = hop(here, X2)
    weights = (r.wa, r.wb, r.wc)
    grads = (r.ga, r.wb, r.wc)
    rds = (r.act.at[pl.ds(0, 3)].reshape((2, 1, 4, 2, 2, UNIT, WIDTH)), r.rdb, r.rdc)
    slabs = [w.reshape(4, WIDTH, WIDTH) for w in weights]
    gslabs = [w.reshape(4, WIDTH, WIDTH) for w in grads]
    layer = Layer(slabs, gslabs, r.vec, lengths, r.x, r.x, r.x, r.gvec, b)

    def own_at(phase):
        ylow, z, x, yhigh = (s for s, n in own_box(here))
        return (ylow, here.core, z, x, yhigh) if phase < 2 else (z, x, yhigh, ylow, here.core)

    def mate_copy(which, k):
        mate = mates(here)[k]
        return remote(r.stage.at[which, member_of(mate)], r.final.at[which, 0, me],
                      r.mate_send.at[which, k], r.mate_recv.at[which, k], mate)

    def assemble(which):
        for k in range(3):
            mate_copy(which, k).wait()
        r.final[which, 0, me] = r.stage[which, me]
        for i in range(4):
            r.tall[12 * i:12 * i + 12, :] = r.final[which, 0, i, 0:12, :].astype(F32)
        weights[which][own_at(which)] = r.tall[...].astype(BF)

    def push(phase, part, found, slot, there):
        w = weights[phase]
        for box in found:
            view = w.at[slices(phase, here.core, box, part)]
            remote(view, view, r.send.at[phase, part, slot], r.recv.at[phase, part, slot], there).start()

    def share(phase, part, found):
        w = weights[phase]
        for box in found:
            view = w.at[slices(phase, here.core, box, part)]
            remote(view, view, r.sib_send.at[phase, part], r.sib_recv.at[phase, part], sibling).start()

    def gather_first(phase):
        for part in range(PARTS):
            for slot, there in enumerate(trio(here, ORDERS[part])):
                push(phase, part, boxes(here, ()), slot, there)

    def gather(phase, step):
        w = weights[phase]
        for part in range(PARTS):
            order = ORDERS[part]
            if step == 2:
                for slot in range(3):
                    wait_units(w, phase, 1, part, r.recv.at[phase, part, slot])
            else:
                wait_units(w, phase, 1 << (step - 1), part, r.recv.at[phase, part, step])
            there = hop(here, order[step])
            if step < 4:
                push(phase, part, boxes(here, order[:step]), step + 1, there)
            else:
                for half, found in enumerate(halves(boxes(here, order[:4]))):
                    push(phase, part, found, 5 + half, there)
                share(phase, part, boxes(here, order[:4]))

    def gather_last(phase, half):
        for part in range(PARTS):
            order = ORDERS[part]
            wait_units(weights[phase], phase, 8, part, r.recv.at[phase, part, 5 + half])
            share(phase, part, halves(boxes(hop(here, order[4]), order[:4]))[half])

    def gathered(phase, parts=range(PARTS)):
        for part in parts:
            wait_units(weights[phase], phase, 32, part, r.sib_recv.at[phase, part])

    def gather_sent(phase):
        for part in range(PARTS):
            wait_units(weights[phase], phase, 32, part, r.sib_send.at[phase, part])
            for slot, n in enumerate((1, 1, 1, 4, 8, 8, 8)):
                wait_units(weights[phase], phase, n, part, r.send.at[phase, part, slot])

    def vec_tile(place):
        return (place.z, place.x % 2, place.y * 2 + place.core)

    def vec_pair(place):
        return (place.z, place.x % 2, pl.ds(place.y // 2 * 4, 4))

    def vec_ring(place):
        return (pl.ds(place.z // 2 * 2, 2), place.x % 2)

    def vec_peers(k):
        return (mates(here), trio(here, (Y3, Z1)), trio(here, (Z3, X1)))[k]

    def vec_copies(k):
        view = r.vt.at[(vec_tile, vec_pair, vec_ring)[k](here)]
        return [remote(view, view, r.vsend.at[3 * k + i], r.vrecv.at[3 * k + i], there) for i, there in enumerate(vec_peers(k))]

    def vec_start(k):
        for copy in vec_copies(k):
            copy.start()

    def vec_wait(k):
        for copy in vec_copies(k):
            copy.wait()

    def expand():
        first = r.vt[:, :, :, 0, :].reshape(64, LANES)
        second = r.vt[:, :, :, 1, :].reshape(64, LANES).astype(BF)
        mask = owner_masks(None)
        turned = [first] + [pltpu.roll(first, LANES - 12 * row, 1) for row in range(1, 8)]
        t = mm_nt(jnp.concatenate(turned, 0).astype(BF), lane_picks(0)).reshape(8, 64, WIDTH)
        for row in range(8):
            r.vec[row:row + 1, :] = jnp.sum(jnp.where(mask, t[row], 0.0), 0, keepdims=True)
        t = mm_nt(second, lane_picks(None))
        for j in range(4):
            r.vec[8 + j:9 + j, :] = jnp.sum(jnp.where(owner_masks(j), t, 0.0), 0, keepdims=True)

    def sib_copy(phase, k):
        g, rd = grads[phase], rds[phase]
        if phase == 0:
            cols = pl.ds(*COLUMNS[k])
            src = g.at[:, pl.ds(sibling.core, 1), :, :, :, :, cols]
            dst = rd.at[:, :, :, :, :, :, cols]
        elif phase == 1:
            src, dst = g.at[k, sibling.core], rd.at[k, 0]
        else:
            src, dst = g.at[k, :, :, :, pl.ds(sibling.core, 1)], rd.at[k]
        return remote(src, dst, r.gsib_send.at[phase, k], r.gsib_recv.at[phase, k], sibling)

    def sib_add(phase, k):
        sib_copy(phase, k).wait()
        g, rd = grads[phase], rds[phase]
        for i in range(4):
            if phase == 0:
                cols = slice(COLUMNS[k][0], sum(COLUMNS[k]))
                at = (slice(None), pl.ds(here.core, 1), i, slice(None), slice(None), slice(None), cols)
                g[at] = g[at] + rd[:, :, i, :, :, :, cols]
            elif phase == 1:
                g[k, here.core, i] = g[k, here.core, i] + rd[k, 0, i]
            else:
                at = (k, i // 2, i % 2, slice(None), pl.ds(here.core, 1))
                g[at] = g[at] + rd[k, i // 2, i % 2]

    def unit_slices(phase, box, chain):
        _, col, cols, row, rows, _ = chain
        return slices(phase, here.core, box, 0)[:5] + (slice(row, row + rows), slice(col, col + cols))

    def hop_start(phase, c, step):
        chain = CHAINS[phase][c]
        _, col, cols, row, rows, order = chain

        def send(box, at, slot, there):
            n = box_count(box)
            src = grads[phase].at[slices(phase, here.core, box, 0)[:5]]
            dst = r.rk.at[phase, pl.ds(at, n)].reshape(src.shape)
            at5 = (slice(None),) * 5 + (pl.ds(row, rows), pl.ds(col, cols))
            remote(src.at[at5], dst.at[at5], r.gsend.at[FIRST[phase] + c, slot], r.grecv.at[FIRST[phase] + c, slot], there).start()
            return at + n

        if step == 1:
            for slot, there in enumerate(trio(here, order)):
                send(boxes(there, ())[0], 28 + slot, slot, there)
            return
        if phase == 0 and step == 3:
            for i, there in enumerate(trio(here, order[2:])):
                at = 16 + 4 * i
                for box in boxes(there, order[:2]):
                    at = send(box, at, 3 + i, there)
            return
        there = hop(here, order[step])
        at = START[1 << step]
        for box in boxes(there, order[:step]):
            at = send(box, at, step + 2, there)

    def landing(phase, c, at, n):
        _, col, cols, row, rows, _ = CHAINS[phase][c]
        return r.rk.at[phase, pl.ds(at, n), pl.ds(row, rows), pl.ds(col, cols)]

    def hop_add(phase, c, step):
        g = grads[phase]
        chain = CHAINS[phase][c]
        if step == 1:
            where = unit_slices(phase, boxes(here, ())[0], chain)
            total = g[where].astype(F32)
            for slot in range(3):
                view = landing(phase, c, 28 + slot, 1)
                pltpu.make_async_copy(view, view, r.grecv.at[FIRST[phase] + c, slot]).wait()
                total = total + view[...].astype(F32).reshape(total.shape)
            g[where] = total.astype(BF)
            return
        if phase == 0 and step == 3:
            for i in range(3):
                view = landing(phase, c, 16 + 4 * i, 4)
                pltpu.make_async_copy(view, view, r.grecv.at[FIRST[phase] + c, 3 + i]).wait()
            at = 16
            for box in boxes(here, chain[5][:2]):
                m = box_count(box)
                where = unit_slices(phase, box, chain)
                total = g[where].astype(F32)
                for i in range(3):
                    total = total + landing(phase, c, at + 4 * i, m)[...].astype(F32).reshape(total.shape)
                g[where] = total.astype(BF)
                at += m
            return
        n = 1 << step
        at = START[n]
        view = landing(phase, c, at, n)
        pltpu.make_async_copy(view, view, r.grecv.at[FIRST[phase] + c, step + 2]).wait()
        for box in boxes(here, chain[5][:step]):
            m = box_count(box)
            where = unit_slices(phase, box, chain)
            old = g[where]
            g[where] = old + landing(phase, c, at, m)[...].reshape(old.shape)
            at += m

    def rep_copy():
        return remote(grads[2].at[own_at(2)], r.rx, r.rep_send.at[0], r.rep_recv.at[0], twin)

    def reduce_first(phase):
        for k in range(2 if phase == 1 else 4):
            sib_add(phase, k)
        for part in range(PARTS):
            hop_start(phase, part, 4)

    def move(phase, c, step):
        hop_add(phase, c, step)
        if step > 1:
            hop_start(phase, c, 1 if phase == 0 and step == 3 else step - 1)

    def reduce(phase, step):
        for part in range(PARTS):
            move(phase, part, step)

    def first_part(part):
        sib_add(0, part)
        for c, chain in enumerate(CUT):
            if chain[0] == part:
                hop_start(0, c, 4)

    def move_part(part, step):
        for c, chain in enumerate(CUT):
            if chain[0] == part:
                move(0, c, step)

    def gmate_copy(which, k):
        others = mates(here)
        there = (others + [twin] + [hop(mate, X2) for mate in others])[k]
        cols = (pl.ds(0, 512), pl.ds(0, WIDTH), pl.ds(512, 256))[which]
        phase = which % 2
        return remote(r.stage.at[phase, member_of(there), :, cols], r.final.at[phase, k // 3 if k < 6 else 1, me, :, cols],
                      r.gmate_send.at[which, k], r.gmate_recv.at[which, k], there)

    def hand_over(which):
        phase = which % 2
        cols = (slice(0, 512), slice(0, WIDTH), slice(512, WIDTH))[which]
        r.tall[:, cols] = grads[phase][own_at(phase) + (slice(None), cols)].astype(F32)
        for i in range(4):
            r.stage[phase, i, 0:12, cols] = r.tall[12 * i:12 * i + 12, cols].astype(BF)
        for k in range(7):
            gmate_copy(which, k).start()

    def deliver(which):
        phase = which % 2
        cols = (slice(0, 512), slice(0, WIDTH), slice(512, WIDTH))[which]
        for k in range(7):
            gmate_copy(which, k).wait()
        r.final[phase, 0, me, :, cols] = r.stage[phase, me, :, cols]
        for i in range(4):
            at = slice(i * WIDTH + cols.start, i * WIDTH + cols.stop)
            dst = oup.at[:, at] if phase else (oqkv.at[:, at] if i < 3 else oout.at[:, cols])
            dst[...] = r.final[phase, 0, i, 0:12, cols].astype(F32) + r.final[phase, 1, i, 0:12, cols].astype(F32)

    def deliver_down():
        rep_copy().wait()
        odown[...] = grads[2][own_at(2)].astype(F32) + r.rx[...].astype(F32)

    def reduce_sent(phase):
        for c in range(len(CHAINS[phase])):
            for slot, n in enumerate((1, 1, 1, 4, 4, 4, 16) if phase == 0 else (1, 1, 1, 0, 4, 8, 16)):
                if n == 0:
                    continue
                view = landing(phase, c, 0, n)
                pltpu.make_async_copy(view, view, r.gsend.at[FIRST[phase] + c, slot]).wait()

    def pack_rows(first, count):
        mask = owner_masks(None).astype(F32).astype(BF)
        pieces = split3(r.gvec[first:first + count, :])
        spread = [piece[i:i + 1, :] * mask for piece in pieces for i in range(count)]
        out = mm(jnp.concatenate(spread, 0), lane_picks(0)).reshape(3, count, 64, LANES)
        out = out[0] + out[1] + out[2]
        total = out[0] if first == 0 else pltpu.roll(out[0], 12 * first, 1)
        for i in range(1, count):
            total = total + pltpu.roll(out[i], 12 * (first + i), 1)
        return total.reshape(4, 2, 8, LANES)

    def pack():
        pieces = split3(r.gvec[8:12, :])
        masks = [owner_masks(j).astype(F32).astype(BF) for j in range(4)]
        spread = [piece[j:j + 1, :] * masks[j] for piece in pieces for j in range(4)]
        out = mm(jnp.concatenate(spread, 0), lane_picks(None)).reshape(12, 64, LANES)
        r.gv[:, :, :, 0, :] = pack_rows(2, 6)
        r.gv[:, :, :, 1, :] = jnp.sum(out, 0).reshape(4, 2, 8, LANES)

    def gvec_copies(k):
        if k == 0:
            peers = mates(here) + [twin] + [hop(mate, X2) for mate in mates(here)]
        else:
            peers = vec_peers(k)
        part, landing_ref = ((vec_tile, r.rv0), (vec_pair, r.rv1), (vec_ring, r.rv2))[k]
        base = (6, 3, 0)[k]
        return [remote(r.gv.at[part(there)], landing_ref.at[i], r.gvsend.at[base + i], r.gvrecv.at[base + i], there)
                for i, there in enumerate(peers)]

    def gvec_start(k):
        for copy in gvec_copies(k):
            copy.start()

    def gvec_add(k):
        part, landing_ref = ((vec_tile, r.rv0), (vec_pair, r.rv1), (vec_ring, r.rv2))[k]
        at = part(here)
        total = r.gv[at]
        for i, copy in enumerate(gvec_copies(k)):
            copy.wait()
            total = total + landing_ref[i].reshape(total.shape)
        r.gv[at] = total

    near = [hop(here, link) for link in (Y1, Y3, Z1, Z3, X1, X3, CORE, X2, Y2, Z2)]
    near += [mates(here)[2], hop(hop(here, Y3), Z1), hop(hop(here, Y1), Z3)]
    near += [hop(mate, X2) for mate in mates(here)]
    near += [hop(hop(here, a), c) for a, c in ((Z3, X1), (X1, Y1), (X1, Y3), (X3, Z1), (X3, Z3))]
    loads = [pltpu.make_async_copy(src, dst, r.loads.at[i]) for i, (src, dst) in enumerate((
        (qkv_in, r.qkv_in), (out_in, r.out_in), (up_in, r.up_in), (down_in, weights[2].at[own_at(2)]), (x_in, r.x)))]
    held = [getattr(r, name) for name in VECTORS] + [r.v8]
    vec_loads = [pltpu.make_async_copy(src, dst, r.loads.at[8 + i]) for i, (src, dst) in enumerate(zip(vecs_in, held))]
    for load in loads[:4] + vec_loads + loads[4:]:
        load.start()
    barrier = pltpu.get_barrier_semaphore()
    for place in near:
        pl.semaphore_signal(barrier, inc=1, device_id=device_of(place), device_id_type=MESH)
    og_load = pltpu.make_async_copy(og_in, r.x, r.loads.at[5])
    own = vec_tile(here)
    r.vt[own] = jnp.zeros((2, LANES), F32)
    for load in loads[:4] + vec_loads:
        load.wait()
    for i in range(8):
        r.vt[own + (slice(0, 1), slice(12 * i, 12 * i + 12))] = held[i][...].astype(F32)
    r.vt[own + (slice(1, 2), slice(0, 48))] = held[8][...].astype(F32)
    for i in range(4):
        r.stage[0, i, 0:12, :] = r.qkv_in[:, i * WIDTH:(i + 1) * WIDTH] if i < 3 else r.out_in[...]
        r.stage[1, i, 0:12, :] = r.up_in[:, i * WIDTH:(i + 1) * WIDTH]
    pl.semaphore_wait(barrier, len(near))
    for k in range(3):
        mate_copy(0, k).start()
    vec_start(0)
    for k in range(3):
        mate_copy(1, k).start()
    gather_first(2)
    assemble(0)
    vec_wait(0)
    vec_start(1)
    gather_first(0)
    assemble(1)
    gather_first(1)
    loads[4].wait()
    b.xt[...] = r.x[...].T
    vec_wait(1)
    vec_start(2)
    gather(0, 2)
    gather(2, 2)
    gather(1, 2)
    gather(0, 3)
    vec_wait(2)
    expand()
    gather(0, 4)
    gather(1, 3)
    gather(2, 3)
    gather_last(0, 0)
    gather_last(0, 1)
    for n in range(3):
        gathered(0, (2 * n, 2 * n + 1))
        layer.project(n)
        if n == 0:
            gather(1, 4)
    gather(2, 4)
    layer.attend()
    gather_last(1, 0)
    gather_last(1, 1)
    layer.attn_out()
    og_load.start()
    b.nlt[...] = b.nl[...].T
    gather_last(2, 0)
    gather_last(2, 1)
    gathered(1)
    layer.feed()
    og_load.wait()
    gathered(2)
    layer.feed_out()
    enc_store = pltpu.make_async_copy(r.x, enc_out, r.loads.at[6])
    enc_store.start()
    gather_sent(2)

    def down_body(j, _):
        layer.feed_back(j)
        layer.down_grads(j)
        sib_copy(2, j).start()
        return 0

    lax.fori_loop(0, 4, down_body, 0)
    for n in range(3):
        layer.norm1_back(n)
    reduce_first(2)
    gather_sent(1)

    def up_body(i, _):
        layer.up_grads(i * 2 + sibling.core)
        sib_copy(1, i).start()
        return 0

    def up_own(i, _):
        layer.up_grads(i * 2 + here.core)
        return 0

    lax.fori_loop(0, 2, up_body, 0)
    lax.fori_loop(0, 2, up_own, 0)
    layer.norm1_rows()
    layer.out_grads()
    reduce(2, 4)
    reduce_first(1)
    layer.out_back()
    pack()
    layer.attend_back(0)
    layer.attend_back(1)
    layer.qkv_grads(*COLUMNS[0])
    sib_copy(0, 0).start()
    reduce(2, 3)
    layer.attend_back(2)
    first_part(0)
    layer.attend_back(3)
    layer.qkv_grads(*COLUMNS[1])
    sib_copy(0, 1).start()
    reduce(1, 4)
    layer.attend_back(4)
    layer.qkv_grads(*COLUMNS[2])
    sib_copy(0, 2).start()
    first_part(1)
    move_part(0, 4)
    reduce(2, 2)
    layer.attend_back(5)
    layer.qkv_grads(*COLUMNS[3])
    sib_copy(0, 3).start()
    first_part(2)
    reduce(1, 3)
    layer.input_grad(0)
    layer.input_grad(1)
    first_part(3)
    r.gv[:, :, :, 0, :] = r.gv[:, :, :, 0, :] + pack_rows(VQ, 2)
    gvec_start(2)
    move_part(1, 4)
    move_part(0, 3)
    layer.input_grad(2)
    sgrad_store = pltpu.make_async_copy(b.second, sgrad_out, r.loads.at[7])
    sgrad_store.start()
    reduce(1, 2)
    move_part(2, 4)
    gvec_add(2)
    gvec_start(1)
    reduce(2, 1)
    rep_copy().start()
    move_part(3, 4)
    reduce(1, 1)
    hand_over(1)
    move_part(0, 1)
    move_part(1, 3)
    move_part(2, 3)
    gvec_add(1)
    gvec_start(0)
    move_part(3, 3)
    deliver_down()
    move_part(1, 1)
    hand_over(0)
    move_part(2, 1)
    move_part(3, 1)
    hand_over(2)
    deliver(1)
    gvec_add(0)
    ovec[...] = r.gv[vec_tile(here)]
    for phase in range(1, 3):
        reduce_sent(phase)
    gather_sent(0)
    reduce_sent(0)
    enc_store.wait()
    sgrad_store.wait()
    deliver(0)
    deliver(2)


def run_layer(lengths, vecs, qkv, out, up, down, x, og):
    vm = pl.BlockSpec(memory_space=pltpu.VMEM)
    hb = pl.BlockSpec(memory_space=pl.ANY)
    return pl.pallas_call(
        mega_kernel,
        out_shape=[
            jax.ShapeDtypeStruct((TOKENS, WIDTH), BF), jax.ShapeDtypeStruct((TOKENS, WIDTH), F32),
            jax.ShapeDtypeStruct((12, 3 * WIDTH), F32), jax.ShapeDtypeStruct((12, WIDTH), F32),
            jax.ShapeDtypeStruct((12, 4 * WIDTH), F32), jax.ShapeDtypeStruct((UNIT, WIDTH), F32), jax.ShapeDtypeStruct((2, LANES), F32),
        ],
        in_specs=[pl.BlockSpec(memory_space=pltpu.SMEM)] + [hb] * 15,
        out_specs=[hb, hb] + [vm] * 5,
        scratch_shapes=[pltpu.VMEM(s, d) for s, d in SCRATCH.values()] + [pltpu.VMEM(s, d) for s, d in BUFFERS.values()]
        + [pltpu.SemaphoreType.DMA(s) for s in SEMS.values()],
        compiler_params=pltpu.CompilerParams(collective_id=1, has_side_effects=True, vmem_limit_bytes=63 * 2**20),
    )(lengths, *vecs, qkv, out, up, down, x, og)


def finish_kernel(*refs):
    srcs, dsts, vec_outs, held, parts, sems = refs[:7], refs[7:13], refs[13:22], refs[22:29], refs[29:38], refs[38]
    loads = [pltpu.make_async_copy(src, mid, sems.at[0, i]) for i, (src, mid) in enumerate(zip(srcs, held))]
    stores = [pltpu.make_async_copy(mid, dst, sems.at[1, i]) for i, (mid, dst) in enumerate(zip(held, dsts))]
    vec_stores = [pltpu.make_async_copy(mid, dst, sems.at[1, 6 + i]) for i, (mid, dst) in enumerate(zip(parts, vec_outs))]
    for load in loads[::-1]:
        load.start()
    loads[6].wait()
    vec = held[6]
    for i in range(8):
        parts[i][...] = vec[0:1, 12 * i:12 * i + 12]
    parts[8][...] = vec[1:2, 0:48]
    for store in vec_stores:
        store.start()
    for load, store in list(zip(loads, stores))[::-1]:
        load.wait()
        store.start()
    for store in vec_stores + stores:
        store.wait()


def finish(results):
    hb = pl.BlockSpec(memory_space=pl.ANY)
    small = [(1, n) for n in [12] * 8 + [48]]
    return pl.pallas_call(
        finish_kernel,
        out_shape=[jax.ShapeDtypeStruct(a.shape, a.dtype) for a in results[:6]] + [jax.ShapeDtypeStruct(n, F32) for n in small],
        in_specs=[hb] * 7,
        out_specs=[hb] * 15,
        scratch_shapes=[pltpu.VMEM(a.shape, a.dtype) for a in results] + [pltpu.VMEM(n, F32) for n in small]
        + [pltpu.SemaphoreType.DMA((2, 15))],
        compiler_params=pltpu.CompilerParams(vmem_limit_bytes=63 * 2**20),
    )(*results)


def local(states, qkv_weight, query_bias, value_bias, out_weight, out_bias, attn_gain, attn_shift, up_weight, up_bias,
          down_weight, down_bias, ffn_gain, ffn_shift, out_grad, lengths):
    vecs = [v.reshape(1, -1) for v in (query_bias, value_bias, out_bias, attn_gain, attn_shift, down_bias, ffn_gain, ffn_shift, up_bias)]
    results = run_layer(
        lengths.reshape(1, 2), vecs, qkv_weight, out_weight, up_weight, down_weight,
        states.reshape(TOKENS, WIDTH), out_grad.reshape(TOKENS, WIDTH))
    enc, sgrad, oqkv, oout, oup, odown, *o = finish(results)
    o = [v.reshape(-1) for v in o]
    return (enc.reshape(states.shape), sgrad.reshape(states.shape), oqkv, o[0], o[1], oout, o[2], o[3], o[4],
            oup, o[8], odown, o[5], o[6], o[7])


def solution(mesh):
    return jax.shard_map(
        local,
        mesh=mesh,
        in_specs=(
            P(None, ("dp", "rep"), None, None),
            P("dp", None),
            P("dp"),
            P("dp"),
            P("dp", None),
            P("dp"),
            P("dp"),
            P("dp"),
            P("dp", None),
            P("dp"),
            P("dp", None),
            P("dp"),
            P("dp"),
            P("dp"),
            P(None, ("dp", "rep"), None, None),
            P(None, ("dp", "rep")),
        ),
        out_specs=(
            P(None, ("dp", "rep"), None, None),
            P(None, ("dp", "rep"), None, None),
            P("dp", None),
            P("dp"),
            P("dp"),
            P("dp", None),
            P("dp"),
            P("dp"),
            P("dp"),
            P("dp", None),
            P("dp"),
            P("dp", None),
            P("dp"),
            P("dp"),
            P("dp"),
        ),
        check_vma=False,
    )
```

```python
import collections
import math
import types

import jax
import jax.numpy as jnp
from jax import lax
from jax.experimental import pallas as pl
from jax.experimental.pallas import tpu as pltpu
from jax.sharding import PartitionSpec as P

Place = collections.namedtuple("Place", "core y z x")
MESH = pl.DeviceIdType.MESH
BF = jnp.bfloat16
F32 = jnp.float32
WIDTH = 768
UNIT = 48
LANES = 128
PARTS = 6

CORE, Y1, Y3, Z1, Z3, X1, X2, X3 = (0, 0), (1, 1), (1, 3), (2, 1), (2, 3), (3, 1), (3, 2), (3, 3)
Y2, Z2 = (1, 2), (2, 2)

ORDERS = (
    (Z1, Z3, Y1, Y3, X1),
    (Y1, Y3, Z1, Z3, X3),
    (Y3, Z1, Z3, X1, Y1),
    (Y1, Z3, X1, Z1, Y3),
    (Y1, Z3, X3, Y3, Z1),
    (Z1, Y3, X3, Y1, Z3),
)


def position():
    dp = lax.axis_index("dp")
    rep = lax.axis_index("rep")
    return Place(dp % 2, (dp // 2) % 4, dp // 16, rep * 2 + (dp // 8) % 2)


def device_of(place):
    dp = ((place.z * 2 + place.x % 2) * 4 + place.y) * 2 + place.core
    return (dp, place.x // 2)


def hop(place, link):
    axis, how = link
    p = place[axis]
    moved = (1 - p, p + 1 - 2 * (p % 2), (p + 2) % 4, 3 - p)[how]
    return Place(*(moved if i == axis else q for i, q in enumerate(place)))


def boxes(place, links):
    y, z, x = place.y, place.z, place.x % 2
    if Y1 in links and Y3 in links:
        ys = [((0, 2), (0, 2))]
    elif Y1 in links:
        ys = [((0, 2), (y // 2, 1))]
    elif Y3 in links:
        ys = [((y % 2, 1), (y // 2, 1)), ((1 - y % 2, 1), (1 - y // 2, 1))]
    else:
        ys = [((y % 2, 1), (y // 2, 1))]
    if Z1 in links and Z3 in links:
        zs = [(0, 4)]
    elif Z1 in links:
        zs = [((z // 2) * 2, 2)]
    elif Z3 in links:
        zs = [(z, 1), (3 - z, 1)]
    else:
        zs = [(z, 1)]
    xs = (0, 2) if X1 in links or X3 in links else (x, 1)
    return [(ylow, zz, xs, yhigh) for (ylow, yhigh) in ys for zz in zs]


def slices(phase, core, box, part):
    ylow, z, x, yhigh = (pl.ds(*s) for s in box)
    cols = pl.ds(part * LANES, LANES)
    if phase < 2:
        return (ylow, pl.ds(core, 1), z, x, yhigh, slice(None), cols)
    return (z, x, yhigh, ylow, pl.ds(core, 1), slice(None), cols)


SHAPES = (
    (2, 2, 4, 2, 2, UNIT, WIDTH),
    (2, 2, 4, 2, 2, UNIT, WIDTH),
    (4, 2, 2, 2, 2, UNIT, WIDTH),
)


def size_box(count):
    sizes = {1: (1, 1, 1, 1), 2: (1, 1, 1, 2), 4: (1, 1, 2, 2), 8: (1, 2, 2, 2), 16: (1, 4, 2, 2), 32: (2, 4, 2, 2)}[count]
    return tuple((0, n) for n in sizes)


def wait_units(ref, phase, count, part, sem):
    view = ref.at[slices(phase, 0, size_box(count), part)]
    pltpu.make_async_copy(view, view, sem).wait()


def remote(src, dst, send_sem, recv_sem, place):
    return pltpu.make_async_remote_copy(
        src_ref=src, dst_ref=dst, send_sem=send_sem, recv_sem=recv_sem,
        device_id=device_of(place), device_id_type=MESH,
    )


def greet(places):
    barrier = pltpu.get_barrier_semaphore()
    for place in places:
        pl.semaphore_signal(barrier, inc=1, device_id=device_of(place), device_id_type=MESH)
    pl.semaphore_wait(barrier, len(places))


def member_of(place):
    return (place.y % 2) * 2 + place.core


def mates(here):
    return [hop(here, CORE), hop(here, Y1), hop(hop(here, CORE), Y1)]


def own_box(here):
    return boxes(here, ())[0]


def trio(place, order):
    a, b = hop(place, order[0]), hop(place, order[1])
    return a, b, hop(a, order[1])


def halves(found):
    if len(found) == 2:
        return [found[:1], found[1:]]
    ylow, (start, n), x, yhigh = found[0]
    return [[(ylow, (start, n // 2), x, yhigh)], [(ylow, (start + n // 2, n // 2), x, yhigh)]]


HALF = 256
SEQ = 256
TOKENS = 512
ROWS = 128
epsilon = 1e-05
NT = (((1,), (1,)), ((), ()))
TN = (((0,), (0,)), ((), ()))
VQ, VV, VO, VAG, VAS, VD, VFG, VFS, VUP = range(9)


def mm(left, right):
    return jnp.dot(left, right, preferred_element_type=F32)


def mm_nt(left, right):
    return lax.dot_general(left, right, NT, preferred_element_type=F32)


def mm_tn(left, right):
    return lax.dot_general(left, right, TN, preferred_element_type=F32)


def normalise(value):
    center = value - jnp.mean(value, -1, keepdims=True)
    scale = lax.rsqrt(jnp.mean(center * center, -1, keepdims=True) + epsilon)
    return center * scale, scale


def norm_back(cot, gain, n, scale):
    e = cot * gain
    return scale * (e - jnp.mean(e, -1, keepdims=True) - n * jnp.mean(e * n, -1, keepdims=True))


def half_masks():
    lane = lax.broadcasted_iota(jnp.int32, (1, LANES), 1)
    low = (lane < 64).astype(F32).astype(BF)
    return low, (1.0 - low.astype(F32)).astype(BF)


def row_masks():
    row = lax.broadcasted_iota(jnp.int32, (LANES, SEQ), 0)
    low = (row < 64).astype(F32).astype(BF)
    return low, (1.0 - low.astype(F32)).astype(BF)


def column_total(ref_rows):
    return jnp.sum(ref_rows.astype(F32), 0, keepdims=True)


class Layer:
    def __init__(self, slabs, grads, vec, lengths, x, og, enc, gvec, b):
        self.slabs, self.grads, self.vec, self.lengths, self.x, self.og = slabs, grads, vec, lengths, x, og
        self.enc, self.gvec, self.b = enc, gvec, b

    def v(self, row):
        return self.vec[row:row + 1, :]

    def project(self, n):
        b = self.b
        cols = slice(n * 256, n * 256 + 256)
        x = self.x[...]
        b.q[:, cols] = ((mm(x, self.slabs[0].at[0][:, cols]) + self.vec[VQ:VQ + 1, cols]).astype(BF).astype(F32) * 0.125).astype(BF)
        b.k[:, cols] = mm(x, self.slabs[0].at[1][:, cols]).astype(BF)
        b.v[:, cols] = (mm(x, self.slabs[0].at[2][:, cols]) + self.vec[VV:VV + 1, cols]).astype(BF)

    def attend(self):
        b = self.b
        masks, tall = half_masks(), row_masks()
        key = lax.broadcasted_iota(jnp.int32, (SEQ, SEQ), 0)

        def body(p, _):
            cols = pl.ds(pl.multiple_of(p * LANES, LANES), LANES)
            rows = [slice(s * SEQ, s * SEQ + SEQ) for s in range(2)]
            scores = [[mm_nt(b.k[rows[s], cols] * masks[a], b.q[rows[s], cols]) for a in range(2)] for s in range(2)]
            low = [[None, None], [None, None]]
            for s in range(2):
                length = self.lengths[0, s]
                for a in range(2):
                    st = jnp.where(key < length, scores[s][a], -1e9)
                    e = jnp.exp(st - jnp.max(st, 0, keepdims=True))
                    att = e * (1.0 / jnp.sum(e, 0, keepdims=True))
                    b.p[s * 12 + p * 2 + a] = att
                    low[s][a] = att.astype(BF)
            for s in range(2):
                vt = b.v[rows[s], cols].T
                out = mm(jnp.concatenate([vt * tall[0], vt * tall[1]], 1), jnp.concatenate(low[s], 0))
                b.mixed[rows[s], cols] = out.T.astype(BF)
            return 0

        lax.fori_loop(0, 6, body, 0)

    def attn_out(self):
        b = self.b
        for n in range(3):
            cols = slice(n * 256, n * 256 + 256)
            acc = mm(b.mixed[...], self.slabs[0].at[3][:, cols]) + self.vec[VO:VO + 1, cols]
            b.n1[:, cols] = self.x[:, cols].astype(F32) + acc

        def body(r, _):
            rows = pl.ds(pl.multiple_of(r * ROWS, ROWS), ROWS)
            n, scale = normalise(b.n1[rows, :])
            b.n1[rows, :] = n
            b.r1[rows, :] = jnp.broadcast_to(scale, (ROWS, LANES))
            b.nl[rows, :] = (n * self.v(VAG) + self.v(VAS)).astype(BF)
            return 0

        lax.fori_loop(0, TOKENS // ROWS, body, 0)

    def feed(self):
        b = self.b

        def body(j, _):
            w = self.slabs[1].at[j]
            for n in range(3):
                cols = slice(n * 256, n * 256 + 256)
                bias = self.vec[pl.ds(VUP + j, 1), cols]
                for h in range(2):
                    rows = slice(h * 256, h * 256 + 256)
                    pre = mm(b.nl[rows, :], w[:, cols]) + bias
                    cdf = 0.5 * (1.0 + lax.erf(pre * (1.0 / math.sqrt(2.0))))
                    pdf = jnp.exp(pre * pre * -0.5) * (1.0 / math.sqrt(2.0 * math.pi))
                    b.act[j, rows, cols] = (pre * cdf).astype(BF)
                    b.gp[j, rows, cols] = cdf + pre * pdf
            return 0

        lax.fori_loop(0, 4, body, 0)

    def feed_out(self):
        b = self.b
        for n in range(3):
            cols = slice(n * 256, n * 256 + 256)
            acc = self.b.n1[:, cols] * self.vec[VAG:VAG + 1, cols] + self.vec[VAS:VAS + 1, cols] + self.vec[VD:VD + 1, cols]
            for j in range(4):
                acc = acc + mm(b.act[j], self.slabs[2].at[j][:, cols])
            b.second[:, cols] = acc

        def body(r, sums):
            rows = pl.ds(pl.multiple_of(r * ROWS, ROWS), ROWS)
            n, scale = normalise(b.second[rows, :])
            c = self.og[rows, :].astype(F32)
            self.enc[rows, :] = (n * self.v(VFG) + self.v(VFS)).astype(BF)
            g = norm_back(c, self.v(VFG), n, scale)
            b.second[rows, :] = g
            low = g.astype(BF)
            b.nl[rows, :] = low
            return sums[0] + column_total(c * n), sums[1] + column_total(c), sums[2] + column_total(low)

        zero = jnp.zeros((1, WIDTH), F32)
        sums = lax.fori_loop(0, TOKENS // ROWS, body, (zero, zero, zero))
        self.gvec[VFG:VFG + 1, :], self.gvec[VFS:VFS + 1, :], self.gvec[VD:VD + 1, :] = sums

    def down_grads(self, j):
        b = self.b
        left = b.act[j].T
        for n in range(3):
            cols = slice(n * 256, n * 256 + 256)
            self.grads[2][j, :, cols] = mm(left, b.nl[:, cols]).astype(BF)

    def feed_back(self, j):
        b = self.b
        w = self.slabs[2].at[j]
        for n in range(3):
            cols = slice(n * 256, n * 256 + 256)
            total = jnp.zeros((1, 256), F32)
            for h in range(2):
                rows = slice(h * 256, h * 256 + 256)
                acc = mm_nt(b.nl[rows, :], w[cols, :])
                low = (acc * b.gp[j, rows, cols]).astype(BF)
                b.gpre[j, rows, cols] = low
                total = total + column_total(low)
            self.gvec[pl.ds(VUP + j, 1), cols] = total

    def up_grads(self, j):
        b = self.b
        for n in range(3):
            cols = slice(n * 256, n * 256 + 256)
            self.grads[1][j, :, cols] = mm(b.nlt[...], b.gpre[j, :, cols]).astype(BF)

    def norm1_back(self, n):
        b = self.b
        cols = slice(n * 256, n * 256 + 256)
        acc = b.second[:, cols]
        for j in range(4):
            acc = acc + mm_nt(b.gpre[j], self.slabs[1].at[j][cols, :])
        b.second[:, cols] = acc

    def norm1_rows(self):
        b = self.b

        def body(r, sums):
            rows = pl.ds(pl.multiple_of(r * ROWS, ROWS), ROWS)
            c = b.second[rows, :]
            n = b.n1[rows, :]
            g = norm_back(c, self.v(VAG), n, b.r1[rows, 0:1])
            b.second[rows, :] = g
            low = g.astype(BF)
            b.nl[rows, :] = low
            return sums[0] + column_total(c * n), sums[1] + column_total(c), sums[2] + column_total(low)

        zero = jnp.zeros((1, WIDTH), F32)
        sums = lax.fori_loop(0, TOKENS // ROWS, body, (zero, zero, zero))
        self.gvec[VAG:VAG + 1, :], self.gvec[VAS:VAS + 1, :], self.gvec[VO:VO + 1, :] = sums

    def out_grads(self):
        b = self.b
        left = b.mixed[...].T
        for n in range(3):
            cols = slice(n * 256, n * 256 + 256)
            self.grads[0][3, :, cols] = mm(left, b.nl[:, cols]).astype(BF)

    def out_back(self):
        b = self.b
        for n in range(3):
            cols = slice(n * 256, n * 256 + 256)
            b.mixed[:, cols] = mm_nt(b.nl[...], self.slabs[0].at[3][cols, :]).astype(BF)

    def attend_back(self, p):
        b = self.b
        masks, tall = half_masks(), row_masks()
        cols = slice(p * LANES, p * LANES + LANES)
        rows = [slice(s * SEQ, s * SEQ + SEQ) for s in range(2)]
        dos = [[b.mixed[rows[s], cols] * masks[a] for a in range(2)] for s in range(2)]
        dps = [[mm_nt(b.v[rows[s], cols], dos[s][a]) for a in range(2)] for s in range(2)]
        low = [[None, None], [None, None]]
        for s in range(2):
            atts = []
            for a in range(2):
                att = b.p[s * 12 + p * 2 + a]
                atts.append(att.astype(BF))
                dp = dps[s][a]
                low[s][a] = (att * (dp - jnp.sum(att * dp, 0, keepdims=True))).astype(BF)
            b.gpre[2, rows[s], cols] = mm(jnp.concatenate(atts, 1), jnp.concatenate(dos[s], 0)).astype(BF)
        for s in range(2):
            q, kt = b.q[rows[s], cols], b.k[rows[s], cols].T
            dk = mm(jnp.concatenate(low[s], 1), jnp.concatenate([q * masks[0], q * masks[1]], 0))
            b.gpre[1, rows[s], cols] = dk.astype(BF)
            dq = mm(jnp.concatenate([kt * tall[0], kt * tall[1]], 1), jnp.concatenate(low[s], 0))
            b.gpre[0, rows[s], cols] = (dq.T * 0.125).astype(BF)

    def qkv_grads(self, start, count):
        b = self.b
        cols = slice(start, start + count)
        if count == LANES:
            both = mm(b.xt[...], jnp.concatenate([b.gpre[0, :, cols], b.gpre[1, :, cols]], 1))
            self.grads[0][0, :, cols] = both[:, :LANES].astype(BF)
            self.grads[0][1, :, cols] = both[:, LANES:].astype(BF)
        else:
            self.grads[0][0, :, cols] = mm(b.xt[...], b.gpre[0, :, cols]).astype(BF)
            self.grads[0][1, :, cols] = mm(b.xt[...], b.gpre[1, :, cols]).astype(BF)
        self.grads[0][2, :, cols] = mm(b.xt[...], b.gpre[2, :, cols]).astype(BF)
        self.gvec[VQ:VQ + 1, cols] = column_total(b.gpre[0, :, cols])
        self.gvec[VV:VV + 1, cols] = column_total(b.gpre[2, :, cols])

    def input_grad(self, n):
        b = self.b
        cols = slice(n * 256, n * 256 + 256)
        acc = b.second[:, cols]
        for j in range(3):
            acc = acc + mm_nt(b.gpre[j], self.slabs[0].at[j][cols, :])
        b.second[:, cols] = acc


BUFFERS = dict(
    q=((TOKENS, WIDTH), BF), k=((TOKENS, WIDTH), BF), v=((TOKENS, WIDTH), BF), p=((24, SEQ, SEQ), F32),
    mixed=((TOKENS, WIDTH), BF), n1=((TOKENS, WIDTH), F32), r1=((TOKENS, LANES), F32), nl=((TOKENS, WIDTH), BF),
    act=((4, TOKENS, WIDTH), BF), gp=((4, TOKENS, WIDTH), F32), second=((TOKENS, WIDTH), F32),
    gpre=((4, TOKENS, WIDTH), BF), xt=((WIDTH, TOKENS), BF), nlt=((WIDTH, TOKENS), BF),
)


START = {16: 0, 8: 16, 4: 24}
WHOLE = tuple((part, part * LANES, LANES, 0, UNIT, ORDERS[part]) for part in range(PARTS))
STRIPS = (
    ((Z1, Z3, Y1, Y3, X1), (Z1, Z3, X1, Y1, Y3), (Y1, Y3, X3, Z3, Z1)),
    ((Y1, Y3, Z1, Z3, X3), (Z1, Z3, X1, Y3, Y1), (Y1, Y3, X3, Z1, Z3)),
)
COLUMNS = ((0, 256), (256, 256), (512, LANES), (640, LANES))
CUT = tuple((part,) + COLUMNS[part] + (16 * i, 16, STRIPS[part % 2][i]) for part in range(4) for i in range(3))
CHAINS = (CUT, WHOLE, WHOLE)
FIRST = (0, 12, 18)
EVERY = ((0, 2), (0, 4), (0, 2), (0, 2))
VECTORS = "v0 v1 v2 v3".split() + "v4 v5 v6 v7".split()
SCRATCH = dict(
    wa=(SHAPES[0], BF), wb=(SHAPES[1], BF), wc=(SHAPES[2], BF), ga=(SHAPES[0], BF),
    rdb=((2, 1, 4, 2, 2, UNIT, WIDTH), BF), rdc=((4, 2, 2, 2, 1, UNIT, WIDTH), BF),
    rk=((3, 31, UNIT, WIDTH), BF), rx=((UNIT, WIDTH), BF), tall=((UNIT, WIDTH), F32),
    stage=((2, 4, 16, WIDTH), BF), final=((2, 2, 4, 16, WIDTH), BF),
    vt=((4, 2, 8, 2, LANES), F32), gv=((4, 2, 8, 2, LANES), F32),
    rv2=((3, 2, 8, 2, LANES), F32), rv1=((3, 4, 2, LANES), F32), rv0=((7, 2, LANES), F32),
    vec=((16, WIDTH), F32), gvec=((16, WIDTH), F32),
    x=((TOKENS, WIDTH), BF), qkv_in=((12, 3 * WIDTH), BF), out_in=((12, WIDTH), BF), up_in=((12, 4 * WIDTH), BF),
    **{name: ((1, 12), BF) for name in VECTORS}, v8=((1, 48), BF),
)
SEMS = dict(
    loads=(17,), mate_send=(2, 3), mate_recv=(2, 3), send=(3,), recv=(3, PARTS, 7),
    sib_send=(3,), sib_recv=(3, PARTS), vsend=(9,), vrecv=(9,),
    gsib_send=(3, PARTS), gsib_recv=(3, PARTS), gsend=(3,), grecv=(24, 7),
    rep_send=(1,), rep_recv=(1,), gmate_send=(3, 7), gmate_recv=(3, 7), gvsend=(13,), gvrecv=(13,),
)


def box_count(box):
    return box[0][1] * box[1][1] * box[2][1] * box[3][1]


def split3(value):
    high = value.astype(BF)
    rest = value - high.astype(F32)
    mid = rest.astype(BF)
    return high, mid, (rest - mid.astype(F32)).astype(BF)


def owner_masks(block):
    d = lax.broadcasted_iota(jnp.int32, (64, WIDTH), 0)
    c = lax.broadcasted_iota(jnp.int32, (64, WIDTH), 1)
    if block is None:
        return d == (c * 43691) >> 19
    return d == 16 * block + ((c * 43691) >> 21)


def lane_picks(row):
    c = lax.broadcasted_iota(jnp.int32, (WIDTH, LANES), 0)
    lane = lax.broadcasted_iota(jnp.int32, (WIDTH, LANES), 1)
    if row is None:
        return (lane == c - 48 * ((c * 43691) >> 21)).astype(F32).astype(BF)
    return (lane == 12 * row + c - 12 * ((c * 43691) >> 19)).astype(F32).astype(BF)


def mega_kernel(lengths, *refs):
    vecs_in, (qkv_in, out_in, up_in, down_in, x_in, og_in,
               enc_out, sgrad_out, oqkv, oout, oup, odown, ovec), scratch = refs[:9], refs[9:22], refs[22:]
    r = b = types.SimpleNamespace(**dict(zip([*SCRATCH, *BUFFERS, *SEMS], scratch)))
    here = position()
    me = member_of(here)
    sibling = hop(here, CORE)
    twin = hop(here, X2)
    weights = (r.wa, r.wb, r.wc)
    grads = (r.ga, r.wb, r.wc)
    rds = (r.act.at[pl.ds(0, 3)].reshape((2, 1, 4, 2, 2, UNIT, WIDTH)), r.rdb, r.rdc)
    slabs = [w.reshape(4, WIDTH, WIDTH) for w in weights]
    gslabs = [w.reshape(4, WIDTH, WIDTH) for w in grads]
    layer = Layer(slabs, gslabs, r.vec, lengths, r.x, r.x, r.x, r.gvec, b)

    def own_at(phase):
        ylow, z, x, yhigh = (s for s, n in own_box(here))
        return (ylow, here.core, z, x, yhigh) if phase < 2 else (z, x, yhigh, ylow, here.core)

    def mate_copy(which, k):
        mate = mates(here)[k]
        return remote(r.stage.at[which, member_of(mate)], r.final.at[which, 0, me],
                      r.mate_send.at[which, k], r.mate_recv.at[which, k], mate)

    def assemble(which):
        for k in range(3):
            mate_copy(which, k).wait()
        r.final[which, 0, me] = r.stage[which, me]
        for i in range(4):
            r.tall[12 * i:12 * i + 12, :] = r.final[which, 0, i, 0:12, :].astype(F32)
        weights[which][own_at(which)] = r.tall[...].astype(BF)

    def push(phase, part, found, slot, there):
        w = weights[phase]
        for box in found:
            view = w.at[slices(phase, here.core, box, part)]
            remote(view, view, r.send.at[phase], r.recv.at[phase, part, slot], there).start()

    def share(phase, part, found):
        w = weights[phase]
        for box in found:
            view = w.at[slices(phase, here.core, box, part)]
            remote(view, view, r.sib_send.at[phase], r.sib_recv.at[phase, part], sibling).start()

    def gather_first(phase):
        for part in range(PARTS):
            for slot, there in enumerate(trio(here, ORDERS[part])):
                push(phase, part, boxes(here, ()), slot, there)

    def gather(phase, step):
        w = weights[phase]
        for part in range(PARTS):
            order = ORDERS[part]
            if step == 2:
                for slot in range(3):
                    wait_units(w, phase, 1, part, r.recv.at[phase, part, slot])
            else:
                wait_units(w, phase, 1 << (step - 1), part, r.recv.at[phase, part, step])
            there = hop(here, order[step])
            if step < 4:
                push(phase, part, boxes(here, order[:step]), step + 1, there)
            else:
                for half, found in enumerate(halves(boxes(here, order[:4]))):
                    push(phase, part, found, 5 + half, there)
                share(phase, part, boxes(here, order[:4]))

    def gather_last(phase, half):
        for part in range(PARTS):
            order = ORDERS[part]
            wait_units(weights[phase], phase, 8, part, r.recv.at[phase, part, 5 + half])
            share(phase, part, halves(boxes(hop(here, order[4]), order[:4]))[half])

    def gathered(phase, parts=range(PARTS)):
        for part in parts:
            wait_units(weights[phase], phase, 32, part, r.sib_recv.at[phase, part])

    def wait_bytes(phase, units, sem):
        view = weights[phase].reshape((64, UNIT, WIDTH)).at[pl.ds(0, units)]
        pltpu.make_async_copy(view, view, sem).wait()

    def gather_sent(phase):
        wait_bytes(phase, 32, r.sib_send.at[phase])
        wait_bytes(phase, 31, r.send.at[phase])

    def vec_tile(place):
        return (place.z, place.x % 2, place.y * 2 + place.core)

    def vec_pair(place):
        return (place.z, place.x % 2, pl.ds(place.y // 2 * 4, 4))

    def vec_ring(place):
        return (pl.ds(place.z // 2 * 2, 2), place.x % 2)

    def vec_peers(k):
        return (mates(here), trio(here, (Y3, Z1)), trio(here, (Z3, X1)))[k]

    def vec_copies(k):
        view = r.vt.at[(vec_tile, vec_pair, vec_ring)[k](here)]
        return [remote(view, view, r.vsend.at[3 * k + i], r.vrecv.at[3 * k + i], there) for i, there in enumerate(vec_peers(k))]

    def vec_start(k):
        for copy in vec_copies(k):
            copy.start()

    def vec_wait(k):
        for copy in vec_copies(k):
            copy.wait()

    def expand():
        first = r.vt[:, :, :, 0, :].reshape(64, LANES)
        second = r.vt[:, :, :, 1, :].reshape(64, LANES).astype(BF)
        mask = owner_masks(None)
        turned = [first] + [pltpu.roll(first, LANES - 12 * row, 1) for row in range(1, 8)]
        t = mm_nt(jnp.concatenate(turned, 0).astype(BF), lane_picks(0)).reshape(8, 64, WIDTH)
        for row in range(8):
            r.vec[row:row + 1, :] = jnp.sum(jnp.where(mask, t[row], 0.0), 0, keepdims=True)
        t = mm_nt(second, lane_picks(None))
        for j in range(4):
            r.vec[8 + j:9 + j, :] = jnp.sum(jnp.where(owner_masks(j), t, 0.0), 0, keepdims=True)

    def sib_copy(phase, k):
        g, rd = grads[phase], rds[phase]
        if phase == 0:
            cols = pl.ds(*COLUMNS[k])
            src = g.at[:, pl.ds(sibling.core, 1), :, :, :, :, cols]
            dst = rd.at[:, :, :, :, :, :, cols]
        elif phase == 1:
            src, dst = g.at[k, sibling.core], rd.at[k, 0]
        else:
            src, dst = g.at[k, :, :, :, pl.ds(sibling.core, 1)], rd.at[k]
        return remote(src, dst, r.gsib_send.at[phase, k], r.gsib_recv.at[phase, k], sibling)

    def sib_add(phase, k):
        sib_copy(phase, k).wait()
        g, rd = grads[phase], rds[phase]
        for i in range(4):
            if phase == 0:
                cols = slice(COLUMNS[k][0], sum(COLUMNS[k]))
                at = (slice(None), pl.ds(here.core, 1), i, slice(None), slice(None), slice(None), cols)
                g[at] = g[at] + rd[:, :, i, :, :, :, cols]
            elif phase == 1:
                g[k, here.core, i] = g[k, here.core, i] + rd[k, 0, i]
            else:
                at = (k, i // 2, i % 2, slice(None), pl.ds(here.core, 1))
                g[at] = g[at] + rd[k, i // 2, i % 2]

    def unit_slices(phase, box, chain):
        _, col, cols, row, rows, _ = chain
        return slices(phase, here.core, box, 0)[:5] + (slice(row, row + rows), slice(col, col + cols))

    def hop_start(phase, c, step):
        chain = CHAINS[phase][c]
        _, col, cols, row, rows, order = chain

        def send(box, at, slot, there):
            n = box_count(box)
            src = grads[phase].at[slices(phase, here.core, box, 0)[:5]]
            dst = r.rk.at[phase, pl.ds(at, n)].reshape(src.shape)
            at5 = (slice(None),) * 5 + (pl.ds(row, rows), pl.ds(col, cols))
            remote(src.at[at5], dst.at[at5], r.gsend.at[phase], r.grecv.at[FIRST[phase] + c, slot], there).start()
            return at + n

        if step == 1:
            for slot, there in enumerate(trio(here, order)):
                send(boxes(there, ())[0], 28 + slot, slot, there)
            return
        if phase == 0 and step == 3:
            for i, there in enumerate(trio(here, order[2:])):
                at = 16 + 4 * i
                for box in boxes(there, order[:2]):
                    at = send(box, at, 3 + i, there)
            return
        there = hop(here, order[step])
        at = START[1 << step]
        for box in boxes(there, order[:step]):
            at = send(box, at, step + 2, there)

    def landing(phase, c, at, n):
        _, col, cols, row, rows, _ = CHAINS[phase][c]
        return r.rk.at[phase, pl.ds(at, n), pl.ds(row, rows), pl.ds(col, cols)]

    def hop_add(phase, c, step):
        g = grads[phase]
        chain = CHAINS[phase][c]
        if step == 1:
            where = unit_slices(phase, boxes(here, ())[0], chain)
            total = g[where].astype(F32)
            for slot in range(3):
                view = landing(phase, c, 28 + slot, 1)
                pltpu.make_async_copy(view, view, r.grecv.at[FIRST[phase] + c, slot]).wait()
                total = total + view[...].astype(F32).reshape(total.shape)
            g[where] = total.astype(BF)
            return
        if phase == 0 and step == 3:
            for i in range(3):
                view = landing(phase, c, 16 + 4 * i, 4)
                pltpu.make_async_copy(view, view, r.grecv.at[FIRST[phase] + c, 3 + i]).wait()
            at = 16
            for box in boxes(here, chain[5][:2]):
                m = box_count(box)
                where = unit_slices(phase, box, chain)
                total = g[where].astype(F32)
                for i in range(3):
                    total = total + landing(phase, c, at + 4 * i, m)[...].astype(F32).reshape(total.shape)
                g[where] = total.astype(BF)
                at += m
            return
        n = 1 << step
        at = START[n]
        view = landing(phase, c, at, n)
        pltpu.make_async_copy(view, view, r.grecv.at[FIRST[phase] + c, step + 2]).wait()
        for box in boxes(here, chain[5][:step]):
            m = box_count(box)
            where = unit_slices(phase, box, chain)
            old = g[where]
            g[where] = old + landing(phase, c, at, m)[...].reshape(old.shape)
            at += m

    def rep_copy():
        return remote(grads[2].at[own_at(2)], r.rx, r.rep_send.at[0], r.rep_recv.at[0], twin)

    def reduce_first(phase):
        for k in range(2 if phase == 1 else 4):
            sib_add(phase, k)
        for part in range(PARTS):
            hop_start(phase, part, 4)

    def move(phase, c, step):
        hop_add(phase, c, step)
        if step > 1:
            hop_start(phase, c, 1 if phase == 0 and step == 3 else step - 1)

    def reduce(phase, step):
        for part in range(PARTS):
            move(phase, part, step)

    def first_part(part):
        sib_add(0, part)
        for c, chain in enumerate(CUT):
            if chain[0] == part:
                hop_start(0, c, 4)

    def move_part(part, step):
        for c, chain in enumerate(CUT):
            if chain[0] == part:
                move(0, c, step)

    def gmate_copy(which, k):
        others = mates(here)
        there = (others + [twin] + [hop(mate, X2) for mate in others])[k]
        cols = (pl.ds(0, 512), pl.ds(0, WIDTH), pl.ds(512, 256))[which]
        phase = which % 2
        return remote(r.stage.at[phase, member_of(there), :, cols], r.final.at[phase, k // 3 if k < 6 else 1, me, :, cols],
                      r.gmate_send.at[which, k], r.gmate_recv.at[which, k], there)

    def hand_over(which):
        phase = which % 2
        cols = (slice(0, 512), slice(0, WIDTH), slice(512, WIDTH))[which]
        r.tall[:, cols] = grads[phase][own_at(phase) + (slice(None), cols)].astype(F32)
        for i in range(4):
            r.stage[phase, i, 0:12, cols] = r.tall[12 * i:12 * i + 12, cols].astype(BF)
        for k in range(7):
            gmate_copy(which, k).start()

    def deliver(which):
        phase = which % 2
        cols = (slice(0, 512), slice(0, WIDTH), slice(512, WIDTH))[which]
        for k in range(7):
            gmate_copy(which, k).wait()
        r.final[phase, 0, me, :, cols] = r.stage[phase, me, :, cols]
        for i in range(4):
            at = slice(i * WIDTH + cols.start, i * WIDTH + cols.stop)
            dst = oup.at[:, at] if phase else (oqkv.at[:, at] if i < 3 else oout.at[:, cols])
            dst[...] = r.final[phase, 0, i, 0:12, cols].astype(F32) + r.final[phase, 1, i, 0:12, cols].astype(F32)

    def deliver_down():
        rep_copy().wait()
        odown[...] = grads[2][own_at(2)].astype(F32) + r.rx[...].astype(F32)

    def reduce_sent(phase):
        wait_bytes(phase, 31, r.gsend.at[phase])

    def pack_rows(first, count):
        mask = owner_masks(None).astype(F32).astype(BF)
        pieces = split3(r.gvec[first:first + count, :])
        spread = [piece[i:i + 1, :] * mask for piece in pieces for i in range(count)]
        out = mm(jnp.concatenate(spread, 0), lane_picks(0)).reshape(3, count, 64, LANES)
        out = out[0] + out[1] + out[2]
        total = out[0] if first == 0 else pltpu.roll(out[0], 12 * first, 1)
        for i in range(1, count):
            total = total + pltpu.roll(out[i], 12 * (first + i), 1)
        return total.reshape(4, 2, 8, LANES)

    def pack():
        pieces = split3(r.gvec[8:12, :])
        masks = [owner_masks(j).astype(F32).astype(BF) for j in range(4)]
        spread = [piece[j:j + 1, :] * masks[j] for piece in pieces for j in range(4)]
        out = mm(jnp.concatenate(spread, 0), lane_picks(None)).reshape(12, 64, LANES)
        r.gv[:, :, :, 0, :] = pack_rows(2, 6)
        r.gv[:, :, :, 1, :] = jnp.sum(out, 0).reshape(4, 2, 8, LANES)

    def gvec_copies(k):
        if k == 0:
            peers = mates(here) + [twin] + [hop(mate, X2) for mate in mates(here)]
        else:
            peers = vec_peers(k)
        part, landing_ref = ((vec_tile, r.rv0), (vec_pair, r.rv1), (vec_ring, r.rv2))[k]
        base = (6, 3, 0)[k]
        return [remote(r.gv.at[part(there)], landing_ref.at[i], r.gvsend.at[base + i], r.gvrecv.at[base + i], there)
                for i, there in enumerate(peers)]

    def gvec_start(k):
        for copy in gvec_copies(k):
            copy.start()

    def gvec_add(k):
        part, landing_ref = ((vec_tile, r.rv0), (vec_pair, r.rv1), (vec_ring, r.rv2))[k]
        at = part(here)
        total = r.gv[at]
        for i, copy in enumerate(gvec_copies(k)):
            copy.wait()
            total = total + landing_ref[i].reshape(total.shape)
        r.gv[at] = total

    near = [hop(here, link) for link in (Y1, Y3, Z1, Z3, X1, X3, CORE, X2, Y2, Z2)]
    near += [mates(here)[2], hop(hop(here, Y3), Z1), hop(hop(here, Y1), Z3)]
    near += [hop(mate, X2) for mate in mates(here)]
    near += [hop(hop(here, a), c) for a, c in ((Z3, X1), (X1, Y1), (X1, Y3), (X3, Z1), (X3, Z3))]
    loads = [pltpu.make_async_copy(src, dst, r.loads.at[i]) for i, (src, dst) in enumerate((
        (qkv_in, r.qkv_in), (out_in, r.out_in), (up_in, r.up_in), (down_in, weights[2].at[own_at(2)]), (x_in, r.x)))]
    held = [getattr(r, name) for name in VECTORS] + [r.v8]
    vec_loads = [pltpu.make_async_copy(src, dst, r.loads.at[8 + i]) for i, (src, dst) in enumerate(zip(vecs_in, held))]
    for load in loads[:4] + vec_loads + loads[4:]:
        load.start()
    barrier = pltpu.get_barrier_semaphore()
    for place in near:
        pl.semaphore_signal(barrier, inc=1, device_id=device_of(place), device_id_type=MESH)
    og_load = pltpu.make_async_copy(og_in, r.x, r.loads.at[5])
    own = vec_tile(here)
    r.vt[own] = jnp.zeros((2, LANES), F32)
    for load in loads[:4] + vec_loads:
        load.wait()
    for i in range(8):
        r.vt[own + (slice(0, 1), slice(12 * i, 12 * i + 12))] = held[i][...].astype(F32)
    r.vt[own + (slice(1, 2), slice(0, 48))] = held[8][...].astype(F32)
    for i in range(4):
        r.stage[0, i, 0:12, :] = r.qkv_in[:, i * WIDTH:(i + 1) * WIDTH] if i < 3 else r.out_in[...]
        r.stage[1, i, 0:12, :] = r.up_in[:, i * WIDTH:(i + 1) * WIDTH]
    pl.semaphore_wait(barrier, len(near))
    for k in range(3):
        mate_copy(0, k).start()
    vec_start(0)
    for k in range(3):
        mate_copy(1, k).start()
    gather_first(2)
    assemble(0)
    vec_wait(0)
    vec_start(1)
    gather_first(0)
    assemble(1)
    gather_first(1)
    loads[4].wait()
    b.xt[...] = r.x[...].T
    vec_wait(1)
    vec_start(2)
    gather(0, 2)
    gather(2, 2)
    gather(1, 2)
    gather(0, 3)
    vec_wait(2)
    expand()
    gather(0, 4)
    gather(1, 3)
    gather(2, 3)
    gather_last(0, 0)
    gather_last(0, 1)
    for n in range(3):
        gathered(0, (2 * n, 2 * n + 1))
        layer.project(n)
        if n == 0:
            gather(1, 4)
    gather(2, 4)
    layer.attend()
    gather_last(1, 0)
    gather_last(1, 1)
    layer.attn_out()
    og_load.start()
    b.nlt[...] = b.nl[...].T
    gather_last(2, 0)
    gather_last(2, 1)
    gathered(1)
    layer.feed()
    og_load.wait()
    gathered(2)
    layer.feed_out()
    enc_store = pltpu.make_async_copy(r.x, enc_out, r.loads.at[6])
    enc_store.start()
    gather_sent(2)

    def down_body(j, _):
        layer.feed_back(j)
        layer.down_grads(j)
        sib_copy(2, j).start()
        return 0

    lax.fori_loop(0, 4, down_body, 0)
    for n in range(3):
        layer.norm1_back(n)
    reduce_first(2)
    gather_sent(1)

    def up_body(i, _):
        layer.up_grads(i * 2 + sibling.core)
        sib_copy(1, i).start()
        return 0

    def up_own(i, _):
        layer.up_grads(i * 2 + here.core)
        return 0

    lax.fori_loop(0, 2, up_body, 0)
    lax.fori_loop(0, 2, up_own, 0)
    layer.norm1_rows()
    layer.out_grads()
    reduce(2, 4)
    reduce_first(1)
    layer.out_back()
    pack()
    layer.attend_back(0)
    layer.attend_back(1)
    layer.qkv_grads(*COLUMNS[0])
    sib_copy(0, 0).start()
    reduce(2, 3)
    layer.attend_back(2)
    first_part(0)
    layer.attend_back(3)
    layer.qkv_grads(*COLUMNS[1])
    sib_copy(0, 1).start()
    reduce(1, 4)
    layer.attend_back(4)
    layer.qkv_grads(*COLUMNS[2])
    sib_copy(0, 2).start()
    first_part(1)
    move_part(0, 4)
    reduce(2, 2)
    layer.attend_back(5)
    layer.qkv_grads(*COLUMNS[3])
    sib_copy(0, 3).start()
    first_part(2)
    reduce(1, 3)
    layer.input_grad(0)
    layer.input_grad(1)
    first_part(3)
    r.gv[:, :, :, 0, :] = r.gv[:, :, :, 0, :] + pack_rows(VQ, 2)
    gvec_start(2)
    move_part(1, 4)
    move_part(0, 3)
    layer.input_grad(2)
    sgrad_store = pltpu.make_async_copy(b.second, sgrad_out, r.loads.at[7])
    sgrad_store.start()
    reduce(1, 2)
    move_part(2, 4)
    gvec_add(2)
    gvec_start(1)
    reduce(2, 1)
    rep_copy().start()
    move_part(3, 4)
    reduce(1, 1)
    hand_over(1)
    move_part(0, 1)
    move_part(1, 3)
    move_part(2, 3)
    gvec_add(1)
    gvec_start(0)
    move_part(3, 3)
    deliver_down()
    move_part(1, 1)
    hand_over(0)
    move_part(2, 1)
    move_part(3, 1)
    hand_over(2)
    deliver(1)
    gvec_add(0)
    ovec[...] = r.gv[vec_tile(here)]
    for phase in range(1, 3):
        reduce_sent(phase)
    gather_sent(0)
    reduce_sent(0)
    enc_store.wait()
    sgrad_store.wait()
    deliver(0)
    deliver(2)


def run_layer(lengths, vecs, qkv, out, up, down, x, og):
    vm = pl.BlockSpec(memory_space=pltpu.VMEM)
    hb = pl.BlockSpec(memory_space=pl.ANY)
    return pl.pallas_call(
        mega_kernel,
        out_shape=[
            jax.ShapeDtypeStruct((TOKENS, WIDTH), BF), jax.ShapeDtypeStruct((TOKENS, WIDTH), F32),
            jax.ShapeDtypeStruct((12, 3 * WIDTH), F32), jax.ShapeDtypeStruct((12, WIDTH), F32),
            jax.ShapeDtypeStruct((12, 4 * WIDTH), F32), jax.ShapeDtypeStruct((UNIT, WIDTH), F32), jax.ShapeDtypeStruct((2, LANES), F32),
        ],
        in_specs=[pl.BlockSpec(memory_space=pltpu.SMEM)] + [hb] * 15,
        out_specs=[hb, hb] + [vm] * 5,
        scratch_shapes=[pltpu.VMEM(s, d) for s, d in SCRATCH.values()] + [pltpu.VMEM(s, d) for s, d in BUFFERS.values()]
        + [pltpu.SemaphoreType.DMA(s) for s in SEMS.values()],
        compiler_params=pltpu.CompilerParams(collective_id=1, has_side_effects=True, vmem_limit_bytes=63 * 2**20),
    )(lengths, *vecs, qkv, out, up, down, x, og)


def finish_kernel(*refs):
    srcs, dsts, vec_outs, held, parts, sems = refs[:7], refs[7:13], refs[13:22], refs[22:29], refs[29:38], refs[38]
    loads = [pltpu.make_async_copy(src, mid, sems.at[0, i]) for i, (src, mid) in enumerate(zip(srcs, held))]
    stores = [pltpu.make_async_copy(mid, dst, sems.at[1, i]) for i, (mid, dst) in enumerate(zip(held, dsts))]
    vec_stores = [pltpu.make_async_copy(mid, dst, sems.at[1, 6 + i]) for i, (mid, dst) in enumerate(zip(parts, vec_outs))]
    for load in loads[::-1]:
        load.start()
    loads[6].wait()
    vec = held[6]
    for i in range(8):
        parts[i][...] = vec[0:1, 12 * i:12 * i + 12]
    parts[8][...] = vec[1:2, 0:48]
    for store in vec_stores:
        store.start()
    for load, store in list(zip(loads, stores))[::-1]:
        load.wait()
        store.start()
    for store in vec_stores + stores:
        store.wait()


def finish(results):
    hb = pl.BlockSpec(memory_space=pl.ANY)
    small = [(1, n) for n in [12] * 8 + [48]]
    return pl.pallas_call(
        finish_kernel,
        out_shape=[jax.ShapeDtypeStruct(a.shape, a.dtype) for a in results[:6]] + [jax.ShapeDtypeStruct(n, F32) for n in small],
        in_specs=[hb] * 7,
        out_specs=[hb] * 15,
        scratch_shapes=[pltpu.VMEM(a.shape, a.dtype) for a in results] + [pltpu.VMEM(n, F32) for n in small]
        + [pltpu.SemaphoreType.DMA((2, 15))],
        compiler_params=pltpu.CompilerParams(vmem_limit_bytes=63 * 2**20),
    )(*results)


def local(states, qkv_weight, query_bias, value_bias, out_weight, out_bias, attn_gain, attn_shift, up_weight, up_bias,
          down_weight, down_bias, ffn_gain, ffn_shift, out_grad, lengths):
    vecs = [v.reshape(1, -1) for v in (query_bias, value_bias, out_bias, attn_gain, attn_shift, down_bias, ffn_gain, ffn_shift, up_bias)]
    results = run_layer(
        lengths.reshape(1, 2), vecs, qkv_weight, out_weight, up_weight, down_weight,
        states.reshape(TOKENS, WIDTH), out_grad.reshape(TOKENS, WIDTH))
    enc, sgrad, oqkv, oout, oup, odown, *o = finish(results)
    o = [v.reshape(-1) for v in o]
    return (enc.reshape(states.shape), sgrad.reshape(states.shape), oqkv, o[0], o[1], oout, o[2], o[3], o[4],
            oup, o[8], odown, o[5], o[6], o[7])


def solution(mesh):
    return jax.shard_map(
        local,
        mesh=mesh,
        in_specs=(
            P(None, ("dp", "rep"), None, None),
            P("dp", None),
            P("dp"),
            P("dp"),
            P("dp", None),
            P("dp"),
            P("dp"),
            P("dp"),
            P("dp", None),
            P("dp"),
            P("dp", None),
            P("dp"),
            P("dp"),
            P("dp"),
            P(None, ("dp", "rep"), None, None),
            P(None, ("dp", "rep")),
        ),
        out_specs=(
            P(None, ("dp", "rep"), None, None),
            P(None, ("dp", "rep"), None, None),
            P("dp", None),
            P("dp"),
            P("dp"),
            P("dp", None),
            P("dp"),
            P("dp"),
            P("dp"),
            P("dp", None),
            P("dp"),
            P("dp", None),
            P("dp"),
            P("dp"),
            P("dp"),
        ),
        check_vma=False,
    )
```

```python
import collections
import math
import types

import jax
import jax.numpy as jnp
from jax import lax
from jax.experimental import pallas as pl
from jax.experimental.pallas import tpu as pltpu
from jax.sharding import PartitionSpec as P

Place = collections.namedtuple("Place", "core y z x")
MESH = pl.DeviceIdType.MESH
BF = jnp.bfloat16
F32 = jnp.float32
WIDTH = 768
UNIT = 48
LANES = 128
PARTS = 6

CORE, Y1, Y3, Z1, Z3, X1, X2, X3 = (0, 0), (1, 1), (1, 3), (2, 1), (2, 3), (3, 1), (3, 2), (3, 3)
Y2, Z2 = (1, 2), (2, 2)

ORDERS = (
    (Z1, Z3, Y1, Y3, X1),
    (Y1, Y3, Z1, Z3, X3),
    (Y3, Z1, Z3, X1, Y1),
    (Y1, Z3, X1, Z1, Y3),
    (Y1, Z3, X3, Y3, Z1),
    (Z1, Y3, X3, Y1, Z3),
)


def position():
    dp = lax.axis_index("dp")
    rep = lax.axis_index("rep")
    return Place(dp % 2, (dp // 2) % 4, dp // 16, rep * 2 + (dp // 8) % 2)


def device_of(place):
    dp = ((place.z * 2 + place.x % 2) * 4 + place.y) * 2 + place.core
    return (dp, place.x // 2)


def hop(place, link):
    axis, how = link
    p = place[axis]
    moved = (1 - p, p + 1 - 2 * (p % 2), (p + 2) % 4, 3 - p)[how]
    return Place(*(moved if i == axis else q for i, q in enumerate(place)))


def boxes(place, links):
    y, z, x = place.y, place.z, place.x % 2
    if Y1 in links and Y3 in links:
        ys = [((0, 2), (0, 2))]
    elif Y1 in links:
        ys = [((0, 2), (y // 2, 1))]
    elif Y3 in links:
        ys = [((y % 2, 1), (y // 2, 1)), ((1 - y % 2, 1), (1 - y // 2, 1))]
    else:
        ys = [((y % 2, 1), (y // 2, 1))]
    if Z1 in links and Z3 in links:
        zs = [(0, 4)]
    elif Z1 in links:
        zs = [((z // 2) * 2, 2)]
    elif Z3 in links:
        zs = [(z, 1), (3 - z, 1)]
    else:
        zs = [(z, 1)]
    xs = (0, 2) if X1 in links or X3 in links else (x, 1)
    return [(ylow, zz, xs, yhigh) for (ylow, yhigh) in ys for zz in zs]


def slices(phase, core, box, part):
    ylow, z, x, yhigh = (pl.ds(*s) for s in box)
    cols = pl.ds(part * LANES, LANES)
    if phase < 2:
        return (ylow, pl.ds(core, 1), z, x, yhigh, slice(None), cols)
    return (z, x, yhigh, ylow, pl.ds(core, 1), slice(None), cols)


SHAPES = (
    (2, 2, 4, 2, 2, UNIT, WIDTH),
    (2, 2, 4, 2, 2, UNIT, WIDTH),
    (4, 2, 2, 2, 2, UNIT, WIDTH),
)


def size_box(count):
    sizes = {1: (1, 1, 1, 1), 2: (1, 1, 1, 2), 4: (1, 1, 2, 2), 8: (1, 2, 2, 2), 16: (1, 4, 2, 2), 32: (2, 4, 2, 2)}[count]
    return tuple((0, n) for n in sizes)


def wait_units(ref, phase, count, part, sem):
    view = ref.at[slices(phase, 0, size_box(count), part)]
    pltpu.make_async_copy(view, view, sem).wait()


def remote(src, dst, send_sem, recv_sem, place):
    return pltpu.make_async_remote_copy(
        src_ref=src, dst_ref=dst, send_sem=send_sem, recv_sem=recv_sem,
        device_id=device_of(place), device_id_type=MESH,
    )


def greet(places):
    barrier = pltpu.get_barrier_semaphore()
    for place in places:
        pl.semaphore_signal(barrier, inc=1, device_id=device_of(place), device_id_type=MESH)
    pl.semaphore_wait(barrier, len(places))


def member_of(place):
    return (place.y % 2) * 2 + place.core


def mates(here):
    return [hop(here, CORE), hop(here, Y1), hop(hop(here, CORE), Y1)]


def own_box(here):
    return boxes(here, ())[0]


def trio(place, order):
    a, b = hop(place, order[0]), hop(place, order[1])
    return a, b, hop(a, order[1])


def halves(found):
    if len(found) == 2:
        return [found[:1], found[1:]]
    ylow, (start, n), x, yhigh = found[0]
    return [[(ylow, (start, n // 2), x, yhigh)], [(ylow, (start + n // 2, n // 2), x, yhigh)]]


HALF = 256
SEQ = 256
TOKENS = 512
ROWS = 128
epsilon = 1e-05
NT = (((1,), (1,)), ((), ()))
TN = (((0,), (0,)), ((), ()))
VQ, VV, VO, VAG, VAS, VD, VFG, VFS, VUP = range(9)


def mm(left, right):
    return jnp.dot(left, right, preferred_element_type=F32)


def mm_nt(left, right):
    return lax.dot_general(left, right, NT, preferred_element_type=F32)


def mm_tn(left, right):
    return lax.dot_general(left, right, TN, preferred_element_type=F32)


def normalise(value):
    center = value - jnp.mean(value, -1, keepdims=True)
    scale = lax.rsqrt(jnp.mean(center * center, -1, keepdims=True) + epsilon)
    return center * scale, scale


def norm_back(cot, gain, n, scale):
    e = cot * gain
    return scale * (e - jnp.mean(e, -1, keepdims=True) - n * jnp.mean(e * n, -1, keepdims=True))


def half_masks():
    lane = lax.broadcasted_iota(jnp.int32, (1, LANES), 1)
    low = (lane < 64).astype(F32).astype(BF)
    return low, (1.0 - low.astype(F32)).astype(BF)


def row_masks():
    row = lax.broadcasted_iota(jnp.int32, (LANES, SEQ), 0)
    low = (row < 64).astype(F32).astype(BF)
    return low, (1.0 - low.astype(F32)).astype(BF)


def column_total(ref_rows):
    return jnp.sum(ref_rows.astype(F32), 0, keepdims=True)


class Layer:
    def __init__(self, slabs, grads, vec, lengths, x, og, enc, gvec, b):
        self.slabs, self.grads, self.vec, self.lengths, self.x, self.og = slabs, grads, vec, lengths, x, og
        self.enc, self.gvec, self.b = enc, gvec, b

    def v(self, row):
        return self.vec[row:row + 1, :]

    def project(self, n):
        b = self.b
        cols = slice(n * 256, n * 256 + 256)
        x = self.x[...]
        b.q[:, cols] = ((mm(x, self.slabs[0].at[0][:, cols]) + self.vec[VQ:VQ + 1, cols]).astype(BF).astype(F32) * 0.125).astype(BF)
        b.k[:, cols] = mm(x, self.slabs[0].at[1][:, cols]).astype(BF)
        b.v[:, cols] = (mm(x, self.slabs[0].at[2][:, cols]) + self.vec[VV:VV + 1, cols]).astype(BF)

    def attend(self):
        b = self.b
        masks, tall = half_masks(), row_masks()
        key = lax.broadcasted_iota(jnp.int32, (SEQ, SEQ), 0)

        def body(p, _):
            cols = pl.ds(pl.multiple_of(p * LANES, LANES), LANES)
            rows = [slice(s * SEQ, s * SEQ + SEQ) for s in range(2)]
            scores = [[mm_nt(b.k[rows[s], cols] * masks[a], b.q[rows[s], cols]) for a in range(2)] for s in range(2)]
            low = [[None, None], [None, None]]
            for s in range(2):
                length = self.lengths[0, s]
                for a in range(2):
                    st = jnp.where(key < length, scores[s][a], -1e9)
                    e = jnp.exp(st - jnp.max(st, 0, keepdims=True))
                    att = e * (1.0 / jnp.sum(e, 0, keepdims=True))
                    b.p[s * 12 + p * 2 + a] = att
                    low[s][a] = att.astype(BF)
            for s in range(2):
                vt = b.v[rows[s], cols].T
                out = mm(jnp.concatenate([vt * tall[0], vt * tall[1]], 1), jnp.concatenate(low[s], 0))
                b.mixed[rows[s], cols] = out.T.astype(BF)
            return 0

        lax.fori_loop(0, 6, body, 0)

    def attn_out(self):
        b = self.b
        for n in range(3):
            cols = slice(n * 256, n * 256 + 256)
            acc = mm(b.mixed[...], self.slabs[0].at[3][:, cols]) + self.vec[VO:VO + 1, cols]
            b.n1[:, cols] = self.x[:, cols].astype(F32) + acc

        def body(r, _):
            rows = pl.ds(pl.multiple_of(r * ROWS, ROWS), ROWS)
            n, scale = normalise(b.n1[rows, :])
            b.n1[rows, :] = n
            b.r1[rows, :] = jnp.broadcast_to(scale, (ROWS, LANES))
            b.nl[rows, :] = (n * self.v(VAG) + self.v(VAS)).astype(BF)
            return 0

        lax.fori_loop(0, TOKENS // ROWS, body, 0)

    def feed(self):
        b = self.b

        def body(j, _):
            w = self.slabs[1].at[j]
            for n in range(3):
                cols = slice(n * 256, n * 256 + 256)
                bias = self.vec[pl.ds(VUP + j, 1), cols]
                for h in range(2):
                    rows = slice(h * 256, h * 256 + 256)
                    pre = mm(b.nl[rows, :], w[:, cols]) + bias
                    cdf = 0.5 * (1.0 + lax.erf(pre * (1.0 / math.sqrt(2.0))))
                    pdf = jnp.exp(pre * pre * -0.5) * (1.0 / math.sqrt(2.0 * math.pi))
                    b.act[j, rows, cols] = (pre * cdf).astype(BF)
                    b.gp[j, rows, cols] = cdf + pre * pdf
            return 0

        lax.fori_loop(0, 4, body, 0)

    def feed_out(self):
        b = self.b
        for n in range(3):
            cols = slice(n * 256, n * 256 + 256)
            acc = self.b.n1[:, cols] * self.vec[VAG:VAG + 1, cols] + self.vec[VAS:VAS + 1, cols] + self.vec[VD:VD + 1, cols]
            for j in range(4):
                acc = acc + mm(b.act[j], self.slabs[2].at[j][:, cols])
            b.second[:, cols] = acc

        def body(r, sums):
            rows = pl.ds(pl.multiple_of(r * ROWS, ROWS), ROWS)
            n, scale = normalise(b.second[rows, :])
            c = self.og[rows, :].astype(F32)
            self.enc[rows, :] = (n * self.v(VFG) + self.v(VFS)).astype(BF)
            g = norm_back(c, self.v(VFG), n, scale)
            b.second[rows, :] = g
            low = g.astype(BF)
            b.nl[rows, :] = low
            return sums[0] + column_total(c * n), sums[1] + column_total(c), sums[2] + column_total(low)

        zero = jnp.zeros((1, WIDTH), F32)
        sums = lax.fori_loop(0, TOKENS // ROWS, body, (zero, zero, zero))
        self.gvec[VFG:VFG + 1, :], self.gvec[VFS:VFS + 1, :], self.gvec[VD:VD + 1, :] = sums

    def down_grads(self, j):
        b = self.b
        left = b.act[j].T
        for n in range(3):
            cols = slice(n * 256, n * 256 + 256)
            self.grads[2][j, :, cols] = mm(left, b.nl[:, cols]).astype(BF)

    def feed_back(self, j):
        b = self.b
        w = self.slabs[2].at[j]
        for n in range(3):
            cols = slice(n * 256, n * 256 + 256)
            total = jnp.zeros((1, 256), F32)
            for h in range(2):
                rows = slice(h * 256, h * 256 + 256)
                acc = mm_nt(b.nl[rows, :], w[cols, :])
                low = (acc * b.gp[j, rows, cols]).astype(BF)
                b.gpre[j, rows, cols] = low
                total = total + column_total(low)
            self.gvec[pl.ds(VUP + j, 1), cols] = total

    def up_grads(self, j):
        b = self.b
        for n in range(3):
            cols = slice(n * 256, n * 256 + 256)
            self.grads[1][j, :, cols] = mm(b.nlt[...], b.gpre[j, :, cols]).astype(BF)

    def norm1_back(self, n):
        b = self.b
        cols = slice(n * 256, n * 256 + 256)
        acc = b.second[:, cols]
        for j in range(4):
            acc = acc + mm_nt(b.gpre[j], self.slabs[1].at[j][cols, :])
        b.second[:, cols] = acc

    def norm1_rows(self):
        b = self.b

        def body(r, sums):
            rows = pl.ds(pl.multiple_of(r * ROWS, ROWS), ROWS)
            c = b.second[rows, :]
            n = b.n1[rows, :]
            g = norm_back(c, self.v(VAG), n, b.r1[rows, 0:1])
            b.second[rows, :] = g
            low = g.astype(BF)
            b.nl[rows, :] = low
            return sums[0] + column_total(c * n), sums[1] + column_total(c), sums[2] + column_total(low)

        zero = jnp.zeros((1, WIDTH), F32)
        sums = lax.fori_loop(0, TOKENS // ROWS, body, (zero, zero, zero))
        self.gvec[VAG:VAG + 1, :], self.gvec[VAS:VAS + 1, :], self.gvec[VO:VO + 1, :] = sums

    def out_grads(self):
        b = self.b
        left = b.mixed[...].T
        for n in range(3):
            cols = slice(n * 256, n * 256 + 256)
            self.grads[0][3, :, cols] = mm(left, b.nl[:, cols]).astype(BF)

    def out_back(self):
        b = self.b
        for n in range(3):
            cols = slice(n * 256, n * 256 + 256)
            b.mixed[:, cols] = mm_nt(b.nl[...], self.slabs[0].at[3][cols, :]).astype(BF)

    def attend_back(self, p):
        b = self.b
        masks, tall = half_masks(), row_masks()
        cols = slice(p * LANES, p * LANES + LANES)
        rows = [slice(s * SEQ, s * SEQ + SEQ) for s in range(2)]
        dos = [[b.mixed[rows[s], cols] * masks[a] for a in range(2)] for s in range(2)]
        dps = [[mm_nt(b.v[rows[s], cols], dos[s][a]) for a in range(2)] for s in range(2)]
        low = [[None, None], [None, None]]
        for s in range(2):
            atts = []
            for a in range(2):
                att = b.p[s * 12 + p * 2 + a]
                atts.append(att.astype(BF))
                dp = dps[s][a]
                low[s][a] = (att * (dp - jnp.sum(att * dp, 0, keepdims=True))).astype(BF)
            b.gpre[2, rows[s], cols] = mm(jnp.concatenate(atts, 1), jnp.concatenate(dos[s], 0)).astype(BF)
        for s in range(2):
            q, kt = b.q[rows[s], cols], b.k[rows[s], cols].T
            dk = mm(jnp.concatenate(low[s], 1), jnp.concatenate([q * masks[0], q * masks[1]], 0))
            b.gpre[1, rows[s], cols] = dk.astype(BF)
            dq = mm(jnp.concatenate([kt * tall[0], kt * tall[1]], 1), jnp.concatenate(low[s], 0))
            b.gpre[0, rows[s], cols] = (dq.T * 0.125).astype(BF)

    def qkv_grads(self, start, count):
        b = self.b
        cols = slice(start, start + count)
        if count == LANES:
            both = mm(b.xt[...], jnp.concatenate([b.gpre[0, :, cols], b.gpre[1, :, cols]], 1))
            self.grads[0][0, :, cols] = both[:, :LANES].astype(BF)
            self.grads[0][1, :, cols] = both[:, LANES:].astype(BF)
        else:
            self.grads[0][0, :, cols] = mm(b.xt[...], b.gpre[0, :, cols]).astype(BF)
            self.grads[0][1, :, cols] = mm(b.xt[...], b.gpre[1, :, cols]).astype(BF)
        self.grads[0][2, :, cols] = mm(b.xt[...], b.gpre[2, :, cols]).astype(BF)
        self.gvec[VQ:VQ + 1, cols] = column_total(b.gpre[0, :, cols])
        self.gvec[VV:VV + 1, cols] = column_total(b.gpre[2, :, cols])

    def input_grad(self, n):
        b = self.b
        cols = slice(n * 256, n * 256 + 256)
        acc = b.second[:, cols]
        for j in range(3):
            acc = acc + mm_nt(b.gpre[j], self.slabs[0].at[j][cols, :])
        b.second[:, cols] = acc


BUFFERS = dict(
    q=((TOKENS, WIDTH), BF), k=((TOKENS, WIDTH), BF), v=((TOKENS, WIDTH), BF), p=((24, SEQ, SEQ), F32),
    mixed=((TOKENS, WIDTH), BF), n1=((TOKENS, WIDTH), F32), r1=((TOKENS, LANES), F32), nl=((TOKENS, WIDTH), BF),
    act=((4, TOKENS, WIDTH), BF), gp=((4, TOKENS, WIDTH), F32), second=((TOKENS, WIDTH), F32),
    gpre=((4, TOKENS, WIDTH), BF), xt=((WIDTH, TOKENS), BF), nlt=((WIDTH, TOKENS), BF),
)


START = {16: 0, 8: 16, 4: 24}
WHOLE = tuple((part, part * LANES, LANES, 0, UNIT, ORDERS[part]) for part in range(PARTS))
STRIPS = (
    ((Z1, Z3, Y1, Y3, X1), (Z1, Z3, X1, Y1, Y3), (Y1, Y3, X3, Z3, Z1)),
    ((Y1, Y3, Z1, Z3, X3), (Z1, Z3, X1, Y3, Y1), (Y1, Y3, X3, Z1, Z3)),
)
COLUMNS = ((0, 256), (256, 256), (512, LANES), (640, LANES))
CUT = tuple((part,) + COLUMNS[part] + (16 * i, 16, STRIPS[part % 2][i]) for part in range(4) for i in range(3))
CHAINS = (CUT, WHOLE, WHOLE)
FIRST = (0, 12, 18)
EVERY = ((0, 2), (0, 4), (0, 2), (0, 2))
VECTORS = "v0 v1 v2 v3".split() + "v4 v5 v6 v7".split()
SCRATCH = dict(
    wa=(SHAPES[0], BF), wb=(SHAPES[1], BF), wc=(SHAPES[2], BF), ga=(SHAPES[0], BF),
    rdb=((2, 1, 4, 2, 2, UNIT, WIDTH), BF), rdc=((4, 2, 2, 2, 1, UNIT, WIDTH), BF),
    rk=((3, 31, UNIT, WIDTH), BF), rx=((UNIT, WIDTH), BF), tall=((UNIT, WIDTH), F32),
    stage=((2, 4, 16, WIDTH), BF), final=((2, 2, 4, 16, WIDTH), BF),
    vt=((4, 2, 8, 2, LANES), F32), gv=((4, 2, 8, 2, LANES), F32),
    rv2=((3, 2, 8, 2, LANES), F32), rv1=((3, 4, 2, LANES), F32), rv0=((7, 2, LANES), F32),
    vec=((16, WIDTH), F32), gvec=((16, WIDTH), F32),
    x=((TOKENS, WIDTH), BF), qkv_in=((12, 3 * WIDTH), BF), out_in=((12, WIDTH), BF), up_in=((12, 4 * WIDTH), BF),
    **{name: ((1, 12), BF) for name in VECTORS}, v8=((1, 48), BF),
)
SEMS = dict(
    loads=(17,), mate_send=(2, 3), mate_recv=(2, 3), send=(3,), recv=(3, PARTS, 7),
    sib_send=(3,), sib_recv=(3, PARTS), vsend=(9,), vrecv=(9,),
    gsib_send=(3, PARTS), gsib_recv=(3, PARTS), gsend=(3,), grecv=(24, 7),
    rep_send=(1,), rep_recv=(1,), gmate_send=(3, 7), gmate_recv=(3, 7), gvsend=(13,), gvrecv=(13,),
)


def box_count(box):
    return box[0][1] * box[1][1] * box[2][1] * box[3][1]


def split3(value):
    high = value.astype(BF)
    rest = value - high.astype(F32)
    mid = rest.astype(BF)
    return high, mid, (rest - mid.astype(F32)).astype(BF)


def owner_masks(block):
    d = lax.broadcasted_iota(jnp.int32, (64, WIDTH), 0)
    c = lax.broadcasted_iota(jnp.int32, (64, WIDTH), 1)
    if block is None:
        return d == (c * 43691) >> 19
    return d == 16 * block + ((c * 43691) >> 21)


def lane_picks(row):
    c = lax.broadcasted_iota(jnp.int32, (WIDTH, LANES), 0)
    lane = lax.broadcasted_iota(jnp.int32, (WIDTH, LANES), 1)
    if row is None:
        return (lane == c - 48 * ((c * 43691) >> 21)).astype(F32).astype(BF)
    return (lane == 12 * row + c - 12 * ((c * 43691) >> 19)).astype(F32).astype(BF)


def mega_kernel(lengths, *refs):
    vecs_in, (qkv_in, out_in, up_in, down_in, x_in, og_in,
               enc_out, sgrad_out, oqkv, oout, oup, odown, ovec), scratch = refs[:9], refs[9:22], refs[22:]
    r = b = types.SimpleNamespace(**dict(zip([*SCRATCH, *BUFFERS, *SEMS], scratch)))
    here = position()
    me = member_of(here)
    sibling = hop(here, CORE)
    twin = hop(here, X2)
    weights = (r.wa, r.wb, r.wc)
    grads = (r.ga, r.wb, r.wc)
    rds = (r.act.at[pl.ds(0, 3)].reshape((2, 1, 4, 2, 2, UNIT, WIDTH)), r.rdb, r.rdc)
    slabs = [w.reshape(4, WIDTH, WIDTH) for w in weights]
    gslabs = [w.reshape(4, WIDTH, WIDTH) for w in grads]
    layer = Layer(slabs, gslabs, r.vec, lengths, r.x, r.x, r.x, r.gvec, b)

    def own_at(phase):
        ylow, z, x, yhigh = (s for s, n in own_box(here))
        return (ylow, here.core, z, x, yhigh) if phase < 2 else (z, x, yhigh, ylow, here.core)

    def mate_copy(which, k):
        mate = mates(here)[k]
        return remote(r.stage.at[which, member_of(mate)], r.final.at[which, 0, me],
                      r.mate_send.at[which, k], r.mate_recv.at[which, k], mate)

    def assemble(which):
        for k in range(3):
            mate_copy(which, k).wait()
        r.final[which, 0, me] = r.stage[which, me]
        for i in range(4):
            r.tall[12 * i:12 * i + 12, :] = r.final[which, 0, i, 0:12, :].astype(F32)
        weights[which][own_at(which)] = r.tall[...].astype(BF)

    def push(phase, part, found, slot, there):
        w = weights[phase]
        for box in found:
            view = w.at[slices(phase, here.core, box, part)]
            remote(view, view, r.send.at[phase], r.recv.at[phase, part, slot], there).start()

    def share(phase, part, found):
        w = weights[phase]
        for box in found:
            view = w.at[slices(phase, here.core, box, part)]
            remote(view, view, r.sib_send.at[phase], r.sib_recv.at[phase, part], sibling).start()

    def gather_first(phase):
        for part in range(PARTS):
            for slot, there in enumerate(trio(here, ORDERS[part])):
                push(phase, part, boxes(here, ()), slot, there)

    def gather(phase, step):
        w = weights[phase]
        for part in range(PARTS):
            order = ORDERS[part]
            if step == 2:
                for slot in range(3):
                    wait_units(w, phase, 1, part, r.recv.at[phase, part, slot])
            else:
                wait_units(w, phase, 1 << (step - 1), part, r.recv.at[phase, part, step])
            there = hop(here, order[step])
            if step < 4:
                push(phase, part, boxes(here, order[:step]), step + 1, there)
            else:
                for half, found in enumerate(halves(boxes(here, order[:4]))):
                    push(phase, part, found, 5 + half, there)
                share(phase, part, boxes(here, order[:4]))

    def gather_last(phase, half):
        for part in range(PARTS):
            order = ORDERS[part]
            wait_units(weights[phase], phase, 8, part, r.recv.at[phase, part, 5 + half])
            share(phase, part, halves(boxes(hop(here, order[4]), order[:4]))[half])

    def gathered(phase, parts=range(PARTS)):
        for part in parts:
            wait_units(weights[phase], phase, 32, part, r.sib_recv.at[phase, part])

    def wait_bytes(phase, units, sem):
        view = weights[phase].reshape((64, UNIT, WIDTH)).at[pl.ds(0, units)]
        pltpu.make_async_copy(view, view, sem).wait()

    def gather_sent(phase):
        wait_bytes(phase, 32, r.sib_send.at[phase])
        wait_bytes(phase, 31, r.send.at[phase])

    def vec_tile(place):
        return (place.z, place.x % 2, place.y * 2 + place.core)

    def vec_pair(place):
        return (place.z, place.x % 2, pl.ds(place.y // 2 * 4, 4))

    def vec_ring(place):
        return (pl.ds(place.z // 2 * 2, 2), place.x % 2)

    def vec_peers(k):
        return (mates(here), trio(here, (Y3, Z1)), trio(here, (Z3, X1)))[k]

    def vec_copies(k):
        view = r.vt.at[(vec_tile, vec_pair, vec_ring)[k](here)]
        return [remote(view, view, r.vsend.at[3 * k + i], r.vrecv.at[3 * k + i], there) for i, there in enumerate(vec_peers(k))]

    def vec_start(k):
        for copy in vec_copies(k):
            copy.start()

    def vec_wait(k):
        for copy in vec_copies(k):
            copy.wait()

    def expand():
        first = r.vt[:, :, :, 0, :].reshape(64, LANES)
        second = r.vt[:, :, :, 1, :].reshape(64, LANES).astype(BF)
        mask = owner_masks(None)
        turned = [first] + [pltpu.roll(first, LANES - 12 * row, 1) for row in range(1, 8)]
        t = mm_nt(jnp.concatenate(turned, 0).astype(BF), lane_picks(0)).reshape(8, 64, WIDTH)
        for row in range(8):
            r.vec[row:row + 1, :] = jnp.sum(jnp.where(mask, t[row], 0.0), 0, keepdims=True)
        t = mm_nt(second, lane_picks(None))
        for j in range(4):
            r.vec[8 + j:9 + j, :] = jnp.sum(jnp.where(owner_masks(j), t, 0.0), 0, keepdims=True)

    def sib_copy(phase, k):
        g, rd = grads[phase], rds[phase]
        if phase == 0:
            cols = pl.ds(*COLUMNS[k])
            src = g.at[:, pl.ds(sibling.core, 1), :, :, :, :, cols]
            dst = rd.at[:, :, :, :, :, :, cols]
        elif phase == 1:
            src, dst = g.at[k, sibling.core], rd.at[k, 0]
        else:
            src, dst = g.at[k, :, :, :, pl.ds(sibling.core, 1)], rd.at[k]
        return remote(src, dst, r.gsib_send.at[phase, k], r.gsib_recv.at[phase, k], sibling)

    def sib_add(phase, k):
        sib_copy(phase, k).wait()
        g, rd = grads[phase], rds[phase]
        for i in range(4):
            if phase == 0:
                cols = slice(COLUMNS[k][0], sum(COLUMNS[k]))
                at = (slice(None), pl.ds(here.core, 1), i, slice(None), slice(None), slice(None), cols)
                g[at] = g[at] + rd[:, :, i, :, :, :, cols]
            elif phase == 1:
                g[k, here.core, i] = g[k, here.core, i] + rd[k, 0, i]
            else:
                at = (k, i // 2, i % 2, slice(None), pl.ds(here.core, 1))
                g[at] = g[at] + rd[k, i // 2, i % 2]

    def unit_slices(phase, box, chain):
        _, col, cols, row, rows, _ = chain
        return slices(phase, here.core, box, 0)[:5] + (slice(row, row + rows), slice(col, col + cols))

    def hop_start(phase, c, step):
        chain = CHAINS[phase][c]
        _, col, cols, row, rows, order = chain

        def send(box, at, slot, there):
            n = box_count(box)
            src = grads[phase].at[slices(phase, here.core, box, 0)[:5]]
            dst = r.rk.at[phase, pl.ds(at, n)].reshape(src.shape)
            at5 = (slice(None),) * 5 + (pl.ds(row, rows), pl.ds(col, cols))
            remote(src.at[at5], dst.at[at5], r.gsend.at[phase], r.grecv.at[FIRST[phase] + c, slot], there).start()
            return at + n

        if step == 1:
            for slot, there in enumerate(trio(here, order)):
                send(boxes(there, ())[0], 28 + slot, slot, there)
            return
        if phase == 0 and step == 3:
            for i, there in enumerate(trio(here, order[2:])):
                at = 16 + 4 * i
                for box in boxes(there, order[:2]):
                    at = send(box, at, 3 + i, there)
            return
        there = hop(here, order[step])
        at = START[1 << step]
        for box in boxes(there, order[:step]):
            at = send(box, at, step + 2, there)

    def landing(phase, c, at, n):
        _, col, cols, row, rows, _ = CHAINS[phase][c]
        return r.rk.at[phase, pl.ds(at, n), pl.ds(row, rows), pl.ds(col, cols)]

    def hop_add(phase, c, step):
        g = grads[phase]
        chain = CHAINS[phase][c]
        if step == 1:
            where = unit_slices(phase, boxes(here, ())[0], chain)
            total = g[where].astype(F32)
            for slot in range(3):
                view = landing(phase, c, 28 + slot, 1)
                pltpu.make_async_copy(view, view, r.grecv.at[FIRST[phase] + c, slot]).wait()
                total = total + view[...].astype(F32).reshape(total.shape)
            g[where] = total.astype(BF)
            return
        if phase == 0 and step == 3:
            for i in range(3):
                view = landing(phase, c, 16 + 4 * i, 4)
                pltpu.make_async_copy(view, view, r.grecv.at[FIRST[phase] + c, 3 + i]).wait()
            at = 16
            for box in boxes(here, chain[5][:2]):
                m = box_count(box)
                where = unit_slices(phase, box, chain)
                total = g[where].astype(F32)
                for i in range(3):
                    total = total + landing(phase, c, at + 4 * i, m)[...].astype(F32).reshape(total.shape)
                g[where] = total.astype(BF)
                at += m
            return
        n = 1 << step
        at = START[n]
        view = landing(phase, c, at, n)
        pltpu.make_async_copy(view, view, r.grecv.at[FIRST[phase] + c, step + 2]).wait()
        for box in boxes(here, chain[5][:step]):
            m = box_count(box)
            where = unit_slices(phase, box, chain)
            old = g[where]
            g[where] = old + landing(phase, c, at, m)[...].reshape(old.shape)
            at += m

    def rep_copy():
        return remote(grads[2].at[own_at(2)], r.rx, r.rep_send.at[0], r.rep_recv.at[0], twin)

    def reduce_first(phase):
        for k in range(2 if phase == 1 else 4):
            sib_add(phase, k)
        for part in range(PARTS):
            hop_start(phase, part, 4)

    def move(phase, c, step):
        hop_add(phase, c, step)
        if step > 1:
            hop_start(phase, c, 1 if phase == 0 and step == 3 else step - 1)

    def reduce(phase, step):
        for part in range(PARTS):
            move(phase, part, step)

    def first_part(part):
        sib_add(0, part)
        for c, chain in enumerate(CUT):
            if chain[0] == part:
                hop_start(0, c, 4)

    def move_part(part, step):
        for c, chain in enumerate(CUT):
            if chain[0] == part:
                move(0, c, step)

    def gmate_copy(which, k):
        others = mates(here)
        there = (others + [twin] + [hop(mate, X2) for mate in others])[k]
        cols = (pl.ds(0, 512), pl.ds(0, WIDTH), pl.ds(512, 256))[which]
        phase = which % 2
        return remote(r.stage.at[phase, member_of(there), :, cols], r.final.at[phase, k // 3 if k < 6 else 1, me, :, cols],
                      r.gmate_send.at[which, k], r.gmate_recv.at[which, k], there)

    def hand_over(which):
        phase = which % 2
        cols = (slice(0, 512), slice(0, WIDTH), slice(512, WIDTH))[which]
        r.tall[:, cols] = grads[phase][own_at(phase) + (slice(None), cols)].astype(F32)
        for i in range(4):
            r.stage[phase, i, 0:12, cols] = r.tall[12 * i:12 * i + 12, cols].astype(BF)
        for k in range(7):
            gmate_copy(which, k).start()

    def deliver(which):
        phase = which % 2
        cols = (slice(0, 512), slice(0, WIDTH), slice(512, WIDTH))[which]
        for k in range(7):
            gmate_copy(which, k).wait()
        r.final[phase, 0, me, :, cols] = r.stage[phase, me, :, cols]
        for i in range(4):
            at = slice(i * WIDTH + cols.start, i * WIDTH + cols.stop)
            dst = oup.at[:, at] if phase else (oqkv.at[:, at] if i < 3 else oout.at[:, cols])
            dst[...] = r.final[phase, 0, i, 0:12, cols].astype(F32) + r.final[phase, 1, i, 0:12, cols].astype(F32)

    def deliver_down():
        rep_copy().wait()
        odown[...] = grads[2][own_at(2)].astype(F32) + r.rx[...].astype(F32)

    def reduce_sent(phase):
        wait_bytes(phase, 31, r.gsend.at[phase])

    def pack_rows(first, count):
        mask = owner_masks(None).astype(F32).astype(BF)
        pieces = split3(r.gvec[first:first + count, :])
        spread = [piece[i:i + 1, :] * mask for piece in pieces for i in range(count)]
        out = mm(jnp.concatenate(spread, 0), lane_picks(0)).reshape(3, count, 64, LANES)
        out = out[0] + out[1] + out[2]
        total = out[0] if first == 0 else pltpu.roll(out[0], 12 * first, 1)
        for i in range(1, count):
            total = total + pltpu.roll(out[i], 12 * (first + i), 1)
        return total.reshape(4, 2, 8, LANES)

    def pack():
        pieces = split3(r.gvec[8:12, :])
        masks = [owner_masks(j).astype(F32).astype(BF) for j in range(4)]
        spread = [piece[j:j + 1, :] * masks[j] for piece in pieces for j in range(4)]
        out = mm(jnp.concatenate(spread, 0), lane_picks(None)).reshape(12, 64, LANES)
        r.gv[:, :, :, 0, :] = pack_rows(2, 6)
        r.gv[:, :, :, 1, :] = jnp.sum(out, 0).reshape(4, 2, 8, LANES)

    def gvec_copies(k):
        if k == 0:
            peers = mates(here) + [twin] + [hop(mate, X2) for mate in mates(here)]
        else:
            peers = vec_peers(k)
        part, landing_ref = ((vec_tile, r.rv0), (vec_pair, r.rv1), (vec_ring, r.rv2))[k]
        base = (6, 3, 0)[k]
        return [remote(r.gv.at[part(there)], landing_ref.at[i], r.gvsend.at[base + i], r.gvrecv.at[base + i], there)
                for i, there in enumerate(peers)]

    def gvec_start(k):
        for copy in gvec_copies(k):
            copy.start()

    def gvec_add(k):
        part, landing_ref = ((vec_tile, r.rv0), (vec_pair, r.rv1), (vec_ring, r.rv2))[k]
        at = part(here)
        total = r.gv[at]
        for i, copy in enumerate(gvec_copies(k)):
            copy.wait()
            total = total + landing_ref[i].reshape(total.shape)
        r.gv[at] = total

    near = [hop(here, link) for link in (Y1, Y3, Z1, Z3, X1, X3, CORE, X2, Y2, Z2)]
    near += [mates(here)[2], hop(hop(here, Y3), Z1), hop(hop(here, Y1), Z3)]
    near += [hop(mate, X2) for mate in mates(here)]
    near += [hop(hop(here, a), c) for a, c in ((Z3, X1), (X1, Y1), (X1, Y3), (X3, Z1), (X3, Z3))]
    loads = [pltpu.make_async_copy(src, dst, r.loads.at[i]) for i, (src, dst) in enumerate((
        (qkv_in, r.qkv_in), (out_in, r.out_in), (up_in, r.up_in), (down_in, weights[2].at[own_at(2)]), (x_in, r.x)))]
    held = [getattr(r, name) for name in VECTORS] + [r.v8]
    vec_loads = [pltpu.make_async_copy(src, dst, r.loads.at[8 + i]) for i, (src, dst) in enumerate(zip(vecs_in, held))]
    for load in loads[:4] + vec_loads + loads[4:]:
        load.start()
    barrier = pltpu.get_barrier_semaphore()
    for place in near:
        pl.semaphore_signal(barrier, inc=1, device_id=device_of(place), device_id_type=MESH)
    og_load = pltpu.make_async_copy(og_in, r.x, r.loads.at[5])
    own = vec_tile(here)
    r.vt[own] = jnp.zeros((2, LANES), F32)
    for load in loads[:4] + vec_loads:
        load.wait()
    for i in range(8):
        r.vt[own + (slice(0, 1), slice(12 * i, 12 * i + 12))] = held[i][...].astype(F32)
    r.vt[own + (slice(1, 2), slice(0, 48))] = held[8][...].astype(F32)
    for i in range(4):
        r.stage[0, i, 0:12, :] = r.qkv_in[:, i * WIDTH:(i + 1) * WIDTH] if i < 3 else r.out_in[...]
        r.stage[1, i, 0:12, :] = r.up_in[:, i * WIDTH:(i + 1) * WIDTH]
    pl.semaphore_wait(barrier, len(near))
    for k in range(3):
        mate_copy(0, k).start()
    vec_start(0)
    for k in range(3):
        mate_copy(1, k).start()
    gather_first(2)
    assemble(0)
    vec_wait(0)
    vec_start(1)
    gather_first(0)
    assemble(1)
    gather_first(1)
    loads[4].wait()
    b.xt[...] = r.x[...].T
    vec_wait(1)
    vec_start(2)
    gather(0, 2)
    gather(2, 2)
    gather(1, 2)
    gather(0, 3)
    vec_wait(2)
    expand()
    gather(0, 4)
    gather(1, 3)
    gather(2, 3)
    gather_last(0, 0)
    gather_last(0, 1)
    for n in range(3):
        gathered(0, (2 * n, 2 * n + 1))
        layer.project(n)
        if n == 0:
            gather(1, 4)
    gather(2, 4)
    layer.attend()
    gather_last(1, 0)
    gather_last(1, 1)
    layer.attn_out()
    og_load.start()
    b.nlt[...] = b.nl[...].T
    gather_last(2, 0)
    gather_last(2, 1)
    gathered(1)
    layer.feed()
    og_load.wait()
    gathered(2)
    layer.feed_out()
    enc_store = pltpu.make_async_copy(r.x, enc_out, r.loads.at[6])
    enc_store.start()
    gather_sent(2)

    def down_body(j, _):
        layer.feed_back(j)
        layer.down_grads(j)
        sib_copy(2, j).start()
        return 0

    lax.fori_loop(0, 4, down_body, 0)
    for n in range(3):
        layer.norm1_back(n)
    reduce_first(2)
    gather_sent(1)

    def up_body(i, _):
        layer.up_grads(i * 2 + sibling.core)
        sib_copy(1, i).start()
        return 0

    def up_own(i, _):
        layer.up_grads(i * 2 + here.core)
        return 0

    lax.fori_loop(0, 2, up_body, 0)
    lax.fori_loop(0, 2, up_own, 0)
    layer.norm1_rows()
    layer.out_grads()
    reduce(2, 4)
    reduce_first(1)
    layer.out_back()
    pack()
    layer.attend_back(0)
    layer.attend_back(1)
    layer.qkv_grads(*COLUMNS[0])
    sib_copy(0, 0).start()
    reduce(2, 3)
    layer.attend_back(2)
    first_part(0)
    layer.attend_back(3)
    layer.qkv_grads(*COLUMNS[1])
    sib_copy(0, 1).start()
    reduce(1, 4)
    layer.attend_back(4)
    layer.qkv_grads(*COLUMNS[2])
    sib_copy(0, 2).start()
    first_part(1)
    move_part(0, 4)
    reduce(2, 2)
    layer.attend_back(5)
    layer.qkv_grads(*COLUMNS[3])
    sib_copy(0, 3).start()
    first_part(2)
    layer.input_grad(0)
    layer.input_grad(1)
    first_part(3)
    reduce(1, 3)
    r.gv[:, :, :, 0, :] = r.gv[:, :, :, 0, :] + pack_rows(VQ, 2)
    gvec_start(2)
    move_part(1, 4)
    move_part(0, 3)
    layer.input_grad(2)
    sgrad_store = pltpu.make_async_copy(b.second, sgrad_out, r.loads.at[7])
    sgrad_store.start()
    reduce(1, 2)
    move_part(2, 4)
    gvec_add(2)
    gvec_start(1)
    reduce(2, 1)
    rep_copy().start()
    move_part(3, 4)
    reduce(1, 1)
    hand_over(1)
    move_part(0, 1)
    move_part(1, 3)
    move_part(2, 3)
    gvec_add(1)
    gvec_start(0)
    move_part(3, 3)
    deliver_down()
    move_part(1, 1)
    hand_over(0)
    move_part(2, 1)
    move_part(3, 1)
    hand_over(2)
    deliver(1)
    gvec_add(0)
    ovec[...] = r.gv[vec_tile(here)]
    for phase in range(1, 3):
        reduce_sent(phase)
    gather_sent(0)
    reduce_sent(0)
    enc_store.wait()
    sgrad_store.wait()
    deliver(0)
    deliver(2)


def run_layer(lengths, vecs, qkv, out, up, down, x, og):
    vm = pl.BlockSpec(memory_space=pltpu.VMEM)
    hb = pl.BlockSpec(memory_space=pl.ANY)
    return pl.pallas_call(
        mega_kernel,
        out_shape=[
            jax.ShapeDtypeStruct((TOKENS, WIDTH), BF), jax.ShapeDtypeStruct((TOKENS, WIDTH), F32),
            jax.ShapeDtypeStruct((12, 3 * WIDTH), F32), jax.ShapeDtypeStruct((12, WIDTH), F32),
            jax.ShapeDtypeStruct((12, 4 * WIDTH), F32), jax.ShapeDtypeStruct((UNIT, WIDTH), F32), jax.ShapeDtypeStruct((2, LANES), F32),
        ],
        in_specs=[pl.BlockSpec(memory_space=pltpu.SMEM)] + [hb] * 15,
        out_specs=[hb, hb] + [vm] * 5,
        scratch_shapes=[pltpu.VMEM(s, d) for s, d in SCRATCH.values()] + [pltpu.VMEM(s, d) for s, d in BUFFERS.values()]
        + [pltpu.SemaphoreType.DMA(s) for s in SEMS.values()],
        compiler_params=pltpu.CompilerParams(collective_id=1, has_side_effects=True, vmem_limit_bytes=63 * 2**20),
    )(lengths, *vecs, qkv, out, up, down, x, og)


def finish_kernel(*refs):
    srcs, dsts, vec_outs, held, parts, sems = refs[:7], refs[7:13], refs[13:22], refs[22:29], refs[29:38], refs[38]
    loads = [pltpu.make_async_copy(src, mid, sems.at[0, i]) for i, (src, mid) in enumerate(zip(srcs, held))]
    stores = [pltpu.make_async_copy(mid, dst, sems.at[1, i]) for i, (mid, dst) in enumerate(zip(held, dsts))]
    vec_stores = [pltpu.make_async_copy(mid, dst, sems.at[1, 6 + i]) for i, (mid, dst) in enumerate(zip(parts, vec_outs))]
    for load in loads[::-1]:
        load.start()
    loads[6].wait()
    vec = held[6]
    for i in range(8):
        parts[i][...] = vec[0:1, 12 * i:12 * i + 12]
    parts[8][...] = vec[1:2, 0:48]
    for store in vec_stores:
        store.start()
    for load, store in list(zip(loads, stores))[::-1]:
        load.wait()
        store.start()
    for store in vec_stores + stores:
        store.wait()


def finish(results):
    hb = pl.BlockSpec(memory_space=pl.ANY)
    small = [(1, n) for n in [12] * 8 + [48]]
    return pl.pallas_call(
        finish_kernel,
        out_shape=[jax.ShapeDtypeStruct(a.shape, a.dtype) for a in results[:6]] + [jax.ShapeDtypeStruct(n, F32) for n in small],
        in_specs=[hb] * 7,
        out_specs=[hb] * 15,
        scratch_shapes=[pltpu.VMEM(a.shape, a.dtype) for a in results] + [pltpu.VMEM(n, F32) for n in small]
        + [pltpu.SemaphoreType.DMA((2, 15))],
        compiler_params=pltpu.CompilerParams(vmem_limit_bytes=63 * 2**20),
    )(*results)


def local(states, qkv_weight, query_bias, value_bias, out_weight, out_bias, attn_gain, attn_shift, up_weight, up_bias,
          down_weight, down_bias, ffn_gain, ffn_shift, out_grad, lengths):
    vecs = [v.reshape(1, -1) for v in (query_bias, value_bias, out_bias, attn_gain, attn_shift, down_bias, ffn_gain, ffn_shift, up_bias)]
    results = run_layer(
        lengths.reshape(1, 2), vecs, qkv_weight, out_weight, up_weight, down_weight,
        states.reshape(TOKENS, WIDTH), out_grad.reshape(TOKENS, WIDTH))
    enc, sgrad, oqkv, oout, oup, odown, *o = finish(results)
    o = [v.reshape(-1) for v in o]
    return (enc.reshape(states.shape), sgrad.reshape(states.shape), oqkv, o[0], o[1], oout, o[2], o[3], o[4],
            oup, o[8], odown, o[5], o[6], o[7])


def solution(mesh):
    return jax.shard_map(
        local,
        mesh=mesh,
        in_specs=(
            P(None, ("dp", "rep"), None, None),
            P("dp", None),
            P("dp"),
            P("dp"),
            P("dp", None),
            P("dp"),
            P("dp"),
            P("dp"),
            P("dp", None),
            P("dp"),
            P("dp", None),
            P("dp"),
            P("dp"),
            P("dp"),
            P(None, ("dp", "rep"), None, None),
            P(None, ("dp", "rep")),
        ),
        out_specs=(
            P(None, ("dp", "rep"), None, None),
            P(None, ("dp", "rep"), None, None),
            P("dp", None),
            P("dp"),
            P("dp"),
            P("dp", None),
            P("dp"),
            P("dp"),
            P("dp"),
            P("dp", None),
            P("dp"),
            P("dp", None),
            P("dp"),
            P("dp"),
            P("dp"),
        ),
        check_vma=False,
    )
```
